32 devices in a mesh: groups: 2 (over y), wide: 4 (over z), narrow: 4 (over x, core).
Axes of the slice: x: 2, y: 2, z: 4, core: 2. Of those that a mesh axis runs over, the one named last changes fastest.
Arguments:
- target_states: bfloat16 [256, 8192], P(('groups', 'wide'), 'narrow'), parts along dimension 0, may hold values from -6 to 6
- source_states: bfloat16 [256, 8192], P(('groups', 'wide'), 'narrow'), parts along dimension 0, may hold values from -6 to 6
- target_gate: bfloat16 [8192, 14336], P('narrow', 'wide'), may hold values from -0.0625 to 0.0625
- target_up: bfloat16 [8192, 14336], P('narrow', 'wide'), may hold values from -0.0625 to 0.0625
- source_gate: bfloat16 [8192, 14336], P('narrow', 'wide'), may hold values from -0.0625 to 0.0625
- source_up: bfloat16 [8192, 14336], P('narrow', 'wide'), may hold values from -0.0625 to 0.0625
- token_ids: int32 [256], P(('groups', 'narrow')), parts along dimension 0, may hold values from 0 to 128255
- lengths: int32 [16], P(('groups', 'narrow')), parts along dimension 0, may hold values from 1 to 16
- ratio_weight: float32 [128256], replicated, may hold values from 0.25 to 1
Outputs:
- target_hidden: bfloat16 [256, 14336], P(('groups', 'narrow'), 'wide'), parts along dimension 0
- ratio_hidden: bfloat16 [256, 14336], P(('groups', 'narrow'), 'wide'), parts along dimension 0
The draws below stay inside these ranges and needn't reach their ends.
There are 2 independent parts, one for each index of `groups`. The reference program is written for one: setup_inputs(seed, part) draws one part's arguments, and reference() takes and returns one part's arrays. A program takes and returns all parts, laid end to end along the dimension named above; an argument that names none is the same for every part. Nothing has to cross between parts.
All inputs are finite; a program needn't handle non-finite values.
Results may differ from the reference program's by a relative error of at most 0.02.
Values may be sent and summed in bfloat16 or wider, within the bound.
No kernel may reach another device: no remote copies, remote signals or barrier semaphores. Data moves between devices by JAX's collectives and lax.ppermute only.
A program may use at most 128 MiB of HBM per device.

```python
import math
import jax
import jax.numpy as jnp
import numpy as np
from jax import lax

D = 8192
FF = 14336
VOCAB = 128256
HLEN = 16
TOKENS = 128
HYPS = 8
N_NARROW = 4


def with_ends(entries, key, smallest, high):
    longest = entries.shape.index(max(entries.shape))
    spots = []
    for shift in (0, 1):
        where = [jax.random.randint(jax.random.fold_in(key, axis), (), 0, length) for axis, length in enumerate(entries.shape)]
        where[longest] = (where[longest] + shift) % entries.shape[longest]
        spots.append(tuple(where))
    return entries.at[spots[0]].set(smallest).at[spots[1]].set(high)


def block_levels(key, extent, cuts, smallest, high):
    loudness = 1.0
    for dim, parts in cuts:
        heights = jax.random.uniform(jax.random.fold_in(jax.random.fold_in(key, 6), dim), (parts,), jnp.float32, smallest / len(cuts), high / len(cuts))
        loudness = loudness * jnp.repeat(jnp.exp(heights), extent[dim] // parts).reshape((-1,) + (1,) * (len(extent) - 1 - dim))
    return loudness


def skewed_wide(own_key, extent, number_of, slope):
    loads = [min(1 << octave, number_of + 1 - (1 << octave)) * (1 << 20) // math.isqrt((1 << octave) ** slope) + 1 for octave in range((number_of + 1).bit_length()) if 1 << octave <= number_of]
    spread = 1 + sum(loads) // (1 << 30)
    listing = np.cumsum(np.array([max(1, weight // spread) for weight in loads]))
    ticket = jax.random.randint(jax.random.fold_in(own_key, 1), extent, 0, int(listing[len(loads) - 1]))
    start = jnp.left_shift(1, jnp.searchsorted(jnp.asarray(listing, jnp.int32), ticket, side="right").astype(jnp.int32))
    standing = start - 1 + jax.random.randint(jax.random.fold_in(own_key, 4), extent, 0, 1 << 30) % jnp.minimum(start, number_of + 1 - start)
    return jax.random.permutation(jax.random.fold_in(own_key, 2), number_of)[standing].astype(jnp.int32)


def scatter_about(rng, shape, deviation, reach, shards=(), held_as=jnp.bfloat16):
    array = jax.random.normal(rng, shape, jnp.float32) * deviation
    if len(shards) > 0:
        array = block_levels(rng, shape, shards, -0.22, 0.18) * array
    return jnp.clip(array, min=-reach, max=reach).astype(held_as)


def setup_inputs(seed: int = 0, part: int = 0) -> dict:
    arg_keys = jax.random.split(jax.random.key(seed), 10)
    own_keys = jax.random.split(jax.random.fold_in(arg_keys[9], part), 10)
    target_states = scatter_about(own_keys[0], (TOKENS, D), 1.0, 6.0, ((0, 4), (1, 4)))
    source_states = scatter_about(own_keys[1], (TOKENS, D), 1.0, 6.0, ((0, 4), (1, 4)))
    target_gate = scatter_about(arg_keys[2], (D, FF), D ** -0.5, 0.0625, ((0, 4), (1, 4)))
    target_up = scatter_about(arg_keys[3], (D, FF), D ** -0.5, 0.0625, ((0, 4), (1, 4)))
    source_gate = scatter_about(arg_keys[4], (D, FF), D ** -0.5, 0.0625, ((0, 4), (1, 4)))
    source_up = scatter_about(arg_keys[5], (D, FF), D ** -0.5, 0.0625, ((0, 4), (1, 4)))
    token_ids = with_ends(skewed_wide(own_keys[6], (TOKENS,), VOCAB, 2), jax.random.fold_in(own_keys[6], 3), 0, VOCAB - 1).astype(jnp.int32)
    lengths = with_ends(jax.random.randint(own_keys[7], (HYPS,), 1, HLEN + 1), jax.random.fold_in(own_keys[7], 1), 1, HLEN).astype(jnp.int32)
    ratio_weight = jnp.clip(jnp.exp(jax.random.uniform(arg_keys[8], (VOCAB,), jnp.float32, math.log(0.25), math.log(1.0))), 0.25, 1.0)
    return dict(target_states=target_states, source_states=source_states, target_gate=target_gate, target_up=target_up, source_gate=source_gate, source_up=source_up, token_ids=token_ids, lengths=lengths, ratio_weight=ratio_weight)


def projected(states, weight):
    tile = D // N_NARROW
    total = jnp.zeros((states.shape[0], weight.shape[1]), jnp.float32)
    for index in range(N_NARROW):
        partial_sum = jnp.dot(states[:, index * tile:(index + 1) * tile], weight[index * tile:(index + 1) * tile, :], preferred_element_type=jnp.float32)
        rounded = lax.optimization_barrier(partial_sum.astype(jnp.bfloat16))
        total = total + rounded.astype(jnp.float32)
    return total


def reference(target_states, source_states, target_gate, target_up, source_gate, source_up, token_ids, lengths, ratio_weight):
    target_act = jax.nn.silu(projected(target_states, target_gate)) * projected(target_states, target_up)
    source_act = jax.nn.silu(projected(source_states, source_gate)) * projected(source_states, source_up)
    slots = jnp.arange(HLEN, dtype=jnp.int32)
    live = (slots[None, :] < lengths[:, None]).reshape(-1).astype(jnp.float32)
    weight = ratio_weight[token_ids]
    target_out = (live[:, None] * target_act).astype(jnp.bfloat16)
    ratio_out = (live[:, None] * (target_act - weight[:, None] * source_act)).astype(jnp.bfloat16)
    return target_out, ratio_out
```

```python
import math

import jax
import jax.numpy as jnp
from jax import lax
from jax.sharding import PartitionSpec as P


def ring_gather(piece, axis, size):
    pairs = [(i, (i + 1) % size) for i in range(size)]
    pieces = [piece]
    for _ in range(size - 1):
        pieces.append(lax.ppermute(pieces[-1], axis, pairs))
    return pieces


def halving_order(size):
    bits = size.bit_length() - 1
    reverse = [sum(((p >> b) & 1) << (bits - 1 - b) for b in range(bits)) for p in range(size)]
    return reverse[::-1]


def arrange(pieces, me_wide, me_narrow, wide, narrow):
    piece_rows = pieces[0].shape[0]
    block_rows = piece_rows * wide // narrow
    sub = math.gcd(piece_rows, block_rows)
    place = [0] * narrow
    for position, offset in enumerate(halving_order(narrow)):
        place[offset] = position
    place = jnp.array(place, jnp.int32)
    whole = jnp.zeros((piece_rows * wide, pieces[0].shape[1]), pieces[0].dtype)
    for back, piece in enumerate(pieces):
        for start in range(0, piece_rows, sub):
            row = (me_wide + wide - back) % wide * piece_rows + start
            owner = row // block_rows
            row = place[owner ^ me_narrow] * block_rows + row % block_rows
            whole = lax.dynamic_update_slice_in_dim(whole, piece[start : start + sub], row, axis=0)
    return whole


def halving_sum(terms, axis, size):
    step = 1
    while step < size:
        half = terms.shape[0] // 2
        pairs = [(i, i ^ step) for i in range(size)]
        got = lax.ppermute(terms[:half].astype(jnp.bfloat16), axis, pairs)
        terms = terms[half:] + got.astype(jnp.float32)
        step *= 2
    return terms


def local(mesh_shape, target_states, source_states, target_gate, target_up, source_gate, source_up, token_ids, lengths, ratio_weight):
    wide, narrow = mesh_shape["wide"], mesh_shape["narrow"]
    me_wide, me_narrow = lax.axis_index("wide"), lax.axis_index("narrow")
    own_rows = token_ids.shape[0]

    slot_count = own_rows // lengths.shape[0]
    slots = jnp.arange(slot_count, dtype=jnp.int32)
    live = (slots[None, :] < lengths[:, None]).reshape(-1).astype(jnp.float32)
    weight = ratio_weight[token_ids]

    target_pieces = ring_gather(target_states, "wide", wide)
    source_states, target_pieces = lax.optimization_barrier((source_states, target_pieces))
    source_pieces = ring_gather(source_states, "wide", wide)

    def product(rows, matrix):
        terms = jnp.dot(rows, matrix, preferred_element_type=jnp.float32).astype(jnp.bfloat16)
        return halving_sum(terms.astype(jnp.float32), "narrow", narrow)

    target_rows = arrange(target_pieces, me_wide, me_narrow, wide, narrow)
    target_act = jax.nn.silu(product(target_rows, target_gate)) * product(target_rows, target_up)
    source_rows = arrange(source_pieces, me_wide, me_narrow, wide, narrow)
    source_act = jax.nn.silu(product(source_rows, source_gate)) * product(source_rows, source_up)

    target_out = (live[:, None] * target_act).astype(jnp.bfloat16)
    ratio_out = (live[:, None] * (target_act - weight[:, None] * source_act)).astype(jnp.bfloat16)
    return (target_out, ratio_out)


def solution(mesh):
    placed = (
        P(("groups", "wide"), "narrow"),
        P(("groups", "wide"), "narrow"),
        P("narrow", "wide"),
        P("narrow", "wide"),
        P("narrow", "wide"),
        P("narrow", "wide"),
        P(("groups", "narrow")),
        P(("groups", "narrow")),
        P(),
    )
    mesh_shape = dict(mesh.shape)

    def body(*args):
        return local(mesh_shape, *args)

    return jax.shard_map(
        body,
        mesh=mesh,
        in_specs=placed,
        out_specs=(P(("groups", "narrow"), "wide"), P(("groups", "narrow"), "wide")),
        check_vma=False,
    )
```

```python
import functools
import math

import jax
import jax.numpy as jnp
from jax import lax
from jax.experimental import pallas as pl
from jax.experimental.pallas import tpu as pltpu
from jax.sharding import PartitionSpec as P

IN_VMEM = pl.BlockSpec(memory_space=pltpu.VMEM)
ANYWHERE = pl.BlockSpec(memory_space=pl.ANY)


def gather_pieces(piece, axis, size, relayed):
    pieces = [piece]
    for offset in range(1, size):
        low = offset & -offset if relayed else offset
        pairs = [(i, i ^ low) for i in range(size)]
        pieces.append(lax.ppermute(pieces[offset ^ low], axis, pairs))
    return pieces


def halving_order(size):
    bits = size.bit_length() - 1
    reverse = [sum(((p >> b) & 1) << (bits - 1 - b) for b in range(bits)) for p in range(size)]
    return reverse[::-1]


def spots(piece_rows, wide, narrow):
    me_wide, me_narrow = lax.axis_index("wide"), lax.axis_index("narrow")
    block_rows = piece_rows * wide // narrow
    sub = math.gcd(piece_rows, block_rows)
    found = []
    for offset in range(wide):
        for start in range(0, piece_rows, sub):
            row = (me_wide ^ offset) * piece_rows + start
            block = (row // block_rows) ^ me_narrow
            place = sum(
                jnp.where(block == known, position, 0)
                for position, known in enumerate(halving_order(narrow))
            )
            found.append((offset, start, sub, place * block_rows + row % block_rows))
    return found


def load_kernel(count, *refs):
    outs = refs[-1 - count : -1]
    copies = [pltpu.make_async_copy(refs[i], outs[i], refs[-1].at[i]) for i in range(count)]
    for copy in copies:
        copy.start()
    for copy in copies:
        copy.wait()


def load(arrays, after=()):
    return pl.pallas_call(
        functools.partial(load_kernel, len(arrays)),
        out_shape=tuple(pltpu.VMEM(a.shape, a.dtype) for a in arrays),
        in_specs=[ANYWHERE] * (len(arrays) + len(after)),
        out_specs=tuple(IN_VMEM for _ in arrays),
        scratch_shapes=[pltpu.SemaphoreType.DMA((len(arrays),))],
        compiler_params=pltpu.CompilerParams(vmem_limit_bytes=1 << 20),
        cost_estimate=pl.CostEstimate(
            flops=0, transcendentals=0, bytes_accessed=sum(a.size * a.dtype.itemsize for a in arrays)
        ),
    )(*(pltpu.with_memory_space_constraint(a, pltpu.HBM) for a in arrays), *after)


def place_rows(pieces, narrow, rows):
    for i, start, size, spot in spots(pieces[0].shape[0], len(pieces), narrow):
        rows[pl.ds(pl.multiple_of(spot, size), size), :] = pieces[i][start : start + size, :]


def store_parts(outs, value, cols):
    start = 0
    for out in outs:
        out[:, cols] = value[start : start + out.shape[0]].astype(out.dtype)
        start += out.shape[0]


def tile_of(cols):
    for tile in (512, 256, 128):
        if cols % tile == 0:
            return tile
    return cols


def held_kernel(count, narrow, *refs):
    pieces, matrix, outs, rows = refs[:count], refs[count], refs[count + 2 : -1], refs[-1]
    place_rows(pieces, narrow, rows)
    tile = tile_of(matrix.shape[1])
    for start in range(0, matrix.shape[1], tile):
        cols = slice(start, start + tile)
        store_parts(outs, jnp.dot(rows[...], matrix[:, cols], preferred_element_type=jnp.float32), cols)


def streamed_kernel(count, narrow, *refs):
    pieces, matrix, outs, rows = refs[:count], refs[count], refs[count + 2 : -1], refs[-1]

    @pl.when(pl.program_id(0) == 0)
    def _():
        place_rows(pieces, narrow, rows)

    store_parts(outs, jnp.dot(rows[...], matrix[...], preferred_element_type=jnp.float32), slice(None))


def product(pieces, matrix, narrow, held, after):
    total = pieces[0].shape[0] * len(pieces)
    depth, width = matrix.shape
    sizes, left = [], total
    while left > total // narrow:
        left //= 2
        sizes.append(left)
    sizes.append(left)
    tile = tile_of(width)
    shapes = [jax.ShapeDtypeStruct((size, width), jnp.bfloat16) for size in sizes]
    scratch = [pltpu.VMEM((total, depth), jnp.bfloat16)]
    cost = pl.CostEstimate(
        flops=2 * total * depth * width,
        transcendentals=0,
        bytes_accessed=matrix.size * matrix.dtype.itemsize,
    )
    params = pltpu.CompilerParams(vmem_limit_bytes=(8 if held else 16) << 20)
    if held:
        return pl.pallas_call(
            functools.partial(held_kernel, len(pieces), narrow),
            out_shape=shapes,
            in_specs=[IN_VMEM] * (len(pieces) + 1) + [ANYWHERE],
            out_specs=[IN_VMEM] * len(sizes),
            scratch_shapes=scratch,
            compiler_params=params,
            cost_estimate=cost,
        )(*pieces, pltpu.with_memory_space_constraint(matrix, pltpu.VMEM), after)
    return pl.pallas_call(
        functools.partial(streamed_kernel, len(pieces), narrow),
        out_shape=shapes,
        grid=(width // tile,),
        in_specs=[IN_VMEM] * len(pieces)
        + [pl.BlockSpec((depth, tile), lambda i: (0, i)), ANYWHERE],
        out_specs=[pl.BlockSpec((size, tile), lambda i: (0, i)) for size in sizes],
        scratch_shapes=scratch,
        compiler_params=params,
        cost_estimate=cost,
    )(*pieces, pltpu.with_memory_space_constraint(matrix, pltpu.HBM), after)


def halving_step(parts, given, step, size):
    got = lax.ppermute(parts[0], "narrow", [(i, i ^ step) for i in range(size)])
    parts = list(parts[1:])
    sums, start = [], 0
    for part in parts:
        sums.append(part.astype(jnp.float32) + got[start : start + part.shape[0]].astype(jnp.float32))
        start += part.shape[0]
    if len(sums) > 1:
        sums[0] = sums[0].astype(jnp.bfloat16)
    return sums


def halving_sum(parts, step, size):
    while step < size:
        parts = halving_step(parts, None, step, size)
        step *= 2
    return parts[0]


def local(mesh_shape, target_states, source_states, target_gate, target_up, source_gate, source_up, token_ids, lengths, ratio_weight):
    wide, narrow = mesh_shape["wide"], mesh_shape["narrow"]
    own_rows = token_ids.shape[0]

    slot_count = own_rows // lengths.shape[0]
    slots = jnp.arange(slot_count, dtype=jnp.int32)
    live = (slots[None, :] < lengths[:, None]).reshape(-1).astype(jnp.float32)
    weight = ratio_weight[token_ids]

    target_pieces = gather_pieces(target_states, "wide", wide, False)
    (source_states,) = load((source_states,))
    source_pieces = gather_pieces(source_states, "wide", wide, True)
    target_gate, target_up = load((target_gate, target_up), (live, weight))

    gate = product(target_pieces, target_gate, narrow, True, live)
    upper = product(target_pieces, target_up, narrow, True, gate[0])
    gate = halving_step(gate, None, 1, narrow)
    source_g = product(source_pieces, source_gate, narrow, False, gate[0])
    upper = halving_step(upper, None, 1, narrow)
    source_u = product(source_pieces, source_up, narrow, False, upper[0])

    target_act = jax.nn.silu(halving_sum(gate, 2, narrow)) * halving_sum(upper, 2, narrow)
    target_out = (live[:, None] * target_act).astype(jnp.bfloat16)
    source_act = jax.nn.silu(halving_sum(source_g, 1, narrow)) * halving_sum(source_u, 1, narrow)
    ratio_out = (live[:, None] * (target_act - weight[:, None] * source_act)).astype(jnp.bfloat16)
    return (target_out, ratio_out)


def solution(mesh):
    placed = (
        P(("groups", "wide"), "narrow"),
        P(("groups", "wide"), "narrow"),
        P("narrow", "wide"),
        P("narrow", "wide"),
        P("narrow", "wide"),
        P("narrow", "wide"),
        P(("groups", "narrow")),
        P(("groups", "narrow")),
        P(),
    )
    mesh_shape = dict(mesh.shape)

    def body(*args):
        return local(mesh_shape, *args)

    return jax.shard_map(
        body,
        mesh=mesh,
        in_specs=placed,
        out_specs=(P(("groups", "narrow"), "wide"), P(("groups", "narrow"), "wide")),
        check_vma=False,
    )
```

```python
import functools
import math

import jax
import jax.numpy as jnp
from jax import lax
from jax.experimental import pallas as pl
from jax.experimental.pallas import tpu as pltpu
from jax.sharding import PartitionSpec as P

IN_VMEM = pl.BlockSpec(memory_space=pltpu.VMEM)
IN_SMEM = pl.BlockSpec(memory_space=pltpu.SMEM)
ANYWHERE = pl.BlockSpec(memory_space=pl.ANY)
LANES = 128


def in_hbm(array):
    return pltpu.with_memory_space_constraint(array, pltpu.HBM)


def in_vmem(array):
    return pltpu.with_memory_space_constraint(array, pltpu.VMEM)


def pass_kernel(piece, *refs):
    refs[-1][...] = piece[...]


def passed(piece, after):
    return pl.pallas_call(
        pass_kernel,
        out_shape=jax.ShapeDtypeStruct(piece.shape, piece.dtype),
        in_specs=[IN_VMEM] + [ANYWHERE] * len(after),
        out_specs=IN_VMEM,
        compiler_params=pltpu.CompilerParams(vmem_limit_bytes=1 << 20),
    )(piece, *after)


def gather_pieces(piece, axis, size, after=()):
    pieces = [piece]
    for offset in range(1, size):
        low = offset & -offset
        pairs = [(i, i ^ low) for i in range(size)]
        piece = pieces[offset ^ low]
        if after and offset != low:
            piece = passed(piece, after)
        pieces.append(lax.ppermute(piece, axis, pairs))
    return pieces


def halving_order(size):
    bits = size.bit_length() - 1
    reverse = [sum(((p >> b) & 1) << (bits - 1 - b) for b in range(bits)) for p in range(size)]
    return reverse[::-1]


def place_rows(pieces, rows, narrow):
    me_wide, me_narrow = lax.axis_index("wide"), lax.axis_index("narrow")
    piece_rows = pieces[0].shape[0]
    block_rows = piece_rows * len(pieces) // narrow
    size = math.gcd(piece_rows, block_rows)
    for offset, piece in enumerate(pieces):
        for start in range(0, piece_rows, size):
            row = (me_wide ^ offset) * piece_rows + start
            block = (row // block_rows) ^ me_narrow
            place = sum(
                jnp.where(block == known, position, 0)
                for position, known in enumerate(halving_order(narrow))
            )
            spot = pl.multiple_of(place * block_rows + row % block_rows, size)
            rows[pl.ds(spot, size), :] = piece[start : start + size, :]


def start_loads(sources, spans, dests, sems):
    copies = []
    for i, (source, (start, size)) in enumerate(zip(sources, spans)):
        copies.append(pltpu.make_async_copy(source.at[pl.ds(start, size), :], dests[i], sems.at[i]))
        copies[-1].start()
    return copies


def prepare_kernel(spans, slots, ids, lengths, table, *refs):
    count = len(spans)
    dests, live, weight = refs[count : 2 * count], refs[2 * count], refs[2 * count + 1]
    entries, picked, sems = refs[2 * count + 2 :]
    lookup = pltpu.make_async_copy(table, entries, sems.at[count])
    lookup.start()
    copies = start_loads(refs[:count], spans, dests, sems)
    for i in range(lengths.shape[0]):
        slot = lax.broadcasted_iota(jnp.int32, (slots, LANES), 0)
        live[i * slots : (i + 1) * slots, :] = (slot < lengths[i]).astype(jnp.float32)
    lookup.wait()

    def pick(i, carry):
        entry = ids[i]
        lane = lax.broadcasted_iota(jnp.int32, (1, LANES), 1)
        row = entries[pl.ds(entry // LANES, 1), :]
        picked[pl.ds(i, 1), :] = jnp.where(lane == entry % LANES, row, 0.0)
        return carry

    lax.fori_loop(0, ids.shape[0], pick, 0)
    weight[...] = jnp.broadcast_to(jnp.sum(picked[...], axis=1, keepdims=True), weight.shape)
    for copy in copies:
        copy.wait()


def prepare(loads, ids, lengths, table):
    spans = [span for _, span in loads]
    table = table.reshape(-1, LANES)
    flag = jax.ShapeDtypeStruct((ids.shape[0], LANES), jnp.float32)
    return pl.pallas_call(
        functools.partial(prepare_kernel, spans, ids.shape[0] // lengths.shape[0]),
        out_shape=[pltpu.VMEM((size, m.shape[1]), m.dtype) for m, (_, size) in loads] + [flag, flag],
        in_specs=[IN_SMEM, IN_SMEM, ANYWHERE] + [ANYWHERE] * len(loads),
        out_specs=[IN_VMEM] * (len(loads) + 2),
        scratch_shapes=[
            pltpu.VMEM(table.shape, table.dtype),
            pltpu.VMEM(flag.shape, flag.dtype),
            pltpu.SemaphoreType.DMA((len(loads) + 1,)),
        ],
        compiler_params=pltpu.CompilerParams(vmem_limit_bytes=3 << 20),
    )(*map(in_hbm, (ids, lengths, table, *(m for m, _ in loads))))


def load_kernel(spans, after, *refs):
    dests = refs[len(spans) + after : -1]
    for copy in start_loads(refs[: len(spans)], spans, dests, refs[-1]):
        copy.wait()


def halves(matrix):
    half = matrix.shape[0] // 2
    return [(matrix, (0, half)), (matrix, (half, half))]


def load(loads, after):
    return pl.pallas_call(
        functools.partial(load_kernel, [span for _, span in loads], len(after)),
        out_shape=[pltpu.VMEM((size, m.shape[1]), m.dtype) for m, (_, size) in loads],
        in_specs=[ANYWHERE] * (len(loads) + len(after)),
        out_specs=[IN_VMEM] * len(loads),
        scratch_shapes=[pltpu.SemaphoreType.DMA((len(loads),))],
        compiler_params=pltpu.CompilerParams(vmem_limit_bytes=1 << 20),
    )(*(in_hbm(m) for m, _ in loads), *after)


def tile_of(cols):
    for tile in (512, 256, 128):
        if cols % tile == 0:
            return tile
    return cols


def product_kernel(pieces, parts, spans, after, narrow, placing, *refs):
    tokens, matrices = refs[:pieces], refs[pieces : pieces + parts]
    start = pieces + parts
    sources = refs[start : start + len(spans)]
    start += len(spans) + after
    dests = refs[start : start + len(spans)]
    start += len(spans)
    outs, sems = refs[start:-1], refs[-1]
    copies = start_loads(sources, spans, dests, sems)
    if placing:
        place_rows(tokens, outs[0], narrow)
        tokens, outs = outs[:1], outs[1:]
    width = matrices[0].shape[1]
    tile = tile_of(width)
    for column in range(0, width, tile):
        cols = slice(column, column + tile)
        total, depth = None, 0
        for matrix in matrices:
            rows = tokens[0][:, depth : depth + matrix.shape[0]]
            term = jnp.dot(rows, matrix[:, cols], preferred_element_type=jnp.float32)
            total = term if total is None else total + term
            depth += matrix.shape[0]
        row = 0
        for out in outs:
            out[:, cols] = total[row : row + out.shape[0]].astype(out.dtype)
            row += out.shape[0]
    for copy in copies:
        copy.wait()


def product(tokens, matrices, narrow, after=(), loads=()):
    placing = len(tokens) > 1
    total = sum(t.shape[0] for t in tokens)
    depth, width = tokens[0].shape[1], matrices[0].shape[1]
    sizes, left = [], total
    while left > total // narrow:
        left //= 2
        sizes.append(left)
    sizes.append(left)
    spans = [span for _, span in loads]
    found = pl.pallas_call(
        functools.partial(product_kernel, len(tokens), len(matrices), spans, len(after), narrow, placing),
        out_shape=[pltpu.VMEM((size, m.shape[1]), m.dtype) for m, (_, size) in loads]
        + [jax.ShapeDtypeStruct((total, depth), tokens[0].dtype)] * placing
        + [jax.ShapeDtypeStruct((size, width), jnp.bfloat16) for size in sizes],
        in_specs=[IN_VMEM] * (len(tokens) + len(matrices)) + [ANYWHERE] * (len(loads) + len(after)),
        out_specs=[IN_VMEM] * (len(loads) + placing + len(sizes)),
        scratch_shapes=[pltpu.SemaphoreType.DMA((max(1, len(loads)),))],
        compiler_params=pltpu.CompilerParams(vmem_limit_bytes=6 << 20),
    )(*tokens, *map(in_vmem, matrices), *(in_hbm(m) for m, _ in loads), *after)
    loaded, found = found[: len(loads)], found[len(loads) :]
    return loaded, (found[:1] if placing else tokens), found[placing:]


def next_kernel(behind, count, *refs):
    part, out = refs[0], refs[-1]
    for cols in column_tiles(out.shape[1]):
        total = part[:, cols].astype(jnp.float32)
        for came in refs[1:count]:
            start = came.shape[0] - behind - part.shape[0]
            total += came[start : start + part.shape[0], cols].astype(jnp.float32)
        out[:, cols] = total.astype(out.dtype)


def next_part(parts, got, after):
    step = len(got)
    behind = sum(part.shape[0] for part in parts[step + 1 :])
    return pl.pallas_call(
        functools.partial(next_kernel, behind, 1 + step),
        out_shape=jax.ShapeDtypeStruct(parts[step].shape, jnp.bfloat16),
        in_specs=[IN_VMEM] * (1 + step) + [ANYWHERE] * len(after),
        out_specs=IN_VMEM,
        compiler_params=pltpu.CompilerParams(vmem_limit_bytes=4 << 20),
    )(parts[step], *got, *after)


def exchange(send, step, size):
    return lax.ppermute(send, "narrow", [(i, i ^ (1 << step)) for i in range(size)])


def finish(parts, got, size, after):
    send = parts[0]
    while (1 << len(got)) < size:
        send = next_part(parts, got, after)
        got = got + [exchange(send, len(got), size)]
    return send, [parts[-1]] + got


def own_sum(refs, cols):
    count = refs[0].shape[0]
    return sum(ref[ref.shape[0] - count :, cols].astype(jnp.float32) for ref in refs)


def column_tiles(width):
    tile = tile_of(width)
    return [slice(start, start + tile) for start in range(0, width, tile)]


def target_kernel(count, live, *refs):
    gate, upper, act, out = refs[:count], refs[count : 2 * count], refs[-2], refs[-1]
    for cols in column_tiles(out.shape[1]):
        value = live[:, :1] * (jax.nn.silu(own_sum(gate, cols)) * own_sum(upper, cols))
        act[:, cols] = value
        out[:, cols] = value.astype(out.dtype)


def target_end(live, gate, upper, after):
    shape = gate[0].shape
    return pl.pallas_call(
        functools.partial(target_kernel, len(gate)),
        out_shape=[jax.ShapeDtypeStruct(shape, jnp.float32), jax.ShapeDtypeStruct(shape, jnp.bfloat16)],
        in_specs=[IN_VMEM] * (1 + len(gate) + len(upper)) + [ANYWHERE] * len(after),
        out_specs=[IN_VMEM] * 2,
        compiler_params=pltpu.CompilerParams(vmem_limit_bytes=6 << 20),
    )(live, *gate, *upper, *after)


def source_kernel(live, weight, *refs):
    gate, out = refs[:-1], refs[-1]
    for cols in column_tiles(out.shape[1]):
        out[:, cols] = (live[:, :1] * weight[:, :1]) * jax.nn.silu(own_sum(gate, cols))


def source_middle(live, weight, gate):
    return pl.pallas_call(
        source_kernel,
        out_shape=jax.ShapeDtypeStruct(gate[0].shape, jnp.float32),
        in_specs=[IN_VMEM] * (2 + len(gate)),
        out_specs=IN_VMEM,
        compiler_params=pltpu.CompilerParams(vmem_limit_bytes=6 << 20),
    )(live, weight, *gate)


def ratio_kernel(act, gated, *refs):
    upper, out = refs[:-1], refs[-1]
    for cols in column_tiles(out.shape[1]):
        out[:, cols] = (act[:, cols] - gated[:, cols] * own_sum(upper, cols)).astype(out.dtype)


def ratio_end(act, gated, upper):
    return pl.pallas_call(
        ratio_kernel,
        out_shape=jax.ShapeDtypeStruct(act.shape, jnp.bfloat16),
        in_specs=[IN_VMEM] * (2 + len(upper)),
        out_specs=IN_VMEM,
        compiler_params=pltpu.CompilerParams(vmem_limit_bytes=6 << 20),
    )(act, gated, *upper)


def local(mesh_shape, target_states, source_states, target_gate, target_up, source_gate, source_up, token_ids, lengths, ratio_weight):
    wide, narrow = mesh_shape["wide"], mesh_shape["narrow"]
    gate_top, gate_bottom = halves(source_gate)
    up_top, up_bottom = halves(source_up)

    *target_gate, live, weight = prepare(halves(target_gate), token_ids, lengths, ratio_weight)
    target_pieces = gather_pieces(target_states, "wide", wide, (live,))
    source_pieces = gather_pieces(source_states, "wide", wide)
    target_up = load(halves(target_up), (live, target_pieces[wide // 2]))

    after = (target_up[0], source_pieces[1], source_pieces[wide // 2])
    _, rows, gate = product(target_pieces, target_gate, narrow, after)
    gate_came = [exchange(gate[0], 0, narrow)]
    (gate_top,), _, upper = product(rows, target_up, narrow, (gate[0],), [gate_top])
    upper_came = [exchange(upper[0], 0, narrow)]
    sent, gate = finish(gate, gate_came, narrow, (upper[0],))
    gate_bottom, up_top = load([gate_bottom, up_top], (sent,))
    sent, upper = finish(upper, upper_came, narrow, (gate_bottom, source_pieces[-1]))

    (up_bottom,), rows, source_g = product(
        source_pieces, (gate_top, gate_bottom), narrow, (sent,), [up_bottom]
    )
    gate_came = [exchange(source_g[0], 0, narrow)]
    _, _, source_u = product(rows, (up_top, up_bottom), narrow, (source_g[0], gate[-1], upper[-1]))
    upper_came = [exchange(source_u[0], 0, narrow)]
    sent, source_g = finish(source_g, gate_came, narrow, (source_u[0],))
    act, target_out = target_end(live, gate, upper, (sent,))
    _, source_u = finish(source_u, upper_came, narrow, (act,))
    gated = source_middle(live, weight, source_g)
    ratio_out = ratio_end(act, gated, source_u)
    return (target_out, ratio_out)


def solution(mesh):
    placed = (
        P(("groups", "wide"), "narrow"),
        P(("groups", "wide"), "narrow"),
        P("narrow", "wide"),
        P("narrow", "wide"),
        P("narrow", "wide"),
        P("narrow", "wide"),
        P(("groups", "narrow")),
        P(("groups", "narrow")),
        P(),
    )
    mesh_shape = dict(mesh.shape)

    def body(*args):
        return local(mesh_shape, *args)

    return jax.shard_map(
        body,
        mesh=mesh,
        in_specs=placed,
        out_specs=(P(("groups", "narrow"), "wide"), P(("groups", "narrow"), "wide")),
        check_vma=False,
    )
```

```python
import functools
import math

import jax
import jax.numpy as jnp
from jax import lax
from jax.experimental import pallas as pl
from jax.experimental.pallas import tpu as pltpu
from jax.sharding import PartitionSpec as P

IN_VMEM = pl.BlockSpec(memory_space=pltpu.VMEM)
IN_SMEM = pl.BlockSpec(memory_space=pltpu.SMEM)
ANYWHERE = pl.BlockSpec(memory_space=pl.ANY)
LANES = 128


def in_hbm(array):
    return pltpu.with_memory_space_constraint(array, pltpu.HBM)


def in_vmem(array):
    return pltpu.with_memory_space_constraint(array, pltpu.VMEM)


def pass_kernel(piece, *refs):
    refs[-1][...] = piece[...]


def passed(piece, after):
    return pl.pallas_call(
        pass_kernel,
        out_shape=jax.ShapeDtypeStruct(piece.shape, piece.dtype),
        in_specs=[IN_VMEM] + [ANYWHERE] * len(after),
        out_specs=IN_VMEM,
        compiler_params=pltpu.CompilerParams(vmem_limit_bytes=1 << 20),
    )(piece, *after)


def gather_pieces(piece, axis, size, after=()):
    pieces = [piece]
    for offset in range(1, size):
        low = offset & -offset
        pairs = [(i, i ^ low) for i in range(size)]
        piece = pieces[offset ^ low]
        if after and offset != low:
            piece = passed(piece, after)
        pieces.append(lax.ppermute(piece, axis, pairs))
    return pieces


def halving_order(size):
    bits = size.bit_length() - 1
    reverse = [sum(((p >> b) & 1) << (bits - 1 - b) for b in range(bits)) for p in range(size)]
    return reverse[::-1]


def place_rows(pieces, rows, narrow):
    me_wide, me_narrow = lax.axis_index("wide"), lax.axis_index("narrow")
    piece_rows = pieces[0].shape[0]
    block_rows = piece_rows * len(pieces) // narrow
    size = math.gcd(piece_rows, block_rows)
    for offset, piece in enumerate(pieces):
        for start in range(0, piece_rows, size):
            row = (me_wide ^ offset) * piece_rows + start
            block = (row // block_rows) ^ me_narrow
            place = sum(
                jnp.where(block == known, position, 0)
                for position, known in enumerate(halving_order(narrow))
            )
            spot = pl.multiple_of(place * block_rows + row % block_rows, size)
            rows[pl.ds(spot, size), :] = piece[start : start + size, :]


def start_loads(sources, spans, dests, sems):
    copies = []
    for i, (source, (start, size)) in enumerate(zip(sources, spans)):
        copies.append(pltpu.make_async_copy(source.at[pl.ds(start, size), :], dests[i], sems.at[i]))
        copies[-1].start()
    return copies


def look_up_kernel(slots, ids, lengths, table, *refs):
    live, weight, entries, picked, sem = refs[-5:]
    lookup = pltpu.make_async_copy(table, entries, sem)
    lookup.start()
    for i in range(lengths.shape[0]):
        slot = lax.broadcasted_iota(jnp.int32, (slots, LANES), 0)
        live[i * slots : (i + 1) * slots, :] = (slot < lengths[i]).astype(jnp.float32)
    lookup.wait()

    def pick(i, carry):
        entry = ids[i]
        lane = lax.broadcasted_iota(jnp.int32, (1, LANES), 1)
        row = entries[pl.ds(entry // LANES, 1), :]
        picked[pl.ds(i, 1), :] = jnp.where(lane == entry % LANES, row, 0.0)
        return carry

    lax.fori_loop(0, ids.shape[0], pick, 0)
    weight[...] = jnp.broadcast_to(jnp.sum(picked[...], axis=1, keepdims=True), weight.shape)


def look_up(ids, lengths, table, after):
    table = table.reshape(-1, LANES)
    flag = jax.ShapeDtypeStruct((ids.shape[0], LANES), jnp.float32)
    return pl.pallas_call(
        functools.partial(look_up_kernel, ids.shape[0] // lengths.shape[0]),
        out_shape=[flag, flag],
        in_specs=[IN_SMEM, IN_SMEM] + [ANYWHERE] * (1 + len(after)),
        out_specs=[IN_VMEM, IN_VMEM],
        scratch_shapes=[
            pltpu.VMEM(table.shape, table.dtype),
            pltpu.VMEM(flag.shape, flag.dtype),
            pltpu.SemaphoreType.DMA,
        ],
        compiler_params=pltpu.CompilerParams(vmem_limit_bytes=3 << 20),
    )(*map(in_hbm, (ids, lengths, table)), *after)


def load_kernel(spans, after, *refs):
    dests = refs[len(spans) + after : -1]
    for copy in start_loads(refs[: len(spans)], spans, dests, refs[-1]):
        copy.wait()


def halves(matrix):
    half = matrix.shape[0] // 2
    return [(matrix, (0, half)), (matrix, (half, half))]


def load(loads, after):
    return pl.pallas_call(
        functools.partial(load_kernel, [span for _, span in loads], len(after)),
        out_shape=[pltpu.VMEM((size, m.shape[1]), m.dtype) for m, (_, size) in loads],
        in_specs=[ANYWHERE] * (len(loads) + len(after)),
        out_specs=[IN_VMEM] * len(loads),
        scratch_shapes=[pltpu.SemaphoreType.DMA((len(loads),))],
        compiler_params=pltpu.CompilerParams(vmem_limit_bytes=1 << 20),
    )(*(in_hbm(m) for m, _ in loads), *after)


def tile_of(cols):
    for tile in (512, 256, 128):
        if cols % tile == 0:
            return tile
    return cols


def column_tiles(width):
    tile = tile_of(width)
    return [slice(start, start + tile) for start in range(0, width, tile)]


def product_kernel(pieces, groups, spans, after, narrow, *refs):
    tokens, refs = refs[:pieces], refs[pieces:]
    matrices = []
    for count in groups:
        matrices.append(refs[:count])
        refs = refs[count:]
    sources, refs = refs[: len(spans)], refs[len(spans) + after :]
    dests, outs, sems = refs[: len(spans)], refs[len(spans) : -1], refs[-1]
    copies = start_loads(sources, spans, dests, sems)
    if pieces > 1:
        place_rows(tokens, outs[0], narrow)
        tokens, outs = outs[:1], outs[1:]
    first = 0
    for group in matrices:
        width = group[0].shape[1]
        for cols in column_tiles(width):
            total, depth = None, 0
            for matrix in group:
                rows = tokens[0][:, depth : depth + matrix.shape[0]]
                term = jnp.dot(rows, matrix[:, cols], preferred_element_type=jnp.float32)
                total = term if total is None else total + term
                depth += matrix.shape[0]
            row = 0
            for out in outs:
                out[:, first + cols.start : first + cols.stop] = total[row : row + out.shape[0]].astype(out.dtype)
                row += out.shape[0]
        first += width
    for copy in copies:
        copy.wait()


def part_sizes(total, narrow):
    sizes, left = [], total // 2
    while left > total // narrow:
        left //= 2
        sizes.append(left)
    return sizes + [left]


def product(tokens, groups, narrow, after=(), loads=()):
    placing = len(tokens) > 1
    total = sum(t.shape[0] for t in tokens)
    depth, width = tokens[0].shape[1], sum(group[0].shape[1] for group in groups)
    matrices = [in_vmem(part) for group in groups for part in group]
    sizes = part_sizes(total, narrow)
    found = pl.pallas_call(
        functools.partial(
            product_kernel,
            len(tokens),
            [len(group) for group in groups],
            [span for _, span in loads],
            len(after),
            narrow,
        ),
        out_shape=[pltpu.VMEM((size, m.shape[1]), m.dtype) for m, (_, size) in loads]
        + [jax.ShapeDtypeStruct((total, depth), tokens[0].dtype)] * placing
        + [jax.ShapeDtypeStruct((size, width), jnp.bfloat16) for size in sizes * 2],
        in_specs=[IN_VMEM] * (len(tokens) + len(matrices)) + [ANYWHERE] * (len(loads) + len(after)),
        out_specs=[IN_VMEM] * (len(loads) + placing + 2 * len(sizes)),
        scratch_shapes=[pltpu.SemaphoreType.DMA((max(1, len(loads)),))],
        compiler_params=pltpu.CompilerParams(vmem_limit_bytes=6 << 20),
    )(*tokens, *matrices, *(in_hbm(m) for m, _ in loads), *after)
    loaded, found = found[: len(loads)], found[len(loads) :]
    rows, found = (found[:1], found[1:]) if placing else (tokens, found)
    return loaded, rows, found[: len(sizes)], found[len(sizes) :]


def exchange(array, step, size):
    return lax.ppermute(array, "narrow", [(i, i ^ (1 << step)) for i in range(size)])


def addends(parts, came, k):
    found = [(parts[k], 0)]
    for array, first, behind in came:
        if first <= k < behind:
            found.append((array, sum(part.shape[0] for part in parts[first:k])))
    return [array for array, _ in found], tuple(start for _, start in found)


def added(refs, starts, count, cols):
    return sum(
        ref[start : start + count, cols].astype(jnp.float32) for ref, start in zip(refs, starts)
    )


def next_kernel(starts, *refs):
    out = refs[-1]
    for cols in column_tiles(out.shape[1]):
        out[:, cols] = added(refs, starts, out.shape[0], cols).astype(out.dtype)


def finish(sends, keeps, narrow, after):
    came = [(exchange(send, 0, narrow), k, k + 1) for k, send in enumerate(sends)]
    sent = sends[0]
    for k in range(len(keeps) - 1):
        arrays, starts = addends(keeps, came, k)
        sent = pl.pallas_call(
            functools.partial(next_kernel, starts),
            out_shape=jax.ShapeDtypeStruct(keeps[k].shape, jnp.bfloat16),
            in_specs=[IN_VMEM] * len(arrays) + [ANYWHERE] * len(after),
            out_specs=IN_VMEM,
            compiler_params=pltpu.CompilerParams(vmem_limit_bytes=4 << 20),
        )(*arrays, *after)
        came.append((exchange(sent, k + 1, narrow), k + 1, len(keeps)))
    return sent, addends(keeps, came, len(keeps) - 1)


def own_sum(refs, starts, count, first, cols):
    return added(refs, starts, count, slice(first + cols.start, first + cols.stop))


def target_kernel(starts, live, *refs):
    terms, act, out = refs[: len(starts)], refs[-2], refs[-1]
    count, width = out.shape
    for cols in column_tiles(width):
        gate = own_sum(terms, starts, count, 0, cols)
        upper = own_sum(terms, starts, count, width, cols)
        value = live[:, :1] * (jax.nn.silu(gate) * upper)
        act[:, cols] = value
        out[:, cols] = value.astype(out.dtype)


def target_end(live, own):
    arrays, starts = own
    shape = (live.shape[0], arrays[0].shape[1] // 2)
    return pl.pallas_call(
        functools.partial(target_kernel, starts),
        out_shape=[jax.ShapeDtypeStruct(shape, jnp.float32), jax.ShapeDtypeStruct(shape, jnp.bfloat16)],
        in_specs=[IN_VMEM] * (1 + len(arrays)),
        out_specs=[IN_VMEM] * 2,
        compiler_params=pltpu.CompilerParams(vmem_limit_bytes=6 << 20),
    )(live, *arrays)


def source_kernel(starts, live, weight, *refs):
    terms, out = refs[:-1], refs[-1]
    for cols in column_tiles(out.shape[1]):
        gate = own_sum(terms, starts, out.shape[0], 0, cols)
        out[:, cols] = (live[:, :1] * weight[:, :1]) * jax.nn.silu(gate)


def source_middle(live, weight, own):
    arrays, starts = own
    return pl.pallas_call(
        functools.partial(source_kernel, starts),
        out_shape=jax.ShapeDtypeStruct((live.shape[0], arrays[0].shape[1]), jnp.float32),
        in_specs=[IN_VMEM] * (2 + len(arrays)),
        out_specs=IN_VMEM,
        compiler_params=pltpu.CompilerParams(vmem_limit_bytes=6 << 20),
    )(live, weight, *arrays)


def ratio_kernel(starts, act, gated, *refs):
    terms, out = refs[:-1], refs[-1]
    for cols in column_tiles(out.shape[1]):
        upper = own_sum(terms, starts, out.shape[0], 0, cols)
        out[:, cols] = (act[:, cols] - gated[:, cols] * upper).astype(out.dtype)


def ratio_end(act, gated, own):
    arrays, starts = own
    return pl.pallas_call(
        functools.partial(ratio_kernel, starts),
        out_shape=jax.ShapeDtypeStruct(act.shape, jnp.bfloat16),
        in_specs=[IN_VMEM] * (2 + len(arrays)),
        out_specs=IN_VMEM,
        compiler_params=pltpu.CompilerParams(vmem_limit_bytes=6 << 20),
    )(act, gated, *arrays)


def local(mesh_shape, target_states, source_states, target_gate, target_up, source_gate, source_up, token_ids, lengths, ratio_weight):
    wide, narrow = mesh_shape["wide"], mesh_shape["narrow"]
    gate_top, gate_bottom = halves(source_gate)

    target_gate = load(halves(target_gate), ())
    target_pieces = gather_pieces(target_states, "wide", wide, (target_gate[0],))
    source_pieces = gather_pieces(source_states, "wide", wide)
    target_up = load(halves(target_up), (target_gate[0], target_pieces[wide // 2]))

    after = (target_up[0], source_pieces[1], source_pieces[wide // 2])
    _, _, sends, keeps = product(target_pieces, (target_gate, target_up), narrow, after)
    (gate_top,) = load([gate_top], (sends[0],))
    sent, target = finish(sends, keeps, narrow, (gate_top, source_pieces[-1]))
    (gate_bottom,) = load([gate_bottom], (sent,))

    source_up, rows, gate_sends, gate_keeps = product(
        source_pieces, ((gate_top, gate_bottom),), narrow, (sent,), halves(source_up)
    )
    _, _, sends, keeps = product(rows, (source_up,), narrow, (gate_sends[0],))
    sent, source_g = finish(gate_sends, gate_keeps, narrow, (sends[0], target[0][-1]))
    live, weight = look_up(token_ids, lengths, ratio_weight, (sent,))
    act, target_out = target_end(live, target)
    _, source_u = finish(sends, keeps, narrow, (act,))
    gated = source_middle(live, weight, source_g)
    ratio_out = ratio_end(act, gated, source_u)
    return (target_out, ratio_out)


def solution(mesh):
    placed = (
        P(("groups", "wide"), "narrow"),
        P(("groups", "wide"), "narrow"),
        P("narrow", "wide"),
        P("narrow", "wide"),
        P("narrow", "wide"),
        P("narrow", "wide"),
        P(("groups", "narrow")),
        P(("groups", "narrow")),
        P(),
    )
    mesh_shape = dict(mesh.shape)

    def body(*args):
        return local(mesh_shape, *args)

    return jax.shard_map(
        body,
        mesh=mesh,
        in_specs=placed,
        out_specs=(P(("groups", "narrow"), "wide"), P(("groups", "narrow"), "wide")),
        check_vma=False,
    )
```

```python
import functools
import math

import jax
import jax.numpy as jnp
from jax import lax
from jax.experimental import pallas as pl
from jax.experimental.pallas import tpu as pltpu
from jax.sharding import PartitionSpec as P

IN_VMEM = pl.BlockSpec(memory_space=pltpu.VMEM)
IN_SMEM = pl.BlockSpec(memory_space=pltpu.SMEM)
ANYWHERE = pl.BlockSpec(memory_space=pl.ANY)
LANES = 128


def in_hbm(array):
    return pltpu.with_memory_space_constraint(array, pltpu.HBM)


def in_vmem(array):
    return pltpu.with_memory_space_constraint(array, pltpu.VMEM)


def pass_kernel(piece, *refs):
    refs[-1][...] = piece[...]


def passed(piece, after):
    return pl.pallas_call(
        pass_kernel,
        out_shape=jax.ShapeDtypeStruct(piece.shape, piece.dtype),
        in_specs=[IN_VMEM] + [ANYWHERE] * len(after),
        out_specs=IN_VMEM,
        compiler_params=pltpu.CompilerParams(vmem_limit_bytes=1 << 20),
    )(piece, *after)


def gather_pieces(piece, axis, size, after=()):
    pieces = [piece]
    for offset in range(1, size):
        low = offset & -offset
        pairs = [(i, i ^ low) for i in range(size)]
        piece = pieces[offset ^ low]
        if after and offset != low:
            piece = passed(piece, after)
        pieces.append(lax.ppermute(piece, axis, pairs))
    return pieces


def halving_order(size):
    bits = size.bit_length() - 1
    reverse = [sum(((p >> b) & 1) << (bits - 1 - b) for b in range(bits)) for p in range(size)]
    return reverse[::-1]


def place_rows(pieces, rows, narrow):
    me_wide, me_narrow = lax.axis_index("wide"), lax.axis_index("narrow")
    piece_rows = pieces[0].shape[0]
    block_rows = piece_rows * len(pieces) // narrow
    size = math.gcd(piece_rows, block_rows)
    for offset, piece in enumerate(pieces):
        for start in range(0, piece_rows, size):
            row = (me_wide ^ offset) * piece_rows + start
            block = (row // block_rows) ^ me_narrow
            place = sum(
                jnp.where(block == known, position, 0)
                for position, known in enumerate(halving_order(narrow))
            )
            spot = pl.multiple_of(place * block_rows + row % block_rows, size)
            rows[pl.ds(spot, size), :] = piece[start : start + size, :]


def start_loads(sources, spans, dests, sems):
    copies = []
    for i, (source, (start, size)) in enumerate(zip(sources, spans)):
        copies.append(pltpu.make_async_copy(source.at[pl.ds(start, size), :], dests[i], sems.at[i]))
        copies[-1].start()
    return copies


def look_up_kernel(slots, ids, lengths, table, *refs):
    live, weight, entries, picked, sem = refs[-5:]
    lookup = pltpu.make_async_copy(table, entries, sem)
    lookup.start()
    for i in range(lengths.shape[0]):
        slot = lax.broadcasted_iota(jnp.int32, (slots, LANES), 0)
        live[i * slots : (i + 1) * slots, :] = (slot < lengths[i]).astype(jnp.float32)
    lookup.wait()

    def pick(i, carry):
        entry = ids[i]
        lane = lax.broadcasted_iota(jnp.int32, (1, LANES), 1)
        row = entries[pl.ds(entry // LANES, 1), :]
        picked[pl.ds(i, 1), :] = jnp.where(lane == entry % LANES, row, 0.0)
        return carry

    lax.fori_loop(0, ids.shape[0], pick, 0)
    weight[...] = jnp.broadcast_to(jnp.sum(picked[...], axis=1, keepdims=True), weight.shape)


def look_up(ids, lengths, table, after):
    table = table.reshape(-1, LANES)
    flag = jax.ShapeDtypeStruct((ids.shape[0], LANES), jnp.float32)
    return pl.pallas_call(
        functools.partial(look_up_kernel, ids.shape[0] // lengths.shape[0]),
        out_shape=[flag, flag],
        in_specs=[IN_SMEM, IN_SMEM] + [ANYWHERE] * (1 + len(after)),
        out_specs=[IN_VMEM, IN_VMEM],
        scratch_shapes=[
            pltpu.VMEM(table.shape, table.dtype),
            pltpu.VMEM(flag.shape, flag.dtype),
            pltpu.SemaphoreType.DMA,
        ],
        compiler_params=pltpu.CompilerParams(vmem_limit_bytes=3 << 20),
    )(*map(in_hbm, (ids, lengths, table)), *after)


def load_kernel(spans, after, *refs):
    dests = refs[len(spans) + after : -1]
    for copy in start_loads(refs[: len(spans)], spans, dests, refs[-1]):
        copy.wait()


def halves(matrix):
    half = matrix.shape[0] // 2
    return [(matrix, (0, half)), (matrix, (half, half))]


def load(loads, after):
    return pl.pallas_call(
        functools.partial(load_kernel, [span for _, span in loads], len(after)),
        out_shape=[pltpu.VMEM((size, m.shape[1]), m.dtype) for m, (_, size) in loads],
        in_specs=[ANYWHERE] * (len(loads) + len(after)),
        out_specs=[IN_VMEM] * len(loads),
        scratch_shapes=[pltpu.SemaphoreType.DMA((len(loads),))],
        compiler_params=pltpu.CompilerParams(vmem_limit_bytes=1 << 20),
    )(*(in_hbm(m) for m, _ in loads), *after)


def tile_of(cols):
    for tile in (512, 256, 128):
        if cols % tile == 0:
            return tile
    return cols


def column_tiles(width):
    tile = tile_of(width)
    return [slice(start, start + tile) for start in range(0, width, tile)]


def shifted(cols, first):
    return slice(first + cols.start, first + cols.stop)


def product_kernel(pieces, groups, chunk, spans, after, narrow, *refs):
    tokens, refs = refs[:pieces], refs[pieces:]
    matrices = []
    for count in groups:
        matrices.append(refs[:count])
        refs = refs[count:]
    sources, refs = refs[: len(spans)], refs[len(spans) + after :]
    dests, outs, sems = refs[: len(spans)], refs[len(spans) : -1], refs[-1]
    copies = start_loads(sources, spans, dests, sems)
    if pieces > 1:
        place_rows(tokens, outs[0], narrow)
        tokens, outs = outs[:1], outs[1:]
    begin, width = chunk
    for place, group in enumerate(matrices):
        for cols in column_tiles(width):
            total, depth = None, 0
            for matrix in group:
                rows = tokens[0][:, depth : depth + matrix.shape[0]]
                part = matrix[:, begin + cols.start : begin + cols.stop]
                term = jnp.dot(rows, part, preferred_element_type=jnp.float32)
                total = term if total is None else total + term
                depth += matrix.shape[0]
            cols, row = shifted(cols, place * width), 0
            for out in outs:
                out[:, cols] = total[row : row + out.shape[0]].astype(out.dtype)
                row += out.shape[0]
    for copy in copies:
        copy.wait()


def part_sizes(total, narrow):
    sizes, left = [], total // 2
    while left > total // narrow:
        left //= 2
        sizes.append(left)
    return sizes + [left]


def product(tokens, groups, chunk, narrow, after=(), loads=()):
    placing = len(tokens) > 1
    total = sum(t.shape[0] for t in tokens)
    depth, width = tokens[0].shape[1], chunk[1] * len(groups)
    matrices = [in_vmem(part) for group in groups for part in group]
    sizes = part_sizes(total, narrow)
    found = pl.pallas_call(
        functools.partial(
            product_kernel,
            len(tokens),
            [len(group) for group in groups],
            chunk,
            [span for _, span in loads],
            len(after),
            narrow,
        ),
        out_shape=[pltpu.VMEM((size, m.shape[1]), m.dtype) for m, (_, size) in loads]
        + [jax.ShapeDtypeStruct((total, depth), tokens[0].dtype)] * placing
        + [jax.ShapeDtypeStruct((size, width), jnp.bfloat16) for size in sizes * 2],
        in_specs=[IN_VMEM] * (len(tokens) + len(matrices)) + [ANYWHERE] * (len(loads) + len(after)),
        out_specs=[IN_VMEM] * (len(loads) + placing + 2 * len(sizes)),
        scratch_shapes=[pltpu.SemaphoreType.DMA((max(1, len(loads)),))],
        compiler_params=pltpu.CompilerParams(vmem_limit_bytes=6 << 20),
    )(*tokens, *matrices, *(in_hbm(m) for m, _ in loads), *after)
    loaded, found = found[: len(loads)], found[len(loads) :]
    rows, found = (found[:1], found[1:]) if placing else (tokens, found)
    return loaded, rows, found[: len(sizes)], found[len(sizes) :]


def exchange(array, step, size):
    return lax.ppermute(array, "narrow", [(i, i ^ (1 << step)) for i in range(size)])


def addends(parts, came, k):
    found = [(parts[k], 0)]
    for array, first, behind in came:
        if first <= k < behind:
            found.append((array, sum(part.shape[0] for part in parts[first:k])))
    return [array for array, _ in found], tuple(start for _, start in found)


def added(refs, starts, count, cols):
    return sum(
        ref[start : start + count, cols].astype(jnp.float32) for ref, start in zip(refs, starts)
    )


def next_kernel(starts, *refs):
    out = refs[-1]
    for cols in column_tiles(out.shape[1]):
        out[:, cols] = added(refs, starts, out.shape[0], cols).astype(out.dtype)


def finish(sends, keeps, narrow, after):
    came = [(exchange(send, 0, narrow), k, k + 1) for k, send in enumerate(sends)]
    sent = sends[0]
    for k in range(len(keeps) - 1):
        arrays, starts = addends(keeps, came, k)
        sent = pl.pallas_call(
            functools.partial(next_kernel, starts),
            out_shape=jax.ShapeDtypeStruct(keeps[k].shape, jnp.bfloat16),
            in_specs=[IN_VMEM] * len(arrays) + [ANYWHERE] * len(after),
            out_specs=IN_VMEM,
            compiler_params=pltpu.CompilerParams(vmem_limit_bytes=4 << 20),
        )(*arrays, *after)
        came.append((exchange(sent, k + 1, narrow), k + 1, len(keeps)))
    return sent, addends(keeps, came, len(keeps) - 1)


def target_kernel(chunks, starts, live, *refs):
    act, out = refs[-2:]
    for (first, width), offsets in zip(chunks, starts):
        terms, refs = refs[: len(offsets)], refs[len(offsets) :]
        for cols in column_tiles(width):
            gate = added(terms, offsets, out.shape[0], cols)
            upper = added(terms, offsets, out.shape[0], shifted(cols, width))
            value = live[:, :1] * (jax.nn.silu(gate) * upper)
            act[:, shifted(cols, first)] = value
            out[:, shifted(cols, first)] = value.astype(out.dtype)


def target_end(live, chunks, owns):
    arrays = [array for own in owns for array in own[0]]
    shape = (live.shape[0], sum(width for _, width in chunks))
    return pl.pallas_call(
        functools.partial(target_kernel, chunks, [own[1] for own in owns]),
        out_shape=[jax.ShapeDtypeStruct(shape, jnp.float32), jax.ShapeDtypeStruct(shape, jnp.bfloat16)],
        in_specs=[IN_VMEM] * (1 + len(arrays)),
        out_specs=[IN_VMEM] * 2,
        compiler_params=pltpu.CompilerParams(vmem_limit_bytes=6 << 20),
    )(live, *arrays)


def source_kernel(starts, live, weight, *refs):
    terms, out = refs[:-1], refs[-1]
    for cols in column_tiles(out.shape[1]):
        gate = added(terms, starts, out.shape[0], cols)
        out[:, cols] = (live[:, :1] * weight[:, :1]) * jax.nn.silu(gate)


def source_middle(live, weight, own):
    arrays, starts = own
    return pl.pallas_call(
        functools.partial(source_kernel, starts),
        out_shape=jax.ShapeDtypeStruct((live.shape[0], arrays[0].shape[1]), jnp.float32),
        in_specs=[IN_VMEM] * (2 + len(arrays)),
        out_specs=IN_VMEM,
        compiler_params=pltpu.CompilerParams(vmem_limit_bytes=6 << 20),
    )(live, weight, *arrays)


def ratio_kernel(starts, act, gated, *refs):
    terms, out = refs[:-1], refs[-1]
    for cols in column_tiles(out.shape[1]):
        upper = added(terms, starts, out.shape[0], cols)
        out[:, cols] = (act[:, cols] - gated[:, cols] * upper).astype(out.dtype)


def ratio_end(act, gated, own):
    arrays, starts = own
    return pl.pallas_call(
        functools.partial(ratio_kernel, starts),
        out_shape=jax.ShapeDtypeStruct(act.shape, jnp.bfloat16),
        in_specs=[IN_VMEM] * (2 + len(arrays)),
        out_specs=IN_VMEM,
        compiler_params=pltpu.CompilerParams(vmem_limit_bytes=6 << 20),
    )(act, gated, *arrays)


def column_chunks(width):
    tile = tile_of(width)
    first = width // tile // 2 * tile
    return [(0, first), (first, width - first)] if first else [(0, width)]


def local(mesh_shape, target_states, source_states, target_gate, target_up, source_gate, source_up, token_ids, lengths, ratio_weight):
    wide, narrow = mesh_shape["wide"], mesh_shape["narrow"]
    width = target_gate.shape[1]
    gate_top, gate_bottom = halves(source_gate)
    up_top, up_bottom = halves(source_up)
    target_gate = load(halves(target_gate), ())
    live, weight = look_up(token_ids, lengths, ratio_weight, (target_gate[0],))
    first = (live,)
    target_pieces = gather_pieces(target_states, "wide", wide, first)
    source_pieces = gather_pieces(source_states, "wide", wide, first)
    after = (*first, target_pieces[wide // 2], source_pieces[wide // 2])
    target_up = load(halves(target_up), after)

    groups = (target_gate, target_up)
    tokens, after = target_pieces, (target_up[0], *source_pieces[1:])
    chunks, made = column_chunks(width), []
    for chunk in chunks:
        loads = [gate_top] if chunk is chunks[-1] else []
        loaded, tokens, sends, keeps = product(tokens, groups, chunk, narrow, after, loads)
        made.append((sends, keeps))
        after = (sends[0],)
    (gate_top,) = loaded
    owns = []
    for sends, keeps in made:
        sent, own = finish(sends, keeps, narrow, after)
        if not owns:
            gate_bottom, up_top = load([gate_bottom, up_top], (sent,))
        owns.append(own)
        after = (up_top, own[0][-1])

    groups, after = ((gate_top, gate_bottom),), (sent, gate_bottom)
    (up_bottom,), rows, gate_sends, gate_keeps = product(
        source_pieces, groups, (0, width), narrow, after, [up_bottom]
    )
    groups, after = ((up_top, up_bottom),), (gate_sends[0],)
    _, _, sends, keeps = product(rows, groups, (0, width), narrow, after)
    sent, source_g = finish(gate_sends, gate_keeps, narrow, (sends[0], owns[-1][0][-1]))
    act, target_out = target_end(live, chunks, owns)
    _, source_u = finish(sends, keeps, narrow, (act,))
    gated = source_middle(live, weight, source_g)
    ratio_out = ratio_end(act, gated, source_u)
    return (target_out, ratio_out)


def solution(mesh):
    placed = (
        P(("groups", "wide"), "narrow"),
        P(("groups", "wide"), "narrow"),
        P("narrow", "wide"),
        P("narrow", "wide"),
        P("narrow", "wide"),
        P("narrow", "wide"),
        P(("groups", "narrow")),
        P(("groups", "narrow")),
        P(),
    )
    mesh_shape = dict(mesh.shape)

    def body(*args):
        return local(mesh_shape, *args)

    return jax.shard_map(
        body,
        mesh=mesh,
        in_specs=placed,
        out_specs=(P(("groups", "narrow"), "wide"), P(("groups", "narrow"), "wide")),
        check_vma=False,
    )
```

```python
import functools
import math

import jax
import jax.numpy as jnp
from jax import lax
from jax.experimental import pallas as pl
from jax.experimental.pallas import tpu as pltpu
from jax.sharding import PartitionSpec as P

IN_VMEM = pl.BlockSpec(memory_space=pltpu.VMEM)
IN_SMEM = pl.BlockSpec(memory_space=pltpu.SMEM)
ANYWHERE = pl.BlockSpec(memory_space=pl.ANY)
LANES = 128


def in_hbm(array):
    return pltpu.with_memory_space_constraint(array, pltpu.HBM)


def in_vmem(array):
    return pltpu.with_memory_space_constraint(array, pltpu.VMEM)


def gather_pieces(piece, axis, size, relayed):
    pieces = [piece]
    for offset in range(1, size):
        low = offset & -offset if relayed else offset
        pairs = [(i, i ^ low) for i in range(size)]
        pieces.append(lax.ppermute(pieces[offset ^ low], axis, pairs))
    return pieces


def halving_order(size):
    bits = size.bit_length() - 1
    reverse = [sum(((p >> b) & 1) << (bits - 1 - b) for b in range(bits)) for p in range(size)]
    return reverse[::-1]


def place_rows(pieces, rows, narrow):
    me_wide, me_narrow = lax.axis_index("wide"), lax.axis_index("narrow")
    piece_rows = pieces[0].shape[0]
    block_rows = piece_rows * len(pieces) // narrow
    size = math.gcd(piece_rows, block_rows)
    for offset, piece in enumerate(pieces):
        for start in range(0, piece_rows, size):
            row = (me_wide ^ offset) * piece_rows + start
            block = (row // block_rows) ^ me_narrow
            place = sum(
                jnp.where(block == known, position, 0)
                for position, known in enumerate(halving_order(narrow))
            )
            spot = pl.multiple_of(place * block_rows + row % block_rows, size)
            rows[pl.ds(spot, size), :] = piece[start : start + size, :]


def start_loads(sources, spans, dests, sems):
    copies = []
    for i, (source, (start, size)) in enumerate(zip(sources, spans)):
        copies.append(pltpu.make_async_copy(source.at[pl.ds(start, size), :], dests[i], sems.at[i]))
        copies[-1].start()
    return copies


def look_up_kernel(slots, ids, lengths, table, *refs):
    live, weight, entries, picked, sem = refs[-5:]
    lookup = pltpu.make_async_copy(table, entries, sem)
    lookup.start()
    for i in range(lengths.shape[0]):
        slot = lax.broadcasted_iota(jnp.int32, (slots, LANES), 0)
        live[i * slots : (i + 1) * slots, :] = (slot < lengths[i]).astype(jnp.float32)
    lookup.wait()

    def pick(i, carry):
        entry = ids[i]
        lane = lax.broadcasted_iota(jnp.int32, (1, LANES), 1)
        row = entries[pl.ds(entry // LANES, 1), :]
        picked[pl.ds(i, 1), :] = jnp.where(lane == entry % LANES, row, 0.0)
        return carry

    lax.fori_loop(0, ids.shape[0], pick, 0)
    weight[...] = jnp.broadcast_to(jnp.sum(picked[...], axis=1, keepdims=True), weight.shape)


def look_up(ids, lengths, table, after):
    table = table.reshape(-1, LANES)
    flag = jax.ShapeDtypeStruct((ids.shape[0], LANES), jnp.float32)
    return pl.pallas_call(
        functools.partial(look_up_kernel, ids.shape[0] // lengths.shape[0]),
        out_shape=[flag, flag],
        in_specs=[IN_SMEM, IN_SMEM] + [ANYWHERE] * (1 + len(after)),
        out_specs=[IN_VMEM, IN_VMEM],
        scratch_shapes=[
            pltpu.VMEM(table.shape, table.dtype),
            pltpu.VMEM(flag.shape, flag.dtype),
            pltpu.SemaphoreType.DMA,
        ],
        compiler_params=pltpu.CompilerParams(vmem_limit_bytes=3 << 20),
    )(*map(in_hbm, (ids, lengths, table)), *after)


def load_kernel(spans, after, *refs):
    dests = refs[len(spans) + after : -1]
    for copy in start_loads(refs[: len(spans)], spans, dests, refs[-1]):
        copy.wait()


def halves(matrix):
    half = matrix.shape[0] // 2
    return [(matrix, (0, half)), (matrix, (half, half))]


def load(loads, after):
    return pl.pallas_call(
        functools.partial(load_kernel, [span for _, span in loads], len(after)),
        out_shape=[pltpu.VMEM((size, m.shape[1]), m.dtype) for m, (_, size) in loads],
        in_specs=[ANYWHERE] * (len(loads) + len(after)),
        out_specs=[IN_VMEM] * len(loads),
        scratch_shapes=[pltpu.SemaphoreType.DMA((len(loads),))],
        compiler_params=pltpu.CompilerParams(vmem_limit_bytes=1 << 20),
    )(*(in_hbm(m) for m, _ in loads), *after)


def tile_of(cols):
    for tile in (512, 256, 128):
        if cols % tile == 0:
            return tile
    return cols


def column_tiles(width):
    tile = tile_of(width)
    return [slice(start, start + tile) for start in range(0, width, tile)]


def column_chunks(width):
    tile = tile_of(width)
    first = width // tile // 2 * tile
    return [(0, first), (first, width - first)] if first else [(0, width)]


def product_kernel(pieces, parts, spans, after, narrow, blocks, *refs):
    tokens, matrices = refs[:pieces], refs[pieces : pieces + parts]
    refs = refs[pieces + parts :]
    sources, refs = refs[: len(spans)], refs[len(spans) + after :]
    dests, outs, sems = refs[: len(spans)], refs[len(spans) : -1], refs[-1]
    copies = start_loads(sources, spans, dests, sems)
    if pieces > 1:
        place_rows(tokens, outs[0], narrow)
        tokens, outs = outs[:1], outs[1:]
    for cols in column_tiles(matrices[0].shape[1]):
        total, depth = None, 0
        for matrix in matrices:
            rows = tokens[0][:, depth : depth + matrix.shape[0]]
            term = jnp.dot(rows, matrix[:, cols], preferred_element_type=jnp.float32)
            total = term if total is None else total + term
            depth += matrix.shape[0]
        for out, (row, col) in zip(outs, blocks):
            if col <= cols.start and cols.stop <= col + out.shape[1]:
                value = total[row : row + out.shape[0]].astype(out.dtype)
                out[:, cols.start - col : cols.stop - col] = value
    for copy in copies:
        copy.wait()


def part_sizes(total, narrow):
    sizes, left = [], total // 2
    while left > total // narrow:
        left //= 2
        sizes.append(left)
    return sizes + [left]


def product(tokens, matrices, narrow, after=(), loads=()):
    placing = len(tokens) > 1
    total = sum(t.shape[0] for t in tokens)
    depth, width = tokens[0].shape[1], matrices[0].shape[1]
    sizes = part_sizes(total, narrow)
    sent = []
    for k in range(len(sizes)):
        sent += [(k, *chunk) for chunk in (column_chunks(width) if k + 1 < len(sizes) else [(0, width)])]
    blocks = [(sum(sizes[:k]), first) for k, first, _ in sent]
    blocks += [(total // 2 + sum(sizes[:k]), 0) for k in range(len(sizes))]
    shapes = [(sizes[k], count) for k, _, count in sent] + [(size, width) for size in sizes]
    found = pl.pallas_call(
        functools.partial(
            product_kernel, len(tokens), len(matrices), [span for _, span in loads], len(after), narrow, blocks
        ),
        out_shape=[pltpu.VMEM((size, m.shape[1]), m.dtype) for m, (_, size) in loads]
        + [jax.ShapeDtypeStruct((total, depth), tokens[0].dtype)] * placing
        + [jax.ShapeDtypeStruct(shape, jnp.bfloat16) for shape in shapes],
        in_specs=[IN_VMEM] * (len(tokens) + len(matrices)) + [ANYWHERE] * (len(loads) + len(after)),
        out_specs=[IN_VMEM] * (len(loads) + placing + len(shapes)),
        scratch_shapes=[pltpu.SemaphoreType.DMA((max(1, len(loads)),))],
        compiler_params=pltpu.CompilerParams(vmem_limit_bytes=4 << 20),
    )(*tokens, *map(in_vmem, matrices), *(in_hbm(m) for m, _ in loads), *after)
    loaded, found = found[: len(loads)], found[len(loads) :]
    rows, found = (found[:1], found[1:]) if placing else (tokens, found)
    sends = [(array, k, first) for array, (k, first, _) in zip(found, sent)]
    return loaded, rows, sends, found[len(sent) :]


def exchange(array, step, size):
    return lax.ppermute(array, "narrow", [(i, i ^ (1 << step)) for i in range(size)])


def addends(parts, came, k):
    found = [(parts[k], (0, 0))]
    for array, first, behind, col in came:
        if first <= k < behind:
            found.append((array, (sum(part.shape[0] for part in parts[first:k]), col)))
    return [array for array, _ in found], tuple(place for _, place in found)


def added(refs, places, count, cols):
    total = None
    for ref, (row, col) in zip(refs, places):
        if col <= cols.start and cols.stop <= col + ref.shape[1]:
            term = ref[row : row + count, cols.start - col : cols.stop - col].astype(jnp.float32)
            total = term if total is None else total + term
    return total


def next_kernel(places, *refs):
    out = refs[-1]
    for cols in column_tiles(out.shape[1]):
        out[:, cols] = added(refs, places, out.shape[0], cols).astype(out.dtype)


def finish(sends, keeps, narrow, after):
    came = [(exchange(array, 0, narrow), k, k + 1, col) for array, k, col in sends]
    sent = sends[0][0]
    for k in range(len(keeps) - 1):
        arrays, places = addends(keeps, came, k)
        sent = pl.pallas_call(
            functools.partial(next_kernel, places),
            out_shape=jax.ShapeDtypeStruct(keeps[k].shape, jnp.bfloat16),
            in_specs=[IN_VMEM] * len(arrays) + [ANYWHERE] * len(after),
            out_specs=IN_VMEM,
            compiler_params=pltpu.CompilerParams(vmem_limit_bytes=2 << 20),
        )(*arrays, *after)
        came.append((exchange(sent, k + 1, narrow), k + 1, len(keeps), 0))
    return sent, addends(keeps, came, len(keeps) - 1)


def target_kernel(starts, live, *refs):
    act, out = refs[-2:]
    count = len(starts[0])
    for cols in column_tiles(out.shape[1]):
        gate = added(refs[:count], starts[0], out.shape[0], cols)
        upper = added(refs[count:], starts[1], out.shape[0], cols)
        value = live[:, :1] * (jax.nn.silu(gate) * upper)
        act[:, cols] = value
        out[:, cols] = value.astype(out.dtype)


def target_end(live, gate, upper):
    arrays = gate[0] + upper[0]
    shape = gate[0][0].shape
    return pl.pallas_call(
        functools.partial(target_kernel, (gate[1], upper[1])),
        out_shape=[jax.ShapeDtypeStruct(shape, jnp.float32), jax.ShapeDtypeStruct(shape, jnp.bfloat16)],
        in_specs=[IN_VMEM] * (1 + len(arrays)),
        out_specs=[IN_VMEM] * 2,
        compiler_params=pltpu.CompilerParams(vmem_limit_bytes=4 << 20),
    )(live, *arrays)


def source_kernel(starts, live, weight, *refs):
    terms, out = refs[:-1], refs[-1]
    for cols in column_tiles(out.shape[1]):
        gate = added(terms, starts, out.shape[0], cols)
        out[:, cols] = (live[:, :1] * weight[:, :1]) * jax.nn.silu(gate)


def source_middle(live, weight, own):
    arrays, starts = own
    return pl.pallas_call(
        functools.partial(source_kernel, starts),
        out_shape=jax.ShapeDtypeStruct((live.shape[0], arrays[0].shape[1]), jnp.float32),
        in_specs=[IN_VMEM] * (2 + len(arrays)),
        out_specs=IN_VMEM,
        compiler_params=pltpu.CompilerParams(vmem_limit_bytes=4 << 20),
    )(live, weight, *arrays)


def ratio_kernel(starts, act, gated, *refs):
    terms, out = refs[:-1], refs[-1]
    for cols in column_tiles(out.shape[1]):
        upper = added(terms, starts, out.shape[0], cols)
        out[:, cols] = (act[:, cols] - gated[:, cols] * upper).astype(out.dtype)


def ratio_end(act, gated, own):
    arrays, starts = own
    return pl.pallas_call(
        functools.partial(ratio_kernel, starts),
        out_shape=jax.ShapeDtypeStruct(act.shape, jnp.bfloat16),
        in_specs=[IN_VMEM] * (2 + len(arrays)),
        out_specs=IN_VMEM,
        compiler_params=pltpu.CompilerParams(vmem_limit_bytes=4 << 20),
    )(act, gated, *arrays)


def local(mesh_shape, target_states, source_states, target_gate, target_up, source_gate, source_up, token_ids, lengths, ratio_weight):
    wide, narrow = mesh_shape["wide"], mesh_shape["narrow"]
    gate_top, gate_bottom = halves(source_gate)
    up_top, up_bottom = halves(source_up)

    target_pieces = gather_pieces(target_states, "wide", wide, False)
    source_pieces = gather_pieces(source_states, "wide", wide, True)
    target_gate = load(halves(target_gate), ())
    target_up = load(halves(target_up), (target_gate[0],))

    after = (target_up[0], source_pieces[1])
    _, rows, sends, keeps = product(target_pieces, target_gate, narrow, after)
    after = (sends[0][0],)
    (gate_top,), _, up_sends, up_keeps = product(rows, target_up, narrow, after, [gate_top])
    sent, target_g = finish(sends, keeps, narrow, (up_sends[0][0],))
    gate_bottom, up_top = load([gate_bottom, up_top], (sent,))
    sent, target_u = finish(up_sends, up_keeps, narrow, (up_top,))

    (up_bottom,), rows, sends, keeps = product(
        source_pieces, (gate_top, gate_bottom), narrow, (sent,), [up_bottom]
    )
    after = (sends[0][0], target_g[0][-1])
    _, _, up_sends, up_keeps = product(rows, (up_top, up_bottom), narrow, after)
    after = (up_sends[0][0], target_u[0][-1])
    sent, source_g = finish(sends, keeps, narrow, after)
    sent, source_u = finish(up_sends, up_keeps, narrow, (sent,))
    live, weight = look_up(token_ids, lengths, ratio_weight, (sent,))
    act, target_out = target_end(live, target_g, target_u)
    gated = source_middle(live, weight, source_g)
    ratio_out = ratio_end(act, gated, source_u)
    return (target_out, ratio_out)


def solution(mesh):
    placed = (
        P(("groups", "wide"), "narrow"),
        P(("groups", "wide"), "narrow"),
        P("narrow", "wide"),
        P("narrow", "wide"),
        P("narrow", "wide"),
        P("narrow", "wide"),
        P(("groups", "narrow")),
        P(("groups", "narrow")),
        P(),
    )
    mesh_shape = dict(mesh.shape)

    def body(*args):
        return local(mesh_shape, *args)

    return jax.shard_map(
        body,
        mesh=mesh,
        in_specs=placed,
        out_specs=(P(("groups", "narrow"), "wide"), P(("groups", "narrow"), "wide")),
        check_vma=False,
    )
```

```python
import functools
import math

import jax
import jax.numpy as jnp
from jax import lax
from jax.experimental import pallas as pl
from jax.experimental.pallas import tpu as pltpu
from jax.sharding import PartitionSpec as P

IN_VMEM = pl.BlockSpec(memory_space=pltpu.VMEM)
IN_SMEM = pl.BlockSpec(memory_space=pltpu.SMEM)
ANYWHERE = pl.BlockSpec(memory_space=pl.ANY)
LANES = 128
IN_FLIGHT = 4


def in_hbm(array):
    return pltpu.with_memory_space_constraint(array, pltpu.HBM)


def in_vmem(array):
    return pltpu.with_memory_space_constraint(array, pltpu.VMEM)


def pass_kernel(piece, *refs):
    refs[-1][...] = piece[...]


def passed(piece, after):
    return pl.pallas_call(
        pass_kernel,
        out_shape=jax.ShapeDtypeStruct(piece.shape, piece.dtype),
        in_specs=[IN_VMEM] + [ANYWHERE] * len(after),
        out_specs=IN_VMEM,
        compiler_params=pltpu.CompilerParams(vmem_limit_bytes=1 << 20),
    )(piece, *after)


def gather_pieces(piece, axis, size, after=()):
    pieces = [piece]
    for offset in range(1, size):
        low = offset & -offset
        pairs = [(i, i ^ low) for i in range(size)]
        piece = pieces[offset ^ low]
        if after and offset != low:
            piece = passed(piece, after)
        pieces.append(lax.ppermute(piece, axis, pairs))
    return pieces


def halving_order(size):
    bits = size.bit_length() - 1
    reverse = [sum(((p >> b) & 1) << (bits - 1 - b) for b in range(bits)) for p in range(size)]
    return reverse[::-1]


def place_rows(pieces, rows, narrow):
    me_wide, me_narrow = lax.axis_index("wide"), lax.axis_index("narrow")
    piece_rows = pieces[0].shape[0]
    block_rows = piece_rows * len(pieces) // narrow
    size = math.gcd(piece_rows, block_rows)
    for offset, piece in enumerate(pieces):
        for start in range(0, piece_rows, size):
            row = (me_wide ^ offset) * piece_rows + start
            block = (row // block_rows) ^ me_narrow
            place = sum(
                jnp.where(block == known, position, 0)
                for position, known in enumerate(halving_order(narrow))
            )
            spot = pl.multiple_of(place * block_rows + row % block_rows, size)
            rows[pl.ds(spot, size), :] = piece[start : start + size, :]


def look_up_kernel(slots, ids, lengths, table, *refs):
    live, weight, entries, picked, sem = refs[-5:]
    lookup = pltpu.make_async_copy(table, entries, sem)
    lookup.start()
    for i in range(lengths.shape[0]):
        slot = lax.broadcasted_iota(jnp.int32, (slots, LANES), 0)
        live[i * slots : (i + 1) * slots, :] = (slot < lengths[i]).astype(jnp.float32)
    lookup.wait()

    def pick(i, carry):
        entry = ids[i]
        lane = lax.broadcasted_iota(jnp.int32, (1, LANES), 1)
        row = entries[pl.ds(entry // LANES, 1), :]
        picked[pl.ds(i, 1), :] = jnp.where(lane == entry % LANES, row, 0.0)
        return carry

    lax.fori_loop(0, ids.shape[0], pick, 0)
    weight[...] = jnp.broadcast_to(jnp.sum(picked[...], axis=1, keepdims=True), weight.shape)


def look_up(ids, lengths, table, after):
    table = table.reshape(-1, LANES)
    flag = jax.ShapeDtypeStruct((ids.shape[0], LANES), jnp.float32)
    return pl.pallas_call(
        functools.partial(look_up_kernel, ids.shape[0] // lengths.shape[0]),
        out_shape=[flag, flag],
        in_specs=[IN_SMEM, IN_SMEM] + [ANYWHERE] * (1 + len(after)),
        out_specs=[IN_VMEM, IN_VMEM],
        scratch_shapes=[
            pltpu.VMEM(table.shape, table.dtype),
            pltpu.VMEM(flag.shape, flag.dtype),
            pltpu.SemaphoreType.DMA,
        ],
        compiler_params=pltpu.CompilerParams(vmem_limit_bytes=3 << 20),
    )(*map(in_hbm, (ids, lengths, table)), *after)


def load_kernel(matrix, *refs):
    dest, sem = refs[-2:]
    copy = pltpu.make_async_copy(matrix, dest, sem)
    copy.start()
    copy.wait()


def load(matrix, after=()):
    return pl.pallas_call(
        load_kernel,
        out_shape=pltpu.VMEM(matrix.shape, matrix.dtype),
        in_specs=[ANYWHERE] * (1 + len(after)),
        out_specs=IN_VMEM,
        scratch_shapes=[pltpu.SemaphoreType.DMA],
        compiler_params=pltpu.CompilerParams(vmem_limit_bytes=1 << 20),
    )(in_hbm(matrix), *after)


def tile_of(cols):
    for tile in (512, 256, 128):
        if cols % tile == 0:
            return tile
    return cols


def column_tiles(width):
    tile = tile_of(width)
    return [slice(start, start + tile) for start in range(0, width, tile)]


def column_chunks(width):
    tile = tile_of(width)
    first = width // tile // 2 * tile
    return [(0, first), (first, width - first)] if first else [(0, width)]


def product_kernel(pieces, after, narrow, blocks, *refs):
    tokens, matrix, refs = refs[:pieces], refs[pieces], refs[pieces + 1 + after :]
    tiles, copies = column_tiles(matrix.shape[1]), []
    if len(blocks) < len(refs) - (pieces > 1):
        here, sems = refs[-2:]
        refs = refs[:-2]
        for i, cols in enumerate(tiles):
            copies.append(pltpu.make_async_copy(matrix.at[:, cols], here.at[:, cols], sems.at[i]))
        matrix = here
    for copy in copies[:IN_FLIGHT]:
        copy.start()
    if pieces > 1:
        place_rows(tokens, refs[0], narrow)
        tokens, refs = refs[:1], refs[1:]
    for i, cols in enumerate(tiles):
        if copies:
            copies[i].wait()
        if i + IN_FLIGHT < len(copies):
            copies[i + IN_FLIGHT].start()
        total = jnp.dot(tokens[0][...], matrix[:, cols], preferred_element_type=jnp.float32)
        for out, (row, col) in zip(refs, blocks):
            if col <= cols.start and cols.stop <= col + out.shape[1]:
                value = total[row : row + out.shape[0]].astype(out.dtype)
                out[:, cols.start - col : cols.stop - col] = value


def part_sizes(total, narrow):
    sizes, left = [], total // 2
    while left > total // narrow:
        left //= 2
        sizes.append(left)
    return sizes + [left]


def product(tokens, matrix, held, narrow, after):
    placing = len(tokens) > 1
    total = sum(t.shape[0] for t in tokens)
    depth, width = matrix.shape
    sizes = part_sizes(total, narrow)
    sent = []
    for k in range(len(sizes)):
        sent += [(k, *chunk) for chunk in (column_chunks(width) if k + 1 < len(sizes) else [(0, width)])]
    blocks = [(sum(sizes[:k]), first) for k, first, _ in sent]
    blocks += [(total // 2 + sum(sizes[:k]), 0) for k in range(len(sizes))]
    shapes = [(sizes[k], count) for k, _, count in sent] + [(size, width) for size in sizes]
    stream = [
        pltpu.VMEM(matrix.shape, matrix.dtype),
        pltpu.SemaphoreType.DMA((len(column_tiles(width)),)),
    ]
    room = 4 + (0 if held else 1 + matrix.size * matrix.dtype.itemsize >> 20)
    found = pl.pallas_call(
        functools.partial(product_kernel, len(tokens), len(after), narrow, blocks),
        out_shape=[jax.ShapeDtypeStruct((total, depth), tokens[0].dtype)] * placing
        + [jax.ShapeDtypeStruct(shape, jnp.bfloat16) for shape in shapes],
        in_specs=[IN_VMEM] * len(tokens) + [IN_VMEM if held else ANYWHERE] + [ANYWHERE] * len(after),
        out_specs=[IN_VMEM] * (placing + len(shapes)),
        scratch_shapes=[] if held else stream,
        compiler_params=pltpu.CompilerParams(vmem_limit_bytes=room << 20),
    )(*tokens, (in_vmem if held else in_hbm)(matrix), *after)
    rows, found = (found[:1], found[1:]) if placing else (tokens, found)
    sends = [(array, k, first) for array, (k, first, _) in zip(found, sent)]
    return rows, sends, found[len(sent) :]


def exchange(array, step, size):
    return lax.ppermute(array, "narrow", [(i, i ^ (1 << step)) for i in range(size)])


def addends(parts, came, k):
    found = [(parts[k], (0, 0))]
    for array, first, behind, col in came:
        if first <= k < behind:
            found.append((array, (sum(part.shape[0] for part in parts[first:k]), col)))
    return [array for array, _ in found], tuple(place for _, place in found)


def added(refs, places, count, cols):
    total = None
    for ref, (row, col) in zip(refs, places):
        if col <= cols.start and cols.stop <= col + ref.shape[1]:
            term = ref[row : row + count, cols.start - col : cols.stop - col].astype(jnp.float32)
            total = term if total is None else total + term
    return total


def next_kernel(places, *refs):
    out = refs[-1]
    for cols in column_tiles(out.shape[1]):
        out[:, cols] = added(refs, places, out.shape[0], cols).astype(out.dtype)


def finish(sends, keeps, narrow, after):
    came = [(exchange(array, 0, narrow), k, k + 1, col) for array, k, col in sends]
    sent = sends[0][0]
    for k in range(len(keeps) - 1):
        arrays, places = addends(keeps, came, k)
        sent = pl.pallas_call(
            functools.partial(next_kernel, places),
            out_shape=jax.ShapeDtypeStruct(keeps[k].shape, jnp.bfloat16),
            in_specs=[IN_VMEM] * len(arrays) + [ANYWHERE] * len(after),
            out_specs=IN_VMEM,
            compiler_params=pltpu.CompilerParams(vmem_limit_bytes=2 << 20),
        )(*arrays, *after)
        came.append((exchange(sent, k + 1, narrow), k + 1, len(keeps), 0))
    return sent, addends(keeps, came, len(keeps) - 1)


def target_kernel(starts, live, *refs):
    act, out = refs[-2:]
    count = len(starts[0])
    for cols in column_tiles(out.shape[1]):
        gate = added(refs[:count], starts[0], out.shape[0], cols)
        upper = added(refs[count:], starts[1], out.shape[0], cols)
        value = live[:, :1] * (jax.nn.silu(gate) * upper)
        act[:, cols] = value
        out[:, cols] = value.astype(out.dtype)


def target_end(live, gate, upper):
    arrays = gate[0] + upper[0]
    shape = gate[0][0].shape
    return pl.pallas_call(
        functools.partial(target_kernel, (gate[1], upper[1])),
        out_shape=[jax.ShapeDtypeStruct(shape, jnp.float32), jax.ShapeDtypeStruct(shape, jnp.bfloat16)],
        in_specs=[IN_VMEM] * (1 + len(arrays)),
        out_specs=[IN_VMEM] * 2,
        compiler_params=pltpu.CompilerParams(vmem_limit_bytes=4 << 20),
    )(live, *arrays)


def source_kernel(starts, live, weight, *refs):
    terms, out = refs[:-1], refs[-1]
    for cols in column_tiles(out.shape[1]):
        gate = added(terms, starts, out.shape[0], cols)
        out[:, cols] = (live[:, :1] * weight[:, :1]) * jax.nn.silu(gate)


def source_middle(live, weight, own):
    arrays, starts = own
    return pl.pallas_call(
        functools.partial(source_kernel, starts),
        out_shape=jax.ShapeDtypeStruct((live.shape[0], arrays[0].shape[1]), jnp.float32),
        in_specs=[IN_VMEM] * (2 + len(arrays)),
        out_specs=IN_VMEM,
        compiler_params=pltpu.CompilerParams(vmem_limit_bytes=4 << 20),
    )(live, weight, *arrays)


def ratio_kernel(starts, act, gated, *refs):
    terms, out = refs[:-1], refs[-1]
    for cols in column_tiles(out.shape[1]):
        upper = added(terms, starts, out.shape[0], cols)
        out[:, cols] = (act[:, cols] - gated[:, cols] * upper).astype(out.dtype)


def ratio_end(act, gated, own):
    arrays, starts = own
    return pl.pallas_call(
        functools.partial(ratio_kernel, starts),
        out_shape=jax.ShapeDtypeStruct(act.shape, jnp.bfloat16),
        in_specs=[IN_VMEM] * (2 + len(arrays)),
        out_specs=IN_VMEM,
        compiler_params=pltpu.CompilerParams(vmem_limit_bytes=4 << 20),
    )(act, gated, *arrays)


def local(mesh_shape, target_states, source_states, target_gate, target_up, source_gate, source_up, token_ids, lengths, ratio_weight):
    wide, narrow = mesh_shape["wide"], mesh_shape["narrow"]
    target_gate = load(target_gate)
    target_pieces = gather_pieces(target_states, "wide", wide, (target_gate,))
    source_pieces = gather_pieces(source_states, "wide", wide)
    target_up = load(target_up, (target_gate, target_pieces[wide // 2]))

    after = (target_up, source_pieces[1], source_pieces[wide // 2])
    rows, sends, keeps = product(target_pieces, target_gate, True, narrow, after)
    _, up_sends, up_keeps = product(rows, target_up, True, narrow, (sends[0][0],))
    sent, target_g = finish(sends, keeps, narrow, (up_sends[0][0], source_pieces[-1]))
    sent, target_u = finish(up_sends, up_keeps, narrow, (sent,))

    rows, sends, keeps = product(source_pieces, source_gate, False, narrow, (sent,))
    after = (sends[0][0], target_g[0][-1])
    _, up_sends, up_keeps = product(rows, source_up, False, narrow, after)
    after = (up_sends[0][0], target_u[0][-1])
    sent, source_g = finish(sends, keeps, narrow, after)
    sent, source_u = finish(up_sends, up_keeps, narrow, (sent,))
    live, weight = look_up(token_ids, lengths, ratio_weight, (sent,))
    act, target_out = target_end(live, target_g, target_u)
    gated = source_middle(live, weight, source_g)
    ratio_out = ratio_end(act, gated, source_u)
    return (target_out, ratio_out)


def solution(mesh):
    placed = (
        P(("groups", "wide"), "narrow"),
        P(("groups", "wide"), "narrow"),
        P("narrow", "wide"),
        P("narrow", "wide"),
        P("narrow", "wide"),
        P("narrow", "wide"),
        P(("groups", "narrow")),
        P(("groups", "narrow")),
        P(),
    )
    mesh_shape = dict(mesh.shape)

    def body(*args):
        return local(mesh_shape, *args)

    return jax.shard_map(
        body,
        mesh=mesh,
        in_specs=placed,
        out_specs=(P(("groups", "narrow"), "wide"), P(("groups", "narrow"), "wide")),
        check_vma=False,
    )
```

```python
import functools
import math

import jax
import jax.numpy as jnp
from jax import lax
from jax.experimental import pallas as pl
from jax.experimental.pallas import tpu as pltpu
from jax.sharding import PartitionSpec as P

IN_VMEM = pl.BlockSpec(memory_space=pltpu.VMEM)
IN_SMEM = pl.BlockSpec(memory_space=pltpu.SMEM)
ANYWHERE = pl.BlockSpec(memory_space=pl.ANY)
LANES = 128


def in_hbm(array):
    return pltpu.with_memory_space_constraint(array, pltpu.HBM)


def in_vmem(array):
    return pltpu.with_memory_space_constraint(array, pltpu.VMEM)


def pass_kernel(piece, *refs):
    refs[-1][...] = piece[...]


def passed(piece, after):
    return pl.pallas_call(
        pass_kernel,
        out_shape=jax.ShapeDtypeStruct(piece.shape, piece.dtype),
        in_specs=[IN_VMEM] + [ANYWHERE] * len(after),
        out_specs=IN_VMEM,
        compiler_params=pltpu.CompilerParams(vmem_limit_bytes=1 << 20),
    )(piece, *after)


def gather_pieces(piece, axis, size, after=()):
    pieces = [piece]
    for offset in range(1, size):
        low = offset & -offset
        pairs = [(i, i ^ low) for i in range(size)]
        piece = pieces[offset ^ low]
        if after and offset != low:
            piece = passed(piece, after)
        pieces.append(lax.ppermute(piece, axis, pairs))
    return pieces


def halving_order(size):
    bits = size.bit_length() - 1
    reverse = [sum(((p >> b) & 1) << (bits - 1 - b) for b in range(bits)) for p in range(size)]
    return reverse[::-1]


def place_rows(pieces, rows, narrow):
    me_wide, me_narrow = lax.axis_index("wide"), lax.axis_index("narrow")
    piece_rows = pieces[0].shape[0]
    block_rows = piece_rows * len(pieces) // narrow
    size = math.gcd(piece_rows, block_rows)
    for offset, piece in enumerate(pieces):
        for start in range(0, piece_rows, size):
            row = (me_wide ^ offset) * piece_rows + start
            block = (row // block_rows) ^ me_narrow
            place = sum(
                jnp.where(block == known, position, 0)
                for position, known in enumerate(halving_order(narrow))
            )
            spot = pl.multiple_of(place * block_rows + row % block_rows, size)
            rows[pl.ds(spot, size), :] = piece[start : start + size, :]


def look_up_kernel(slots, ids, lengths, table, *refs):
    live, weight, entries, picked, sem = refs[-5:]
    lookup = pltpu.make_async_copy(table, entries, sem)
    lookup.start()
    for i in range(lengths.shape[0]):
        slot = lax.broadcasted_iota(jnp.int32, (slots, LANES), 0)
        live[i * slots : (i + 1) * slots, :] = (slot < lengths[i]).astype(jnp.float32)
    lookup.wait()

    def pick(i, carry):
        entry = ids[i]
        lane = lax.broadcasted_iota(jnp.int32, (1, LANES), 1)
        row = entries[pl.ds(entry // LANES, 1), :]
        picked[pl.ds(i, 1), :] = jnp.where(lane == entry % LANES, row, 0.0)
        return carry

    lax.fori_loop(0, ids.shape[0], pick, 0)
    weight[...] = jnp.broadcast_to(jnp.sum(picked[...], axis=1, keepdims=True), weight.shape)


def look_up(ids, lengths, table, after):
    table = table.reshape(-1, LANES)
    flag = jax.ShapeDtypeStruct((ids.shape[0], LANES), jnp.float32)
    return pl.pallas_call(
        functools.partial(look_up_kernel, ids.shape[0] // lengths.shape[0]),
        out_shape=[flag, flag],
        in_specs=[IN_SMEM, IN_SMEM] + [ANYWHERE] * (1 + len(after)),
        out_specs=[IN_VMEM, IN_VMEM],
        scratch_shapes=[
            pltpu.VMEM(table.shape, table.dtype),
            pltpu.VMEM(flag.shape, flag.dtype),
            pltpu.SemaphoreType.DMA,
        ],
        compiler_params=pltpu.CompilerParams(vmem_limit_bytes=3 << 20),
    )(*map(in_hbm, (ids, lengths, table)), *after)


def load_kernel(matrix, *refs):
    dest, sem = refs[-2:]
    copy = pltpu.make_async_copy(matrix, dest, sem)
    copy.start()
    copy.wait()


def load(matrix, after=()):
    return pl.pallas_call(
        load_kernel,
        out_shape=pltpu.VMEM(matrix.shape, matrix.dtype),
        in_specs=[ANYWHERE] * (1 + len(after)),
        out_specs=IN_VMEM,
        scratch_shapes=[pltpu.SemaphoreType.DMA],
        compiler_params=pltpu.CompilerParams(vmem_limit_bytes=1 << 20),
    )(in_hbm(matrix), *after)


def tile_of(cols):
    for tile in (512, 256, 128):
        if cols % tile == 0:
            return tile
    return cols


def column_tiles(width):
    tile = tile_of(width)
    return [slice(start, start + tile) for start in range(0, width, tile)]


def column_chunks(width):
    tile = tile_of(width)
    first = width // tile // 2 * tile
    return [(0, first), (first, width - first)] if first else [(0, width)]


def product_kernel(pieces, after, narrow, blocks, *refs):
    tokens, matrix, outs = refs[:pieces], refs[pieces], refs[pieces + 1 + after :]
    if pieces > 1:
        place_rows(tokens, outs[0], narrow)
        tokens, outs = outs[:1], outs[1:]
    for cols in column_tiles(matrix.shape[1]):
        total = jnp.dot(tokens[0][...], matrix[:, cols], preferred_element_type=jnp.float32)
        for out, (row, col) in zip(outs, blocks):
            if col <= cols.start and cols.stop <= col + out.shape[1]:
                value = total[row : row + out.shape[0]].astype(out.dtype)
                out[:, cols.start - col : cols.stop - col] = value


def part_sizes(total, narrow):
    sizes, left = [], total // 2
    while left > total // narrow:
        left //= 2
        sizes.append(left)
    return sizes + [left]


def product(tokens, matrix, narrow, after):
    placing = len(tokens) > 1
    total = sum(t.shape[0] for t in tokens)
    depth, width = matrix.shape
    sizes = part_sizes(total, narrow)
    sent = []
    for k in range(len(sizes)):
        sent += [(k, *chunk) for chunk in (column_chunks(width) if k + 1 < len(sizes) else [(0, width)])]
    blocks = [(sum(sizes[:k]), first) for k, first, _ in sent]
    blocks += [(total // 2 + sum(sizes[:k]), 0) for k in range(len(sizes))]
    shapes = [(sizes[k], count) for k, _, count in sent] + [(size, width) for size in sizes]
    found = pl.pallas_call(
        functools.partial(product_kernel, len(tokens), len(after), narrow, blocks),
        out_shape=[jax.ShapeDtypeStruct((total, depth), tokens[0].dtype)] * placing
        + [jax.ShapeDtypeStruct(shape, jnp.bfloat16) for shape in shapes],
        in_specs=[IN_VMEM] * len(tokens) + [IN_VMEM] + [ANYWHERE] * len(after),
        out_specs=[IN_VMEM] * (placing + len(shapes)),
        compiler_params=pltpu.CompilerParams(vmem_limit_bytes=4 << 20),
    )(*tokens, in_vmem(matrix), *after)
    rows, found = (found[:1], found[1:]) if placing else (tokens, found)
    sends = [(array, k, first) for array, (k, first, _) in zip(found, sent)]
    return rows, sends, found[len(sent) :]


def exchange(array, step, size):
    return lax.ppermute(array, "narrow", [(i, i ^ (1 << step)) for i in range(size)])


def addends(parts, came, k):
    found = [(parts[k], (0, 0))]
    for array, first, behind, col in came:
        if first <= k < behind:
            found.append((array, (sum(part.shape[0] for part in parts[first:k]), col)))
    return [array for array, _ in found], tuple(place for _, place in found)


def added(refs, places, count, cols):
    total = None
    for ref, (row, col) in zip(refs, places):
        if col <= cols.start and cols.stop <= col + ref.shape[1]:
            term = ref[row : row + count, cols.start - col : cols.stop - col].astype(jnp.float32)
            total = term if total is None else total + term
    return total


def next_kernel(places, *refs):
    out = refs[-1]
    for cols in column_tiles(out.shape[1]):
        out[:, cols] = added(refs, places, out.shape[0], cols).astype(out.dtype)


def finish(sends, keeps, narrow, after):
    came = [(exchange(array, 0, narrow), k, k + 1, col) for array, k, col in sends]
    sent = sends[0][0]
    for k in range(len(keeps) - 1):
        arrays, places = addends(keeps, came, k)
        sent = pl.pallas_call(
            functools.partial(next_kernel, places),
            out_shape=jax.ShapeDtypeStruct(keeps[k].shape, jnp.bfloat16),
            in_specs=[IN_VMEM] * len(arrays) + [ANYWHERE] * len(after),
            out_specs=IN_VMEM,
            compiler_params=pltpu.CompilerParams(vmem_limit_bytes=2 << 20),
        )(*arrays, *after)
        came.append((exchange(sent, k + 1, narrow), k + 1, len(keeps), 0))
    return sent, addends(keeps, came, len(keeps) - 1)


def target_kernel(places, live, *refs):
    act, out = refs[-2:]
    count = len(places[0])
    for cols in column_tiles(out.shape[1]):
        gate = added(refs[:count], places[0], out.shape[0], cols)
        upper = added(refs[count:], places[1], out.shape[0], cols)
        value = live[:, :1] * (jax.nn.silu(gate) * upper)
        act[:, cols] = value
        out[:, cols] = value.astype(out.dtype)


def target_end(live, gate, upper):
    arrays = gate[0] + upper[0]
    shape = gate[0][0].shape
    return pl.pallas_call(
        functools.partial(target_kernel, (gate[1], upper[1])),
        out_shape=[jax.ShapeDtypeStruct(shape, jnp.float32), jax.ShapeDtypeStruct(shape, jnp.bfloat16)],
        in_specs=[IN_VMEM] * (1 + len(arrays)),
        out_specs=[IN_VMEM] * 2,
        compiler_params=pltpu.CompilerParams(vmem_limit_bytes=4 << 20),
    )(live, *arrays)


def source_kernel(starts, live, weight, *refs):
    terms, out = refs[:-1], refs[-1]
    for cols in column_tiles(out.shape[1]):
        gate = added(terms, starts, out.shape[0], cols)
        out[:, cols] = (live[:, :1] * weight[:, :1]) * jax.nn.silu(gate)


def source_middle(live, weight, own):
    arrays, starts = own
    return pl.pallas_call(
        functools.partial(source_kernel, starts),
        out_shape=jax.ShapeDtypeStruct((live.shape[0], arrays[0].shape[1]), jnp.float32),
        in_specs=[IN_VMEM] * (2 + len(arrays)),
        out_specs=IN_VMEM,
        compiler_params=pltpu.CompilerParams(vmem_limit_bytes=4 << 20),
    )(live, weight, *arrays)


def ratio_kernel(starts, act, gated, *refs):
    terms, out = refs[:-1], refs[-1]
    for cols in column_tiles(out.shape[1]):
        upper = added(terms, starts, out.shape[0], cols)
        out[:, cols] = (act[:, cols] - gated[:, cols] * upper).astype(out.dtype)


def ratio_end(act, gated, own):
    arrays, starts = own
    return pl.pallas_call(
        functools.partial(ratio_kernel, starts),
        out_shape=jax.ShapeDtypeStruct(act.shape, jnp.bfloat16),
        in_specs=[IN_VMEM] * (2 + len(arrays)),
        out_specs=IN_VMEM,
        compiler_params=pltpu.CompilerParams(vmem_limit_bytes=4 << 20),
    )(act, gated, *arrays)


def local(mesh_shape, target_states, source_states, target_gate, target_up, source_gate, source_up, token_ids, lengths, ratio_weight):
    wide, narrow = mesh_shape["wide"], mesh_shape["narrow"]
    target_gate = load(target_gate)
    target_pieces = gather_pieces(target_states, "wide", wide, (target_gate,))
    source_pieces = gather_pieces(source_states, "wide", wide)
    target_up = load(target_up, (target_gate, target_pieces[wide // 2]))

    after = (target_up,)
    rows, sends, keeps = product(target_pieces, target_gate, narrow, after)
    _, up_sends, up_keeps = product(rows, target_up, narrow, (sends[0][0],))
    sent, target_g = finish(sends, keeps, narrow, (up_sends[0][0], *source_pieces[1:]))
    sent, target_u = finish(up_sends, up_keeps, narrow, (sent,))

    rows, sends, keeps = product(source_pieces, source_gate, narrow, (sent,))
    after = (sends[0][0], target_g[0][-1])
    _, up_sends, up_keeps = product(rows, source_up, narrow, after)
    sent, source_g = finish(sends, keeps, narrow, (up_sends[0][0],))
    sent, source_u = finish(up_sends, up_keeps, narrow, (sent, target_u[0][-1]))
    live, weight = look_up(token_ids, lengths, ratio_weight, (sent,))
    act, target_out = target_end(live, target_g, target_u)
    gated = source_middle(live, weight, source_g)
    ratio_out = ratio_end(act, gated, source_u)
    return (target_out, ratio_out)


def solution(mesh):
    placed = (
        P(("groups", "wide"), "narrow"),
        P(("groups", "wide"), "narrow"),
        P("narrow", "wide"),
        P("narrow", "wide"),
        P("narrow", "wide"),
        P("narrow", "wide"),
        P(("groups", "narrow")),
        P(("groups", "narrow")),
        P(),
    )
    mesh_shape = dict(mesh.shape)

    def body(*args):
        return local(mesh_shape, *args)

    return jax.shard_map(
        body,
        mesh=mesh,
        in_specs=placed,
        out_specs=(P(("groups", "narrow"), "wide"), P(("groups", "narrow"), "wide")),
        check_vma=False,
    )
```

```python
import functools
import math

import jax
import jax.numpy as jnp
from jax import lax
from jax.experimental import pallas as pl
from jax.experimental.pallas import tpu as pltpu
from jax.sharding import PartitionSpec as P

IN_VMEM = pl.BlockSpec(memory_space=pltpu.VMEM)
IN_SMEM = pl.BlockSpec(memory_space=pltpu.SMEM)
ANYWHERE = pl.BlockSpec(memory_space=pl.ANY)
LANES = 128


def in_hbm(array):
    return pltpu.with_memory_space_constraint(array, pltpu.HBM)


def in_vmem(array):
    return pltpu.with_memory_space_constraint(array, pltpu.VMEM)


def pass_kernel(piece, *refs):
    refs[-1][...] = piece[...]


def passed(piece, after):
    return pl.pallas_call(
        pass_kernel,
        out_shape=jax.ShapeDtypeStruct(piece.shape, piece.dtype),
        in_specs=[IN_VMEM] + [ANYWHERE] * len(after),
        out_specs=IN_VMEM,
        compiler_params=pltpu.CompilerParams(vmem_limit_bytes=1 << 20),
    )(piece, *after)


def gather_pieces(piece, axis, size, after=()):
    pieces = [piece]
    for offset in range(1, size):
        low = offset & -offset
        pairs = [(i, i ^ low) for i in range(size)]
        piece = pieces[offset ^ low]
        if after and offset != low:
            piece = passed(piece, after)
        pieces.append(lax.ppermute(piece, axis, pairs))
    return pieces


def halving_order(size):
    bits = size.bit_length() - 1
    reverse = [sum(((p >> b) & 1) << (bits - 1 - b) for b in range(bits)) for p in range(size)]
    return reverse[::-1]


def place_rows(pieces, rows, narrow):
    me_wide, me_narrow = lax.axis_index("wide"), lax.axis_index("narrow")
    piece_rows = pieces[0].shape[0]
    block_rows = piece_rows * len(pieces) // narrow
    size = math.gcd(piece_rows, block_rows)
    for offset, piece in enumerate(pieces):
        for start in range(0, piece_rows, size):
            row = (me_wide ^ offset) * piece_rows + start
            block = (row // block_rows) ^ me_narrow
            place = sum(
                jnp.where(block == known, position, 0)
                for position, known in enumerate(halving_order(narrow))
            )
            spot = pl.multiple_of(place * block_rows + row % block_rows, size)
            rows[pl.ds(spot, size), :] = piece[start : start + size, :]


def look_up_kernel(slots, ids, lengths, table, *refs):
    live, weight, entries, picked, sem = refs[-5:]
    lookup = pltpu.make_async_copy(table, entries, sem)
    lookup.start()
    for i in range(lengths.shape[0]):
        slot = lax.broadcasted_iota(jnp.int32, (slots, LANES), 0)
        live[i * slots : (i + 1) * slots, :] = (slot < lengths[i]).astype(jnp.float32)
    lookup.wait()

    def pick(i, carry):
        entry = ids[i]
        lane = lax.broadcasted_iota(jnp.int32, (1, LANES), 1)
        row = entries[pl.ds(entry // LANES, 1), :]
        picked[pl.ds(i, 1), :] = jnp.where(lane == entry % LANES, row, 0.0)
        return carry

    lax.fori_loop(0, ids.shape[0], pick, 0)
    weight[...] = jnp.broadcast_to(jnp.sum(picked[...], axis=1, keepdims=True), weight.shape)


def look_up(ids, lengths, table, after):
    table = table.reshape(-1, LANES)
    flag = jax.ShapeDtypeStruct((ids.shape[0], LANES), jnp.float32)
    return pl.pallas_call(
        functools.partial(look_up_kernel, ids.shape[0] // lengths.shape[0]),
        out_shape=[flag, flag],
        in_specs=[IN_SMEM, IN_SMEM] + [ANYWHERE] * (1 + len(after)),
        out_specs=[IN_VMEM, IN_VMEM],
        scratch_shapes=[
            pltpu.VMEM(table.shape, table.dtype),
            pltpu.VMEM(flag.shape, flag.dtype),
            pltpu.SemaphoreType.DMA,
        ],
        compiler_params=pltpu.CompilerParams(vmem_limit_bytes=3 << 20),
    )(*map(in_hbm, (ids, lengths, table)), *after)


def load_kernel(matrix, *refs):
    dest, sem = refs[-2:]
    copy = pltpu.make_async_copy(matrix, dest, sem)
    copy.start()
    copy.wait()


def load(matrix, after=()):
    return pl.pallas_call(
        load_kernel,
        out_shape=pltpu.VMEM(matrix.shape, matrix.dtype),
        in_specs=[ANYWHERE] * (1 + len(after)),
        out_specs=IN_VMEM,
        scratch_shapes=[pltpu.SemaphoreType.DMA],
        compiler_params=pltpu.CompilerParams(vmem_limit_bytes=1 << 20),
    )(in_hbm(matrix), *after)


def tile_of(cols):
    for tile in (512, 256, 128):
        if cols % tile == 0:
            return tile
    return cols


def column_tiles(width):
    tile = tile_of(width)
    return [slice(start, start + tile) for start in range(0, width, tile)]


def column_chunks(width):
    tile = tile_of(width)
    first = width // tile // 2 * tile
    return [(0, first), (first, width - first)] if first else [(0, width)]


def product_kernel(pieces, after, narrow, blocks, *refs):
    tokens, matrix, outs = refs[:pieces], refs[pieces], refs[pieces + 1 + after :]
    if pieces > 1:
        place_rows(tokens, outs[0], narrow)
        tokens, outs = outs[:1], outs[1:]
    for cols in column_tiles(matrix.shape[1]):
        total = jnp.dot(tokens[0][...], matrix[:, cols], preferred_element_type=jnp.float32)
        for out, (row, col) in zip(outs, blocks):
            if col <= cols.start and cols.stop <= col + out.shape[1]:
                value = total[row : row + out.shape[0]].astype(out.dtype)
                out[:, cols.start - col : cols.stop - col] = value


def part_sizes(total, narrow):
    sizes, left = [], total // 2
    while left > total // narrow:
        left //= 2
        sizes.append(left)
    return sizes + [left]


def product(tokens, matrix, narrow, after):
    placing = len(tokens) > 1
    total = sum(t.shape[0] for t in tokens)
    depth, width = matrix.shape
    sizes = part_sizes(total, narrow)
    sent = []
    for k in range(len(sizes)):
        sent += [(k, *chunk) for chunk in (column_chunks(width) if k + 1 < len(sizes) else [(0, width)])]
    blocks = [(sum(sizes[:k]), first) for k, first, _ in sent]
    blocks += [(total // 2 + sum(sizes[:k]), 0) for k in range(len(sizes))]
    shapes = [(sizes[k], count) for k, _, count in sent] + [(size, width) for size in sizes]
    found = pl.pallas_call(
        functools.partial(product_kernel, len(tokens), len(after), narrow, blocks),
        out_shape=[jax.ShapeDtypeStruct((total, depth), tokens[0].dtype)] * placing
        + [jax.ShapeDtypeStruct(shape, jnp.bfloat16) for shape in shapes],
        in_specs=[IN_VMEM] * len(tokens) + [IN_VMEM] + [ANYWHERE] * len(after),
        out_specs=[IN_VMEM] * (placing + len(shapes)),
        compiler_params=pltpu.CompilerParams(vmem_limit_bytes=4 << 20),
    )(*tokens, in_vmem(matrix), *after)
    rows, found = (found[:1], found[1:]) if placing else (tokens, found)
    sends = [(array, k, first) for array, (k, first, _) in zip(found, sent)]
    return rows, sends, found[len(sent) :]


def exchange(array, step, size):
    return lax.ppermute(array, "narrow", [(i, i ^ (1 << step)) for i in range(size)])


def addends(parts, came, k):
    found = [(parts[k], (0, 0))]
    for array, first, behind, col in came:
        if first <= k < behind:
            found.append((array, (sum(part.shape[0] for part in parts[first:k]), col)))
    return [array for array, _ in found], tuple(place for _, place in found)


def added(refs, places, count, cols):
    total = None
    for ref, (row, col) in zip(refs, places):
        if col <= cols.start and cols.stop <= col + ref.shape[1]:
            term = ref[row : row + count, cols.start - col : cols.stop - col].astype(jnp.float32)
            total = term if total is None else total + term
    return total


def next_kernel(places, *refs):
    out = refs[-1]
    for cols in column_tiles(out.shape[1]):
        out[:, cols] = added(refs, places, out.shape[0], cols).astype(out.dtype)


def finish(sends, keeps, narrow, after):
    came = [(exchange(array, 0, narrow), k, k + 1, col) for array, k, col in sends]
    sent = sends[0][0]
    for k in range(len(keeps) - 1):
        arrays, places = addends(keeps, came, k)
        sent = pl.pallas_call(
            functools.partial(next_kernel, places),
            out_shape=jax.ShapeDtypeStruct(keeps[k].shape, jnp.bfloat16),
            in_specs=[IN_VMEM] * len(arrays) + [ANYWHERE] * len(after),
            out_specs=IN_VMEM,
            compiler_params=pltpu.CompilerParams(vmem_limit_bytes=2 << 20),
        )(*arrays, *after)
        came.append((exchange(sent, k + 1, narrow), k + 1, len(keeps), 0))
    return sent, addends(keeps, came, len(keeps) - 1)


def target_kernel(places, live, *refs):
    act, out = refs[-2:]
    count = len(places[0])
    for cols in column_tiles(out.shape[1]):
        gate = added(refs[:count], places[0], out.shape[0], cols)
        upper = added(refs[count:], places[1], out.shape[0], cols)
        value = live[:, :1] * (jax.nn.silu(gate) * upper)
        act[:, cols] = value
        out[:, cols] = value.astype(out.dtype)


def target_end(live, gate, upper):
    arrays = gate[0] + upper[0]
    shape = gate[0][0].shape
    return pl.pallas_call(
        functools.partial(target_kernel, (gate[1], upper[1])),
        out_shape=[jax.ShapeDtypeStruct(shape, jnp.float32), jax.ShapeDtypeStruct(shape, jnp.bfloat16)],
        in_specs=[IN_VMEM] * (1 + len(arrays)),
        out_specs=[IN_VMEM] * 2,
        compiler_params=pltpu.CompilerParams(vmem_limit_bytes=4 << 20),
    )(live, *arrays)


def source_kernel(starts, live, weight, *refs):
    terms, out = refs[:-1], refs[-1]
    for cols in column_tiles(out.shape[1]):
        gate = added(terms, starts, out.shape[0], cols)
        out[:, cols] = (live[:, :1] * weight[:, :1]) * jax.nn.silu(gate)


def source_middle(live, weight, own):
    arrays, starts = own
    return pl.pallas_call(
        functools.partial(source_kernel, starts),
        out_shape=jax.ShapeDtypeStruct((live.shape[0], arrays[0].shape[1]), jnp.float32),
        in_specs=[IN_VMEM] * (2 + len(arrays)),
        out_specs=IN_VMEM,
        compiler_params=pltpu.CompilerParams(vmem_limit_bytes=4 << 20),
    )(live, weight, *arrays)


def ratio_kernel(starts, act, gated, *refs):
    terms, out = refs[:-1], refs[-1]
    for cols in column_tiles(out.shape[1]):
        upper = added(terms, starts, out.shape[0], cols)
        out[:, cols] = (act[:, cols] - gated[:, cols] * upper).astype(out.dtype)


def ratio_end(act, gated, own):
    arrays, starts = own
    return pl.pallas_call(
        functools.partial(ratio_kernel, starts),
        out_shape=jax.ShapeDtypeStruct(act.shape, jnp.bfloat16),
        in_specs=[IN_VMEM] * (2 + len(arrays)),
        out_specs=IN_VMEM,
        compiler_params=pltpu.CompilerParams(vmem_limit_bytes=4 << 20),
    )(act, gated, *arrays)


def local(mesh_shape, target_states, source_states, target_gate, target_up, source_gate, source_up, token_ids, lengths, ratio_weight):
    wide, narrow = mesh_shape["wide"], mesh_shape["narrow"]
    target_gate = load(target_gate)
    target_pieces = gather_pieces(target_states, "wide", wide, (target_gate,))
    source_pieces = gather_pieces(source_states, "wide", wide)

    rows, sends, keeps = product(target_pieces, target_gate, narrow, ())
    _, up_sends, up_keeps = product(rows, target_up, narrow, (sends[0][0],))
    sent, target_g = finish(sends, keeps, narrow, (up_sends[0][0], *source_pieces[1:]))
    sent, target_u = finish(up_sends, up_keeps, narrow, (sent,))

    rows, sends, keeps = product(source_pieces, source_gate, narrow, (sent,))
    after = (sends[0][0], target_g[0][-1])
    _, up_sends, up_keeps = product(rows, source_up, narrow, after)
    sent, source_g = finish(sends, keeps, narrow, (up_sends[0][0],))
    sent, source_u = finish(up_sends, up_keeps, narrow, (sent, target_u[0][-1]))
    live, weight = look_up(token_ids, lengths, ratio_weight, (sent,))
    act, target_out = target_end(live, target_g, target_u)
    gated = source_middle(live, weight, source_g)
    ratio_out = ratio_end(act, gated, source_u)
    return (target_out, ratio_out)


def solution(mesh):
    placed = (
        P(("groups", "wide"), "narrow"),
        P(("groups", "wide"), "narrow"),
        P("narrow", "wide"),
        P("narrow", "wide"),
        P("narrow", "wide"),
        P("narrow", "wide"),
        P(("groups", "narrow")),
        P(("groups", "narrow")),
        P(),
    )
    mesh_shape = dict(mesh.shape)

    def body(*args):
        return local(mesh_shape, *args)

    return jax.shard_map(
        body,
        mesh=mesh,
        in_specs=placed,
        out_specs=(P(("groups", "narrow"), "wide"), P(("groups", "narrow"), "wide")),
        check_vma=False,
    )
```

```python
import functools
import math

import jax
import jax.numpy as jnp
from jax import lax
from jax.experimental import pallas as pl
from jax.experimental.pallas import tpu as pltpu
from jax.sharding import PartitionSpec as P

IN_VMEM = pl.BlockSpec(memory_space=pltpu.VMEM)
IN_SMEM = pl.BlockSpec(memory_space=pltpu.SMEM)
ANYWHERE = pl.BlockSpec(memory_space=pl.ANY)
LANES = 128


def in_hbm(array):
    return pltpu.with_memory_space_constraint(array, pltpu.HBM)


def in_vmem(array):
    return pltpu.with_memory_space_constraint(array, pltpu.VMEM)


def pass_kernel(piece, *refs):
    refs[-1][...] = piece[...]


def passed(piece, after):
    return pl.pallas_call(
        pass_kernel,
        out_shape=jax.ShapeDtypeStruct(piece.shape, piece.dtype),
        in_specs=[IN_VMEM] + [ANYWHERE] * len(after),
        out_specs=IN_VMEM,
        compiler_params=pltpu.CompilerParams(vmem_limit_bytes=1 << 20),
    )(piece, *after)


def gather_pieces(piece, axis, size, after=None, relays_after=None):
    pieces = [piece] + [None] * (size - 1)
    near = [1 << b for b in range(size.bit_length() - 1)]
    for offset in near[::-1] + [o for o in range(size) if o & (o - 1)]:
        low = offset & -offset
        source = pieces[offset ^ low]
        if after is not None and offset == low:
            source = passed(piece, (after,))
        if relays_after is not None and offset != low:
            source = passed(source, (relays_after,))
        pieces[offset] = lax.ppermute(source, axis, [(i, i ^ low) for i in range(size)])
        after = pieces[offset] if after is not None else None
    return pieces


def halving_order(size):
    bits = size.bit_length() - 1
    reverse = [sum(((p >> b) & 1) << (bits - 1 - b) for b in range(bits)) for p in range(size)]
    return reverse[::-1]


def place_rows(pieces, rows, narrow):
    me_wide, me_narrow = lax.axis_index("wide"), lax.axis_index("narrow")
    piece_rows = pieces[0].shape[0]
    block_rows = piece_rows * len(pieces) // narrow
    size = math.gcd(piece_rows, block_rows)
    for offset, piece in enumerate(pieces):
        for start in range(0, piece_rows, size):
            row = (me_wide ^ offset) * piece_rows + start
            block = (row // block_rows) ^ me_narrow
            place = sum(
                jnp.where(block == known, position, 0)
                for position, known in enumerate(halving_order(narrow))
            )
            spot = pl.multiple_of(place * block_rows + row % block_rows, size)
            rows[pl.ds(spot, size), :] = piece[start : start + size, :]


def look_up_kernel(slots, ids, lengths, table, *refs):
    live, weight, entries, picked, sem = refs[-5:]
    lookup = pltpu.make_async_copy(table, entries, sem)
    lookup.start()
    for i in range(lengths.shape[0]):
        slot = lax.broadcasted_iota(jnp.int32, (slots, LANES), 0)
        live[i * slots : (i + 1) * slots, :] = (slot < lengths[i]).astype(jnp.float32)
    lookup.wait()

    def pick(i, carry):
        entry = ids[i]
        lane = lax.broadcasted_iota(jnp.int32, (1, LANES), 1)
        row = entries[pl.ds(entry // LANES, 1), :]
        picked[pl.ds(i, 1), :] = jnp.where(lane == entry % LANES, row, 0.0)
        return carry

    lax.fori_loop(0, ids.shape[0], pick, 0)
    weight[...] = jnp.broadcast_to(jnp.sum(picked[...], axis=1, keepdims=True), weight.shape)


def look_up(ids, lengths, table, after):
    table = table.reshape(-1, LANES)
    flag = jax.ShapeDtypeStruct((ids.shape[0], LANES), jnp.float32)
    return pl.pallas_call(
        functools.partial(look_up_kernel, ids.shape[0] // lengths.shape[0]),
        out_shape=[flag, flag],
        in_specs=[IN_SMEM, IN_SMEM] + [ANYWHERE] * (1 + len(after)),
        out_specs=[IN_VMEM, IN_VMEM],
        scratch_shapes=[
            pltpu.VMEM(table.shape, table.dtype),
            pltpu.VMEM(flag.shape, flag.dtype),
            pltpu.SemaphoreType.DMA,
        ],
        compiler_params=pltpu.CompilerParams(vmem_limit_bytes=3 << 20),
    )(*map(in_hbm, (ids, lengths, table)), *after)


def load_kernel(matrix, *refs):
    dest, sem = refs[-2:]
    copy = pltpu.make_async_copy(matrix, dest, sem)
    copy.start()
    copy.wait()


def load(matrix, after=()):
    return pl.pallas_call(
        load_kernel,
        out_shape=pltpu.VMEM(matrix.shape, matrix.dtype),
        in_specs=[ANYWHERE] * (1 + len(after)),
        out_specs=IN_VMEM,
        scratch_shapes=[pltpu.SemaphoreType.DMA],
        compiler_params=pltpu.CompilerParams(vmem_limit_bytes=1 << 20),
    )(in_hbm(matrix), *after)


def tile_of(cols):
    for tile in (512, 256, 128):
        if cols % tile == 0:
            return tile
    return cols


def column_tiles(width):
    tile = tile_of(width)
    return [slice(start, start + tile) for start in range(0, width, tile)]


def column_chunks(width):
    tile = tile_of(width)
    first = width // tile // 2 * tile
    return [(0, first), (first, width - first)] if first else [(0, width)]


def product_kernel(pieces, after, narrow, blocks, *refs):
    tokens, matrix = refs[:pieces], refs[pieces]
    beside, outs = refs[pieces + 1 : len(refs) - len(blocks) - (pieces > 1) - after], refs[-len(blocks) :]
    if pieces > 1:
        rows = refs[-len(blocks) - 1]
        place_rows(tokens, rows, narrow)
        tokens = [rows]
    for earlier in beside:
        outs[-1][:, : earlier.shape[1]] = earlier[...]
    for cols in column_tiles(matrix.shape[1]):
        total = jnp.dot(tokens[0][...], matrix[:, cols], preferred_element_type=jnp.float32)
        for out, (row, col) in zip(outs, blocks):
            if col <= cols.start and cols.stop <= col + out.shape[1]:
                value = total[row : row + out.shape[0]].astype(out.dtype)
                out[:, cols.start - col : cols.stop - col] = value


def part_sizes(total, narrow):
    sizes, left = [], total // 2
    while left > total // narrow:
        left //= 2
        sizes.append(left)
    return sizes + [left]


def product(tokens, matrix, narrow, after, beside=(), split=True):
    placing = len(tokens) > 1
    total = sum(t.shape[0] for t in tokens)
    depth, width = matrix.shape
    sizes = part_sizes(total, narrow)
    sent = [(k, *cols) for k in range(len(sizes) - 1) for cols in (column_chunks(width) if split else [(0, width)])]
    ahead = sum(b.shape[1] for b in beside)
    blocks = [(sum(sizes[:k]), first) for k, first, _ in sent]
    blocks += [(total // 2 + sum(sizes[:k]), 0) for k in range(len(sizes))]
    blocks += [(sum(sizes[:-1]), -ahead)]
    shapes = [(sizes[k], count) for k, _, count in sent] + [(size, width) for size in sizes]
    shapes += [(sizes[-1], ahead + width)]
    found = pl.pallas_call(
        functools.partial(product_kernel, len(tokens), len(after), narrow, blocks),
        out_shape=[jax.ShapeDtypeStruct((total, depth), tokens[0].dtype)] * placing
        + [jax.ShapeDtypeStruct(shape, jnp.bfloat16) for shape in shapes],
        in_specs=[IN_VMEM] * (len(tokens) + 1 + len(beside)) + [ANYWHERE] * len(after),
        out_specs=[IN_VMEM] * (placing + len(shapes)),
        compiler_params=pltpu.CompilerParams(vmem_limit_bytes=4 << 20),
    )(*tokens, in_vmem(matrix), *beside, *after)
    rows, found = (found[:1], found[1:]) if placing else (tokens, found)
    sends = [(array, k, first) for array, (k, first, _) in zip(found, sent)]
    return rows, sends, found[-1], found[len(sent) : -1]


def exchange(array, step, size):
    return lax.ppermute(array, "narrow", [(i, i ^ (1 << step)) for i in range(size)])


def addends(parts, came, k):
    found = [(parts[k], (0, 0))]
    for array, first, behind, col in came:
        if first <= k < behind:
            found.append((array, (sum(part.shape[0] for part in parts[first:k]), col)))
    return [array for array, _ in found], tuple(place for _, place in found)


def added(refs, places, count, cols):
    total = None
    for ref, (row, col) in zip(refs, places):
        if col <= cols.start and cols.stop <= col + ref.shape[1]:
            term = ref[row : row + count, cols.start - col : cols.stop - col].astype(jnp.float32)
            total = term if total is None else total + term
    return total


def next_kernel(places, *refs):
    out = refs[-1]
    for cols in column_tiles(out.shape[1]):
        out[:, cols] = added(refs, places, out.shape[0], cols).astype(out.dtype)


def finish(sends, keeps, own, narrow, after):
    last = len(keeps) - 1
    came = [(exchange(array, 0, narrow), k, k + 1, col) for array, k, col in sends]
    came.append((own[0], last, last + 1, own[1]))
    sent = keeps[-1]
    for k in range(last):
        arrays, places = addends(keeps, came, k)
        sent = pl.pallas_call(
            functools.partial(next_kernel, places),
            out_shape=jax.ShapeDtypeStruct(keeps[k].shape, jnp.bfloat16),
            in_specs=[IN_VMEM] * len(arrays) + [ANYWHERE] * len(after),
            out_specs=IN_VMEM,
            compiler_params=pltpu.CompilerParams(vmem_limit_bytes=2 << 20),
        )(*arrays, *after)
        came.append((exchange(sent, k + 1, narrow), k + 1, len(keeps), 0))
    return sent, addends(keeps, came, len(keeps) - 1)


def target_kernel(places, live, *refs):
    act, out = refs[-2:]
    count = len(places[0])
    for cols in column_tiles(out.shape[1]):
        gate = added(refs[:count], places[0], out.shape[0], cols)
        upper = added(refs[count:], places[1], out.shape[0], cols)
        value = live[:, :1] * (jax.nn.silu(gate) * upper)
        act[:, cols] = value
        out[:, cols] = value.astype(out.dtype)


def target_end(live, gate, upper):
    arrays = gate[0] + upper[0]
    shape = gate[0][0].shape
    return pl.pallas_call(
        functools.partial(target_kernel, (gate[1], upper[1])),
        out_shape=[jax.ShapeDtypeStruct(shape, jnp.float32), jax.ShapeDtypeStruct(shape, jnp.bfloat16)],
        in_specs=[IN_VMEM] * (1 + len(arrays)),
        out_specs=[IN_VMEM] * 2,
        compiler_params=pltpu.CompilerParams(vmem_limit_bytes=4 << 20),
    )(live, *arrays)


def source_kernel(starts, live, weight, *refs):
    terms, out = refs[:-1], refs[-1]
    for cols in column_tiles(out.shape[1]):
        gate = added(terms, starts, out.shape[0], cols)
        out[:, cols] = (live[:, :1] * weight[:, :1]) * jax.nn.silu(gate)


def source_middle(live, weight, own):
    arrays, starts = own
    return pl.pallas_call(
        functools.partial(source_kernel, starts),
        out_shape=jax.ShapeDtypeStruct((live.shape[0], arrays[0].shape[1]), jnp.float32),
        in_specs=[IN_VMEM] * (2 + len(arrays)),
        out_specs=IN_VMEM,
        compiler_params=pltpu.CompilerParams(vmem_limit_bytes=4 << 20),
    )(live, weight, *arrays)


def ratio_kernel(starts, act, gated, *refs):
    terms, out = refs[:-1], refs[-1]
    for cols in column_tiles(out.shape[1]):
        upper = added(terms, starts, out.shape[0], cols)
        out[:, cols] = (act[:, cols] - gated[:, cols] * upper).astype(out.dtype)


def ratio_end(act, gated, own):
    arrays, starts = own
    return pl.pallas_call(
        functools.partial(ratio_kernel, starts),
        out_shape=jax.ShapeDtypeStruct(act.shape, jnp.bfloat16),
        in_specs=[IN_VMEM] * (2 + len(arrays)),
        out_specs=IN_VMEM,
        compiler_params=pltpu.CompilerParams(vmem_limit_bytes=4 << 20),
    )(act, gated, *arrays)


def local(mesh_shape, target_states, source_states, target_gate, target_up, source_gate, source_up, token_ids, lengths, ratio_weight):
    wide, narrow = mesh_shape["wide"], mesh_shape["narrow"]
    target_gate = load(target_gate)
    target_pieces = gather_pieces(target_states, "wide", wide, relays_after=target_gate)
    source_pieces = gather_pieces(source_states, "wide", wide, target_pieces[wide // 2])
    width = target_gate.shape[1]

    rows, sends, own, keeps = product(target_pieces, target_gate, narrow, (), split=False)
    _, up_sends, own, up_keeps = product(rows, target_up, narrow, (keeps[0],), (own,))
    target_own = exchange(own, 0, narrow)
    after = (up_keeps[0], *source_pieces[1:])
    sent, target_g = finish(sends, keeps, (target_own, 0), narrow, after)
    sent, target_u = finish(up_sends, up_keeps, (target_own, -width), narrow, (sent,))

    rows, sends, own, keeps = product(source_pieces, source_gate, narrow, (sent,))
    after = (keeps[0], target_g[0][-1])
    _, up_sends, own, up_keeps = product(rows, source_up, narrow, after, (own,))
    own = exchange(own, 0, narrow)
    sent, source_g = finish(sends, keeps, (own, 0), narrow, (up_keeps[0], target_own))
    sent, source_u = finish(up_sends, up_keeps, (own, -width), narrow, (sent, target_u[0][-1]))
    live, weight = look_up(token_ids, lengths, ratio_weight, (sent,))
    act, target_out = target_end(live, target_g, target_u)
    gated = source_middle(live, weight, source_g)
    ratio_out = ratio_end(act, gated, source_u)
    return (target_out, ratio_out)


def solution(mesh):
    placed = (
        P(("groups", "wide"), "narrow"),
        P(("groups", "wide"), "narrow"),
        P("narrow", "wide"),
        P("narrow", "wide"),
        P("narrow", "wide"),
        P("narrow", "wide"),
        P(("groups", "narrow")),
        P(("groups", "narrow")),
        P(),
    )
    mesh_shape = dict(mesh.shape)

    def body(*args):
        return local(mesh_shape, *args)

    return jax.shard_map(
        body,
        mesh=mesh,
        in_specs=placed,
        out_specs=(P(("groups", "narrow"), "wide"), P(("groups", "narrow"), "wide")),
        check_vma=False,
    )
```

```python
import functools
import math

import jax
import jax.numpy as jnp
from jax import lax
from jax.experimental import pallas as pl
from jax.experimental.pallas import tpu as pltpu
from jax.sharding import PartitionSpec as P

IN_VMEM = pl.BlockSpec(memory_space=pltpu.VMEM)
IN_SMEM = pl.BlockSpec(memory_space=pltpu.SMEM)
ANYWHERE = pl.BlockSpec(memory_space=pl.ANY)
LANES = 128


def in_hbm(array):
    return pltpu.with_memory_space_constraint(array, pltpu.HBM)


def in_vmem(array):
    return pltpu.with_memory_space_constraint(array, pltpu.VMEM)


def pass_kernel(piece, *refs):
    refs[-1][...] = piece[...]


def passed(piece, after):
    return pl.pallas_call(
        pass_kernel,
        out_shape=jax.ShapeDtypeStruct(piece.shape, piece.dtype),
        in_specs=[IN_VMEM] + [ANYWHERE] * len(after),
        out_specs=IN_VMEM,
        compiler_params=pltpu.CompilerParams(vmem_limit_bytes=1 << 20),
    )(piece, *after)


def gather_pieces(piece, axis, size, chained=False, relays_after=None):
    pieces = [piece] + [None] * (size - 1)
    after, near = None, [1 << b for b in range(size.bit_length() - 1)]
    for offset in near[::-1] + [o for o in range(size) if o & (o - 1)]:
        low = offset & -offset
        source = pieces[offset ^ low]
        if after is not None and offset == low:
            source = passed(piece, (after,))
        if relays_after is not None and offset != low:
            source = passed(source, (relays_after,))
        pieces[offset] = lax.ppermute(source, axis, [(i, i ^ low) for i in range(size)])
        after = pieces[offset] if chained else None
    return pieces


def halving_order(size):
    bits = size.bit_length() - 1
    reverse = [sum(((p >> b) & 1) << (bits - 1 - b) for b in range(bits)) for p in range(size)]
    return reverse[::-1]


def place_rows(pieces, rows, narrow):
    me_wide, me_narrow = lax.axis_index("wide"), lax.axis_index("narrow")
    piece_rows = pieces[0].shape[0]
    block_rows = piece_rows * len(pieces) // narrow
    size = math.gcd(piece_rows, block_rows)
    for offset, piece in enumerate(pieces):
        for start in range(0, piece_rows, size):
            row = (me_wide ^ offset) * piece_rows + start
            block = (row // block_rows) ^ me_narrow
            place = sum(
                jnp.where(block == known, position, 0)
                for position, known in enumerate(halving_order(narrow))
            )
            spot = pl.multiple_of(place * block_rows + row % block_rows, size)
            rows[pl.ds(spot, size), :] = piece[start : start + size, :]


def look_up_kernel(slots, ids, lengths, table, *refs):
    live, weight, entries, picked, sem = refs[-5:]
    lookup = pltpu.make_async_copy(table, entries, sem)
    lookup.start()
    for i in range(lengths.shape[0]):
        slot = lax.broadcasted_iota(jnp.int32, (slots, LANES), 0)
        live[i * slots : (i + 1) * slots, :] = (slot < lengths[i]).astype(jnp.float32)
    lookup.wait()

    def pick(i, carry):
        entry = ids[i]
        lane = lax.broadcasted_iota(jnp.int32, (1, LANES), 1)
        row = entries[pl.ds(entry // LANES, 1), :]
        picked[pl.ds(i, 1), :] = jnp.where(lane == entry % LANES, row, 0.0)
        return carry

    lax.fori_loop(0, ids.shape[0], pick, 0)
    weight[...] = jnp.broadcast_to(jnp.sum(picked[...], axis=1, keepdims=True), weight.shape)


def look_up(ids, lengths, table, after):
    table = table.reshape(-1, LANES)
    flag = jax.ShapeDtypeStruct((ids.shape[0], LANES), jnp.float32)
    return pl.pallas_call(
        functools.partial(look_up_kernel, ids.shape[0] // lengths.shape[0]),
        out_shape=[flag, flag],
        in_specs=[IN_SMEM, IN_SMEM] + [ANYWHERE] * (1 + len(after)),
        out_specs=[IN_VMEM, IN_VMEM],
        scratch_shapes=[
            pltpu.VMEM(table.shape, table.dtype),
            pltpu.VMEM(flag.shape, flag.dtype),
            pltpu.SemaphoreType.DMA,
        ],
        compiler_params=pltpu.CompilerParams(vmem_limit_bytes=3 << 20),
    )(*map(in_hbm, (ids, lengths, table)), *after)


def load_kernel(matrix, *refs):
    dest, sem = refs[-2:]
    copy = pltpu.make_async_copy(matrix, dest, sem)
    copy.start()
    copy.wait()


def load(matrix, after=()):
    return pl.pallas_call(
        load_kernel,
        out_shape=pltpu.VMEM(matrix.shape, matrix.dtype),
        in_specs=[ANYWHERE] * (1 + len(after)),
        out_specs=IN_VMEM,
        scratch_shapes=[pltpu.SemaphoreType.DMA],
        compiler_params=pltpu.CompilerParams(vmem_limit_bytes=1 << 20),
    )(in_hbm(matrix), *after)


def tile_of(cols):
    for tile in (512, 256, 128):
        if cols % tile == 0:
            return tile
    return cols


def column_tiles(width):
    tile = tile_of(width)
    return [slice(start, start + tile) for start in range(0, width, tile)]


def column_chunks(width):
    tile = tile_of(width)
    first = width // tile // 2 * tile
    return [(0, first), (first, width - first)] if first else [(0, width)]


def product_kernel(pieces, after, narrow, blocks, *refs):
    tokens, matrix = refs[:pieces], refs[pieces]
    beside, outs = refs[pieces + 1 : len(refs) - len(blocks) - (pieces > 1) - after], refs[-len(blocks) :]
    if pieces > 1:
        rows = refs[-len(blocks) - 1]
        place_rows(tokens, rows, narrow)
        tokens = [rows]
    for earlier in beside:
        outs[-1][:, : earlier.shape[1]] = earlier[...]
    for cols in column_tiles(matrix.shape[1]):
        total = jnp.dot(tokens[0][...], matrix[:, cols], preferred_element_type=jnp.float32)
        for out, (row, col) in zip(outs, blocks):
            if col <= cols.start and cols.stop <= col + out.shape[1]:
                value = total[row : row + out.shape[0]].astype(out.dtype)
                out[:, cols.start - col : cols.stop - col] = value


def part_sizes(total, narrow):
    sizes, left = [], total // 2
    while left > total // narrow:
        left //= 2
        sizes.append(left)
    return sizes + [left]


def product(tokens, matrix, narrow, after, beside=(), split=True):
    placing = len(tokens) > 1
    total = sum(t.shape[0] for t in tokens)
    depth, width = matrix.shape
    sizes = part_sizes(total, narrow)
    sent = [(k, *cols) for k in range(len(sizes) - 1) for cols in (column_chunks(width) if split else [(0, width)])]
    ahead = sum(b.shape[1] for b in beside)
    blocks = [(sum(sizes[:k]), first) for k, first, _ in sent]
    blocks += [(total // 2 + sum(sizes[:k]), 0) for k in range(len(sizes))]
    blocks += [(sum(sizes[:-1]), -ahead)]
    shapes = [(sizes[k], count) for k, _, count in sent] + [(size, width) for size in sizes]
    shapes += [(sizes[-1], ahead + width)]
    found = pl.pallas_call(
        functools.partial(product_kernel, len(tokens), len(after), narrow, blocks),
        out_shape=[jax.ShapeDtypeStruct((total, depth), tokens[0].dtype)] * placing
        + [jax.ShapeDtypeStruct(shape, jnp.bfloat16) for shape in shapes],
        in_specs=[IN_VMEM] * (len(tokens) + 1 + len(beside)) + [ANYWHERE] * len(after),
        out_specs=[IN_VMEM] * (placing + len(shapes)),
        compiler_params=pltpu.CompilerParams(vmem_limit_bytes=4 << 20),
    )(*tokens, in_vmem(matrix), *beside, *after)
    rows, found = (found[:1], found[1:]) if placing else (tokens, found)
    sends = [(array, k, first) for array, (k, first, _) in zip(found, sent)]
    return rows, sends, found[-1], found[len(sent) : -1]


def exchange(array, step, size):
    return lax.ppermute(array, "narrow", [(i, i ^ (1 << step)) for i in range(size)])


def addends(parts, came, k):
    found = [(parts[k], (0, 0))]
    for array, first, behind, col in came:
        if first <= k < behind:
            found.append((array, (sum(part.shape[0] for part in parts[first:k]), col)))
    return [array for array, _ in found], tuple(place for _, place in found)


def added(refs, places, count, cols):
    total = None
    for ref, (row, col) in zip(refs, places):
        if col <= cols.start and cols.stop <= col + ref.shape[1]:
            term = ref[row : row + count, cols.start - col : cols.stop - col].astype(jnp.float32)
            total = term if total is None else total + term
    return total


def next_kernel(places, *refs):
    out = refs[-1]
    for cols in column_tiles(out.shape[1]):
        out[:, cols] = added(refs, places, out.shape[0], cols).astype(out.dtype)


def finish(sends, keeps, own, narrow, after):
    last = len(keeps) - 1
    came = [(exchange(array, 0, narrow), k, k + 1, col) for array, k, col in sends]
    came.append((own[0], last, last + 1, own[1]))
    sent = keeps[-1]
    for k in range(last):
        arrays, places = addends(keeps, came, k)
        sent = pl.pallas_call(
            functools.partial(next_kernel, places),
            out_shape=jax.ShapeDtypeStruct(keeps[k].shape, jnp.bfloat16),
            in_specs=[IN_VMEM] * len(arrays) + [ANYWHERE] * len(after),
            out_specs=IN_VMEM,
            compiler_params=pltpu.CompilerParams(vmem_limit_bytes=2 << 20),
        )(*arrays, *after)
        came.append((exchange(sent, k + 1, narrow), k + 1, len(keeps), 0))
    return sent, addends(keeps, came, len(keeps) - 1)


def target_kernel(places, live, *refs):
    act, out = refs[-2:]
    count = len(places[0])
    for cols in column_tiles(out.shape[1]):
        gate = added(refs[:count], places[0], out.shape[0], cols)
        upper = added(refs[count:], places[1], out.shape[0], cols)
        value = live[:, :1] * (jax.nn.silu(gate) * upper)
        act[:, cols] = value
        out[:, cols] = value.astype(out.dtype)


def target_end(live, gate, upper):
    arrays = gate[0] + upper[0]
    shape = gate[0][0].shape
    return pl.pallas_call(
        functools.partial(target_kernel, (gate[1], upper[1])),
        out_shape=[jax.ShapeDtypeStruct(shape, jnp.float32), jax.ShapeDtypeStruct(shape, jnp.bfloat16)],
        in_specs=[IN_VMEM] * (1 + len(arrays)),
        out_specs=[IN_VMEM] * 2,
        compiler_params=pltpu.CompilerParams(vmem_limit_bytes=4 << 20),
    )(live, *arrays)


def source_kernel(starts, live, weight, *refs):
    terms, out = refs[:-1], refs[-1]
    for cols in column_tiles(out.shape[1]):
        gate = added(terms, starts, out.shape[0], cols)
        out[:, cols] = (live[:, :1] * weight[:, :1]) * jax.nn.silu(gate)


def source_middle(live, weight, own):
    arrays, starts = own
    return pl.pallas_call(
        functools.partial(source_kernel, starts),
        out_shape=jax.ShapeDtypeStruct((live.shape[0], arrays[0].shape[1]), jnp.float32),
        in_specs=[IN_VMEM] * (2 + len(arrays)),
        out_specs=IN_VMEM,
        compiler_params=pltpu.CompilerParams(vmem_limit_bytes=4 << 20),
    )(live, weight, *arrays)


def ratio_kernel(starts, act, gated, *refs):
    terms, out = refs[:-1], refs[-1]
    for cols in column_tiles(out.shape[1]):
        upper = added(terms, starts, out.shape[0], cols)
        out[:, cols] = (act[:, cols] - gated[:, cols] * upper).astype(out.dtype)


def ratio_end(act, gated, own):
    arrays, starts = own
    return pl.pallas_call(
        functools.partial(ratio_kernel, starts),
        out_shape=jax.ShapeDtypeStruct(act.shape, jnp.bfloat16),
        in_specs=[IN_VMEM] * (2 + len(arrays)),
        out_specs=IN_VMEM,
        compiler_params=pltpu.CompilerParams(vmem_limit_bytes=4 << 20),
    )(act, gated, *arrays)


def local(mesh_shape, target_states, source_states, target_gate, target_up, source_gate, source_up, token_ids, lengths, ratio_weight):
    wide, narrow = mesh_shape["wide"], mesh_shape["narrow"]
    target_gate = load(target_gate)
    target_pieces = gather_pieces(target_states, "wide", wide, relays_after=target_gate)
    source_pieces = gather_pieces(source_states, "wide", wide, chained=True)
    width = target_gate.shape[1]

    rows, sends, own, keeps = product(target_pieces, target_gate, narrow, ())
    _, up_sends, own, up_keeps = product(rows, target_up, narrow, (keeps[0],), (own,))
    target_own = exchange(own, 0, narrow)
    after = (up_keeps[0], *source_pieces[1:])
    sent, target_g = finish(sends, keeps, (target_own, 0), narrow, after)
    sent, target_u = finish(up_sends, up_keeps, (target_own, -width), narrow, (sent,))

    rows, sends, own, keeps = product(source_pieces, source_gate, narrow, (sent,))
    after = (keeps[0], target_g[0][-1])
    _, up_sends, own, up_keeps = product(rows, source_up, narrow, after, (own,))
    own = exchange(own, 0, narrow)
    sent, source_g = finish(sends, keeps, (own, 0), narrow, (up_keeps[0], target_own))
    sent, source_u = finish(up_sends, up_keeps, (own, -width), narrow, (sent, target_u[0][-1]))
    live, weight = look_up(token_ids, lengths, ratio_weight, (sent,))
    act, target_out = target_end(live, target_g, target_u)
    gated = source_middle(live, weight, source_g)
    ratio_out = ratio_end(act, gated, source_u)
    return (target_out, ratio_out)


def solution(mesh):
    placed = (
        P(("groups", "wide"), "narrow"),
        P(("groups", "wide"), "narrow"),
        P("narrow", "wide"),
        P("narrow", "wide"),
        P("narrow", "wide"),
        P("narrow", "wide"),
        P(("groups", "narrow")),
        P(("groups", "narrow")),
        P(),
    )
    mesh_shape = dict(mesh.shape)

    def body(*args):
        return local(mesh_shape, *args)

    return jax.shard_map(
        body,
        mesh=mesh,
        in_specs=placed,
        out_specs=(P(("groups", "narrow"), "wide"), P(("groups", "narrow"), "wide")),
        check_vma=False,
    )
```

```python
import functools
import math

import jax
import jax.numpy as jnp
from jax import lax
from jax.experimental import pallas as pl
from jax.experimental.pallas import tpu as pltpu
from jax.sharding import PartitionSpec as P

IN_VMEM = pl.BlockSpec(memory_space=pltpu.VMEM)
IN_SMEM = pl.BlockSpec(memory_space=pltpu.SMEM)
ANYWHERE = pl.BlockSpec(memory_space=pl.ANY)
LANES = 128


def in_hbm(array):
    return pltpu.with_memory_space_constraint(array, pltpu.HBM)


def in_vmem(array):
    return pltpu.with_memory_space_constraint(array, pltpu.VMEM)


def pass_kernel(count, *refs):
    for source, dest in zip(refs[:count], refs[-count:]):
        dest[...] = source[...]


def passed(arrays, after):
    return pl.pallas_call(
        functools.partial(pass_kernel, len(arrays)),
        out_shape=[jax.ShapeDtypeStruct(a.shape, a.dtype) for a in arrays],
        in_specs=[IN_VMEM] * len(arrays) + [ANYWHERE] * len(after),
        out_specs=[IN_VMEM] * len(arrays),
        compiler_params=pltpu.CompilerParams(vmem_limit_bytes=2 << 20),
    )(*arrays, *after)


def stack_kernel(*refs):
    row = 0
    for source in refs[:-1]:
        refs[-1][row : row + source.shape[0], :] = source[...]
        row += source.shape[0]


def stacked(arrays):
    rows = sum(a.shape[0] for a in arrays)
    return pl.pallas_call(
        stack_kernel,
        out_shape=jax.ShapeDtypeStruct((rows, arrays[0].shape[1]), arrays[0].dtype),
        in_specs=[IN_VMEM] * len(arrays),
        out_specs=IN_VMEM,
        compiler_params=pltpu.CompilerParams(vmem_limit_bytes=2 << 20),
    )(*arrays)


def gather_pieces(piece, axis, size, relays_after):
    pieces = [piece]
    for offset in range(1, size):
        low = offset & -offset
        source = pieces[offset ^ low]
        if offset != low:
            (source,) = passed([source], (relays_after,))
        pieces.append(lax.ppermute(source, axis, [(i, i ^ low) for i in range(size)]))
    return pieces, [(i, 0) for i in range(size)]


def gather_doubling(piece, axis, size):
    arrays, order, spots, low = [piece], [0], {0: (0, 0)}, size // 2
    while low:
        send = stacked(arrays) if len(arrays) > 1 else piece
        arrays.append(lax.ppermute(send, axis, [(i, i ^ low) for i in range(size)]))
        for place, offset in enumerate(order):
            spots[offset ^ low] = (len(arrays) - 1, place * piece.shape[0])
        order += [offset ^ low for offset in order]
        low //= 2
    return arrays, [spots[offset] for offset in range(size)]


def halving_order(size):
    bits = size.bit_length() - 1
    reverse = [sum(((p >> b) & 1) << (bits - 1 - b) for b in range(bits)) for p in range(size)]
    return reverse[::-1]


def place_rows(arrays, spots, rows, narrow):
    me_wide, me_narrow = lax.axis_index("wide"), lax.axis_index("narrow")
    piece_rows = rows.shape[0] // len(spots)
    block_rows = rows.shape[0] // narrow
    size = math.gcd(piece_rows, block_rows)
    for offset, (index, first) in enumerate(spots):
        for start in range(0, piece_rows, size):
            row = (me_wide ^ offset) * piece_rows + start
            block = (row // block_rows) ^ me_narrow
            place = sum(
                jnp.where(block == known, position, 0)
                for position, known in enumerate(halving_order(narrow))
            )
            spot = pl.multiple_of(place * block_rows + row % block_rows, size)
            rows[pl.ds(spot, size), :] = arrays[index][first + start : first + start + size, :]


def look_up_kernel(slots, ids, lengths, table, *refs):
    live, weight, entries, picked, sem = refs[-5:]
    lookup = pltpu.make_async_copy(table, entries, sem)
    lookup.start()
    for i in range(lengths.shape[0]):
        slot = lax.broadcasted_iota(jnp.int32, (slots, LANES), 0)
        live[i * slots : (i + 1) * slots, :] = (slot < lengths[i]).astype(jnp.float32)
    lookup.wait()

    def pick(i, carry):
        entry = ids[i]
        lane = lax.broadcasted_iota(jnp.int32, (1, LANES), 1)
        row = entries[pl.ds(entry // LANES, 1), :]
        picked[pl.ds(i, 1), :] = jnp.where(lane == entry % LANES, row, 0.0)
        return carry

    lax.fori_loop(0, ids.shape[0], pick, 0)
    weight[...] = jnp.broadcast_to(jnp.sum(picked[...], axis=1, keepdims=True), weight.shape)


def look_up(ids, lengths, table, after):
    table = table.reshape(-1, LANES)
    flag = jax.ShapeDtypeStruct((ids.shape[0], LANES), jnp.float32)
    return pl.pallas_call(
        functools.partial(look_up_kernel, ids.shape[0] // lengths.shape[0]),
        out_shape=[flag, flag],
        in_specs=[IN_SMEM, IN_SMEM] + [ANYWHERE] * (1 + len(after)),
        out_specs=[IN_VMEM, IN_VMEM],
        scratch_shapes=[
            pltpu.VMEM(table.shape, table.dtype),
            pltpu.VMEM(flag.shape, flag.dtype),
            pltpu.SemaphoreType.DMA,
        ],
        compiler_params=pltpu.CompilerParams(vmem_limit_bytes=3 << 20),
    )(*map(in_hbm, (ids, lengths, table)), *after)


def load_kernel(matrix, *refs):
    dest, sem = refs[-2:]
    copy = pltpu.make_async_copy(matrix, dest, sem)
    copy.start()
    copy.wait()


def load(matrix, after=()):
    return pl.pallas_call(
        load_kernel,
        out_shape=pltpu.VMEM(matrix.shape, matrix.dtype),
        in_specs=[ANYWHERE] * (1 + len(after)),
        out_specs=IN_VMEM,
        scratch_shapes=[pltpu.SemaphoreType.DMA],
        compiler_params=pltpu.CompilerParams(vmem_limit_bytes=1 << 20),
    )(in_hbm(matrix), *after)


def tile_of(cols):
    for tile in (512, 256, 128):
        if cols % tile == 0:
            return tile
    return cols


def column_tiles(width):
    tile = tile_of(width)
    return [slice(start, start + tile) for start in range(0, width, tile)]


def column_chunks(width):
    tile = tile_of(width)
    first = width // tile // 2 * tile
    return [(0, first), (first, width - first)] if first else [(0, width)]


def product_kernel(pieces, spots, after, narrow, blocks, *refs):
    tokens, matrix = refs[:pieces], refs[pieces]
    beside, outs = refs[pieces + 1 : len(refs) - len(blocks) - (pieces > 1) - after], refs[-len(blocks) :]
    if pieces > 1:
        rows = refs[-len(blocks) - 1]
        place_rows(tokens, spots, rows, narrow)
        tokens = [rows]
    for earlier in beside:
        outs[-1][:, : earlier.shape[1]] = earlier[...]
    for cols in column_tiles(matrix.shape[1]):
        total = jnp.dot(tokens[0][...], matrix[:, cols], preferred_element_type=jnp.float32)
        for out, (row, col) in zip(outs, blocks):
            if col <= cols.start and cols.stop <= col + out.shape[1]:
                value = total[row : row + out.shape[0]].astype(out.dtype)
                out[:, cols.start - col : cols.stop - col] = value


def part_sizes(total, narrow):
    sizes, left = [], total // 2
    while left > total // narrow:
        left //= 2
        sizes.append(left)
    return sizes + [left]


def product(tokens, matrix, narrow, after, beside=(), spots=()):
    placing = len(tokens) > 1
    total = sum(t.shape[0] for t in tokens)
    depth, width = matrix.shape
    sizes = part_sizes(total, narrow)
    sent = [(k, *cols) for k in range(len(sizes) - 1) for cols in column_chunks(width)]
    ahead = sum(b.shape[1] for b in beside)
    blocks = [(sum(sizes[:k]), first) for k, first, _ in sent]
    blocks += [(total // 2 + sum(sizes[:k]), 0) for k in range(len(sizes))]
    blocks += [(sum(sizes[:-1]), -ahead)]
    shapes = [(sizes[k], count) for k, _, count in sent] + [(size, width) for size in sizes]
    shapes += [(sizes[-1], ahead + width)]
    found = pl.pallas_call(
        functools.partial(product_kernel, len(tokens), spots, len(after), narrow, blocks),
        out_shape=[jax.ShapeDtypeStruct((total, depth), tokens[0].dtype)] * placing
        + [jax.ShapeDtypeStruct(shape, jnp.bfloat16) for shape in shapes],
        in_specs=[IN_VMEM] * (len(tokens) + 1 + len(beside)) + [ANYWHERE] * len(after),
        out_specs=[IN_VMEM] * (placing + len(shapes)),
        compiler_params=pltpu.CompilerParams(vmem_limit_bytes=4 << 20),
    )(*tokens, in_vmem(matrix), *beside, *after)
    rows, found = (found[:1], found[1:]) if placing else (tokens, found)
    sends = [(array, k, first) for array, (k, first, _) in zip(found, sent)]
    return rows, sends, found[-1], found[len(sent) : -1]


def resent(sends, after):
    if not sends:
        return sends
    arrays = passed([array for array, _, _ in sends], after)
    return [(array, k, col) for array, (_, k, col) in zip(arrays, sends)]


def exchange(array, step, size):
    return lax.ppermute(array, "narrow", [(i, i ^ (1 << step)) for i in range(size)])


def addends(parts, came, k):
    found = [(parts[k], (0, 0))]
    for array, first, behind, col in came:
        if first <= k < behind:
            found.append((array, (sum(part.shape[0] for part in parts[first:k]), col)))
    return [array for array, _ in found], tuple(place for _, place in found)


def added(refs, places, count, cols):
    total = None
    for ref, (row, col) in zip(refs, places):
        if col <= cols.start and cols.stop <= col + ref.shape[1]:
            term = ref[row : row + count, cols.start - col : cols.stop - col].astype(jnp.float32)
            total = term if total is None else total + term
    return total


def next_kernel(places, *refs):
    out = refs[-1]
    for cols in column_tiles(out.shape[1]):
        out[:, cols] = added(refs, places, out.shape[0], cols).astype(out.dtype)


def finish(sends, keeps, own, narrow, after):
    last = len(keeps) - 1
    came = [(exchange(array, 0, narrow), k, k + 1, col) for array, k, col in sends]
    came.append((own[0], last, last + 1, own[1]))
    sent = keeps[-1]
    for k in range(last):
        arrays, places = addends(keeps, came, k)
        sent = pl.pallas_call(
            functools.partial(next_kernel, places),
            out_shape=jax.ShapeDtypeStruct(keeps[k].shape, jnp.bfloat16),
            in_specs=[IN_VMEM] * len(arrays) + [ANYWHERE] * len(after),
            out_specs=IN_VMEM,
            compiler_params=pltpu.CompilerParams(vmem_limit_bytes=2 << 20),
        )(*arrays, *after)
        came.append((exchange(sent, k + 1, narrow), k + 1, len(keeps), 0))
    return sent, addends(keeps, came, len(keeps) - 1)


def target_kernel(places, live, *refs):
    act, out = refs[-2:]
    count = len(places[0])
    for cols in column_tiles(out.shape[1]):
        gate = added(refs[:count], places[0], out.shape[0], cols)
        upper = added(refs[count:], places[1], out.shape[0], cols)
        value = live[:, :1] * (jax.nn.silu(gate) * upper)
        act[:, cols] = value
        out[:, cols] = value.astype(out.dtype)


def target_end(live, gate, upper):
    arrays = gate[0] + upper[0]
    shape = gate[0][0].shape
    return pl.pallas_call(
        functools.partial(target_kernel, (gate[1], upper[1])),
        out_shape=[jax.ShapeDtypeStruct(shape, jnp.float32), jax.ShapeDtypeStruct(shape, jnp.bfloat16)],
        in_specs=[IN_VMEM] * (1 + len(arrays)),
        out_specs=[IN_VMEM] * 2,
        compiler_params=pltpu.CompilerParams(vmem_limit_bytes=4 << 20),
    )(live, *arrays)


def source_kernel(starts, live, weight, *refs):
    terms, out = refs[:-1], refs[-1]
    for cols in column_tiles(out.shape[1]):
        gate = added(terms, starts, out.shape[0], cols)
        out[:, cols] = (live[:, :1] * weight[:, :1]) * jax.nn.silu(gate)


def source_middle(live, weight, own):
    arrays, starts = own
    return pl.pallas_call(
        functools.partial(source_kernel, starts),
        out_shape=jax.ShapeDtypeStruct((live.shape[0], arrays[0].shape[1]), jnp.float32),
        in_specs=[IN_VMEM] * (2 + len(arrays)),
        out_specs=IN_VMEM,
        compiler_params=pltpu.CompilerParams(vmem_limit_bytes=4 << 20),
    )(live, weight, *arrays)


def ratio_kernel(starts, act, gated, *refs):
    terms, out = refs[:-1], refs[-1]
    for cols in column_tiles(out.shape[1]):
        upper = added(terms, starts, out.shape[0], cols)
        out[:, cols] = (act[:, cols] - gated[:, cols] * upper).astype(out.dtype)


def ratio_end(act, gated, own):
    arrays, starts = own
    return pl.pallas_call(
        functools.partial(ratio_kernel, starts),
        out_shape=jax.ShapeDtypeStruct(act.shape, jnp.bfloat16),
        in_specs=[IN_VMEM] * (2 + len(arrays)),
        out_specs=IN_VMEM,
        compiler_params=pltpu.CompilerParams(vmem_limit_bytes=4 << 20),
    )(act, gated, *arrays)


def local(mesh_shape, target_states, source_states, target_gate, target_up, source_gate, source_up, token_ids, lengths, ratio_weight):
    wide, narrow = mesh_shape["wide"], mesh_shape["narrow"]
    target_gate = load(target_gate)
    target_pieces, target_spots = gather_pieces(target_states, "wide", wide, target_gate)
    source_pieces, source_spots = gather_doubling(source_states, "wide", wide)
    width = target_gate.shape[1]

    rows, sends, own, keeps = product(target_pieces, target_gate, narrow, (), spots=target_spots)
    _, up_sends, own, up_keeps = product(rows, target_up, narrow, (keeps[0],), (own,))
    target_own = exchange(own, 0, narrow)
    after = (up_keeps[0], *source_pieces[1:])
    sent, target_g = finish(sends, keeps, (target_own, 0), narrow, after)
    rows, gate_sends, own, gate_keeps = product(source_pieces, source_gate, narrow, (sent,), spots=source_spots)
    after = (gate_keeps[0],)
    sent, target_u = finish(up_sends, up_keeps, (target_own, -width), narrow, after)
    _, sends, own, keeps = product(rows, source_up, narrow, (sent,), (own,))
    sends = resent(sends, (target_g[0][-1],))
    own = exchange(own, 0, narrow)
    sent, source_g = finish(gate_sends, gate_keeps, (own, 0), narrow, (keeps[0], target_own))
    sent, source_u = finish(sends, keeps, (own, -width), narrow, (sent, target_u[0][-1]))
    live, weight = look_up(token_ids, lengths, ratio_weight, (sent,))
    act, target_out = target_end(live, target_g, target_u)
    gated = source_middle(live, weight, source_g)
    ratio_out = ratio_end(act, gated, source_u)
    return (target_out, ratio_out)


def solution(mesh):
    placed = (
        P(("groups", "wide"), "narrow"),
        P(("groups", "wide"), "narrow"),
        P("narrow", "wide"),
        P("narrow", "wide"),
        P("narrow", "wide"),
        P("narrow", "wide"),
        P(("groups", "narrow")),
        P(("groups", "narrow")),
        P(),
    )
    mesh_shape = dict(mesh.shape)

    def body(*args):
        return local(mesh_shape, *args)

    return jax.shard_map(
        body,
        mesh=mesh,
        in_specs=placed,
        out_specs=(P(("groups", "narrow"), "wide"), P(("groups", "narrow"), "wide")),
        check_vma=False,
    )
```

```python
import functools
import math

import jax
import jax.numpy as jnp
from jax import lax
from jax.experimental import pallas as pl
from jax.experimental.pallas import tpu as pltpu
from jax.sharding import PartitionSpec as P

IN_VMEM = pl.BlockSpec(memory_space=pltpu.VMEM)
IN_SMEM = pl.BlockSpec(memory_space=pltpu.SMEM)
ANYWHERE = pl.BlockSpec(memory_space=pl.ANY)
LANES = 128


def in_hbm(array):
    return pltpu.with_memory_space_constraint(array, pltpu.HBM)


def in_vmem(array):
    return pltpu.with_memory_space_constraint(array, pltpu.VMEM)


def pass_kernel(count, *refs):
    for source, dest in zip(refs[:count], refs[-count:]):
        dest[...] = source[...]


def passed(arrays, after):
    return pl.pallas_call(
        functools.partial(pass_kernel, len(arrays)),
        out_shape=[jax.ShapeDtypeStruct(a.shape, a.dtype) for a in arrays],
        in_specs=[IN_VMEM] * len(arrays) + [ANYWHERE] * len(after),
        out_specs=[IN_VMEM] * len(arrays),
        compiler_params=pltpu.CompilerParams(vmem_limit_bytes=2 << 20),
    )(*arrays, *after)


def stack_kernel(*refs):
    row = 0
    for source in refs[:-1]:
        refs[-1][row : row + source.shape[0], :] = source[...]
        row += source.shape[0]


def stacked(arrays):
    rows = sum(a.shape[0] for a in arrays)
    return pl.pallas_call(
        stack_kernel,
        out_shape=jax.ShapeDtypeStruct((rows, arrays[0].shape[1]), arrays[0].dtype),
        in_specs=[IN_VMEM] * len(arrays),
        out_specs=IN_VMEM,
        compiler_params=pltpu.CompilerParams(vmem_limit_bytes=2 << 20),
    )(*arrays)


def gather_pieces(piece, axis, size, relays_after):
    pieces = [piece]
    for offset in range(1, size):
        low = offset & -offset
        source = pieces[offset ^ low]
        if offset != low:
            (source,) = passed([source], (relays_after,))
        pieces.append(lax.ppermute(source, axis, [(i, i ^ low) for i in range(size)]))
    return pieces, [(i, 0) for i in range(size)]


def gather_doubling(piece, axis, size):
    arrays, order, spots, low = [piece], [0], {0: (0, 0)}, size // 2
    while low:
        send = stacked(arrays) if len(arrays) > 1 else piece
        arrays.append(lax.ppermute(send, axis, [(i, i ^ low) for i in range(size)]))
        for place, offset in enumerate(order):
            spots[offset ^ low] = (len(arrays) - 1, place * piece.shape[0])
        order += [offset ^ low for offset in order]
        low //= 2
    return arrays, [spots[offset] for offset in range(size)]


def halving_order(size):
    bits = size.bit_length() - 1
    reverse = [sum(((p >> b) & 1) << (bits - 1 - b) for b in range(bits)) for p in range(size)]
    return reverse[::-1]


def place_rows(arrays, spots, rows, narrow):
    me_wide, me_narrow = lax.axis_index("wide"), lax.axis_index("narrow")
    piece_rows = rows.shape[0] // len(spots)
    block_rows = rows.shape[0] // narrow
    size = math.gcd(piece_rows, block_rows)
    for offset, (index, first) in enumerate(spots):
        for start in range(0, piece_rows, size):
            row = (me_wide ^ offset) * piece_rows + start
            block = (row // block_rows) ^ me_narrow
            place = sum(
                jnp.where(block == known, position, 0)
                for position, known in enumerate(halving_order(narrow))
            )
            spot = pl.multiple_of(place * block_rows + row % block_rows, size)
            rows[pl.ds(spot, size), :] = arrays[index][first + start : first + start + size, :]


def look_up_kernel(slots, ids, lengths, table, *refs):
    live, weight, entries, picked, sem = refs[-5:]
    lookup = pltpu.make_async_copy(table, entries, sem)
    lookup.start()
    for i in range(lengths.shape[0]):
        slot = lax.broadcasted_iota(jnp.int32, (slots, LANES), 0)
        live[i * slots : (i + 1) * slots, :] = (slot < lengths[i]).astype(jnp.float32)
    lookup.wait()

    def pick(i, carry):
        entry = ids[i]
        lane = lax.broadcasted_iota(jnp.int32, (1, LANES), 1)
        row = entries[pl.ds(entry // LANES, 1), :]
        picked[pl.ds(i, 1), :] = jnp.where(lane == entry % LANES, row, 0.0)
        return carry

    lax.fori_loop(0, ids.shape[0], pick, 0)
    weight[...] = jnp.broadcast_to(jnp.sum(picked[...], axis=1, keepdims=True), weight.shape)


def look_up(ids, lengths, table, after):
    table = table.reshape(-1, LANES)
    flag = jax.ShapeDtypeStruct((ids.shape[0], LANES), jnp.float32)
    return pl.pallas_call(
        functools.partial(look_up_kernel, ids.shape[0] // lengths.shape[0]),
        out_shape=[flag, flag],
        in_specs=[IN_SMEM, IN_SMEM] + [ANYWHERE] * (1 + len(after)),
        out_specs=[IN_VMEM, IN_VMEM],
        scratch_shapes=[
            pltpu.VMEM(table.shape, table.dtype),
            pltpu.VMEM(flag.shape, flag.dtype),
            pltpu.SemaphoreType.DMA,
        ],
        compiler_params=pltpu.CompilerParams(vmem_limit_bytes=3 << 20),
    )(*map(in_hbm, (ids, lengths, table)), *after)


def load_kernel(first, matrix, *refs):
    dest, sem = refs[-2:]
    copy = pltpu.make_async_copy(matrix.at[pl.ds(first, dest.shape[0]), :], dest, sem)
    copy.start()
    copy.wait()


def load(matrix, first, rows, after=()):
    return in_vmem(
        pl.pallas_call(
            functools.partial(load_kernel, first),
            out_shape=pltpu.VMEM((rows, matrix.shape[1]), matrix.dtype),
            in_specs=[ANYWHERE] * (1 + len(after)),
            out_specs=IN_VMEM,
            scratch_shapes=[pltpu.SemaphoreType.DMA],
            compiler_params=pltpu.CompilerParams(vmem_limit_bytes=1 << 20),
        )(in_hbm(matrix), *after)
    )


def tile_of(cols):
    for tile in (512, 256, 128):
        if cols % tile == 0:
            return tile
    return cols


def column_tiles(width):
    tile = tile_of(width)
    return [slice(start, start + tile) for start in range(0, width, tile)]


def column_chunks(width):
    tile = tile_of(width)
    first = width // tile // 2 * tile
    return [(0, first), (first, width - first)] if first else [(0, width)]


def product_kernel(pieces, parts, spots, after, narrow, blocks, *refs):
    tokens, matrices = refs[:pieces], refs[pieces : pieces + parts]
    beside, outs = refs[pieces + parts : len(refs) - len(blocks) - (pieces > 1) - after], refs[-len(blocks) :]
    if pieces > 1:
        rows = refs[-len(blocks) - 1]
        place_rows(tokens, spots, rows, narrow)
        tokens = [rows]
    for earlier in beside:
        outs[-1][:, : earlier.shape[1]] = earlier[...]
    for cols in column_tiles(matrices[0].shape[1]):
        total, depth = None, 0
        for matrix in matrices:
            part = tokens[0][:, depth : depth + matrix.shape[0]]
            term = jnp.dot(part, matrix[:, cols], preferred_element_type=jnp.float32)
            total = term if total is None else total + term
            depth += matrix.shape[0]
        for out, (row, col) in zip(outs, blocks):
            if col <= cols.start and cols.stop <= col + out.shape[1]:
                value = total[row : row + out.shape[0]].astype(out.dtype)
                out[:, cols.start - col : cols.stop - col] = value


def part_sizes(total, narrow):
    sizes, left = [], total // 2
    while left > total // narrow:
        left //= 2
        sizes.append(left)
    return sizes + [left]


def product(tokens, matrices, narrow, after, beside=(), spots=(), split=True):
    placing = len(tokens) > 1
    total = sum(t.shape[0] for t in tokens)
    depth, width = tokens[0].shape[1], matrices[0].shape[1]
    sizes = part_sizes(total, narrow)
    sent = [(k, *cols) for k in range(len(sizes) - 1) for cols in (column_chunks(width) if split else [(0, width)])]
    ahead = sum(b.shape[1] for b in beside)
    blocks = [(sum(sizes[:k]), first) for k, first, _ in sent]
    blocks += [(total // 2 + sum(sizes[:k]), 0) for k in range(len(sizes))]
    blocks += [(sum(sizes[:-1]), -ahead)]
    shapes = [(sizes[k], count) for k, _, count in sent] + [(size, width) for size in sizes]
    shapes += [(sizes[-1], ahead + width)]
    found = pl.pallas_call(
        functools.partial(product_kernel, len(tokens), len(matrices), spots, len(after), narrow, blocks),
        out_shape=[jax.ShapeDtypeStruct((total, depth), tokens[0].dtype)] * placing
        + [jax.ShapeDtypeStruct(shape, jnp.bfloat16) for shape in shapes],
        in_specs=[IN_VMEM] * (len(tokens) + len(matrices) + len(beside)) + [ANYWHERE] * len(after),
        out_specs=[IN_VMEM] * (placing + len(shapes)),
        compiler_params=pltpu.CompilerParams(vmem_limit_bytes=4 << 20),
    )(*tokens, *matrices, *beside, *after)
    rows, found = (found[:1], found[1:]) if placing else (tokens, found)
    sends = [(array, k, first) for array, (k, first, _) in zip(found, sent)]
    return rows, sends, found[-1], found[len(sent) : -1]


def resent(sends, after):
    if not sends:
        return sends
    arrays = passed([array for array, _, _ in sends], after)
    return [(array, k, col) for array, (_, k, col) in zip(arrays, sends)]


def exchange(array, step, size):
    return lax.ppermute(array, "narrow", [(i, i ^ (1 << step)) for i in range(size)])


def addends(parts, came, k):
    found = [(parts[k], (0, 0))]
    for array, first, behind, col in came:
        if first <= k < behind:
            found.append((array, (sum(part.shape[0] for part in parts[first:k]), col)))
    return [array for array, _ in found], tuple(place for _, place in found)


def added(refs, places, count, cols):
    total = None
    for ref, (row, col) in zip(refs, places):
        if col <= cols.start and cols.stop <= col + ref.shape[1]:
            term = ref[row : row + count, cols.start - col : cols.stop - col].astype(jnp.float32)
            total = term if total is None else total + term
    return total


def next_kernel(places, *refs):
    out = refs[-1]
    for cols in column_tiles(out.shape[1]):
        out[:, cols] = added(refs, places, out.shape[0], cols).astype(out.dtype)


def finish(sends, keeps, own, narrow, after):
    last = len(keeps) - 1
    came = [(exchange(array, 0, narrow), k, k + 1, col) for array, k, col in sends]
    came.append((own[0], last, last + 1, own[1]))
    sent = keeps[-1]
    for k in range(last):
        arrays, places = addends(keeps, came, k)
        sent = pl.pallas_call(
            functools.partial(next_kernel, places),
            out_shape=jax.ShapeDtypeStruct(keeps[k].shape, jnp.bfloat16),
            in_specs=[IN_VMEM] * len(arrays) + [ANYWHERE] * len(after),
            out_specs=IN_VMEM,
            compiler_params=pltpu.CompilerParams(vmem_limit_bytes=2 << 20),
        )(*arrays, *after)
        came.append((exchange(sent, k + 1, narrow), k + 1, len(keeps), 0))
    return sent, addends(keeps, came, len(keeps) - 1)


def target_kernel(places, live, *refs):
    act, out = refs[-2:]
    count = len(places[0])
    for cols in column_tiles(out.shape[1]):
        gate = added(refs[:count], places[0], out.shape[0], cols)
        upper = added(refs[count:], places[1], out.shape[0], cols)
        value = live[:, :1] * (jax.nn.silu(gate) * upper)
        act[:, cols] = value
        out[:, cols] = value.astype(out.dtype)


def target_end(live, gate, upper):
    arrays = gate[0] + upper[0]
    shape = gate[0][0].shape
    return pl.pallas_call(
        functools.partial(target_kernel, (gate[1], upper[1])),
        out_shape=[jax.ShapeDtypeStruct(shape, jnp.float32), jax.ShapeDtypeStruct(shape, jnp.bfloat16)],
        in_specs=[IN_VMEM] * (1 + len(arrays)),
        out_specs=[IN_VMEM] * 2,
        compiler_params=pltpu.CompilerParams(vmem_limit_bytes=4 << 20),
    )(live, *arrays)


def source_kernel(starts, live, weight, *refs):
    terms, out = refs[:-1], refs[-1]
    for cols in column_tiles(out.shape[1]):
        gate = added(terms, starts, out.shape[0], cols)
        out[:, cols] = (live[:, :1] * weight[:, :1]) * jax.nn.silu(gate)


def source_middle(live, weight, own):
    arrays, starts = own
    return pl.pallas_call(
        functools.partial(source_kernel, starts),
        out_shape=jax.ShapeDtypeStruct((live.shape[0], arrays[0].shape[1]), jnp.float32),
        in_specs=[IN_VMEM] * (2 + len(arrays)),
        out_specs=IN_VMEM,
        compiler_params=pltpu.CompilerParams(vmem_limit_bytes=4 << 20),
    )(live, weight, *arrays)


def ratio_kernel(starts, act, gated, *refs):
    terms, out = refs[:-1], refs[-1]
    for cols in column_tiles(out.shape[1]):
        upper = added(terms, starts, out.shape[0], cols)
        out[:, cols] = (act[:, cols] - gated[:, cols] * upper).astype(out.dtype)


def ratio_end(act, gated, own):
    arrays, starts = own
    return pl.pallas_call(
        functools.partial(ratio_kernel, starts),
        out_shape=jax.ShapeDtypeStruct(act.shape, jnp.bfloat16),
        in_specs=[IN_VMEM] * (2 + len(arrays)),
        out_specs=IN_VMEM,
        compiler_params=pltpu.CompilerParams(vmem_limit_bytes=4 << 20),
    )(act, gated, *arrays)


def local(mesh_shape, target_states, source_states, target_gate, target_up, source_gate, source_up, token_ids, lengths, ratio_weight):
    wide, narrow = mesh_shape["wide"], mesh_shape["narrow"]
    depth, width = target_gate.shape
    half = depth // 2
    gate_top = load(target_gate, 0, half)
    gate_bottom = load(target_gate, half, depth - half, (gate_top,))
    target_pieces, target_spots = gather_pieces(target_states, "wide", wide, gate_bottom)
    (source_states,) = passed([source_states], (gate_top,))
    source_pieces, source_spots = gather_doubling(source_states, "wide", wide)

    gate = (gate_top, gate_bottom)
    rows, sends, own, keeps = product(target_pieces, gate, narrow, (), spots=target_spots)
    after = (keeps[0],)
    _, up_sends, own, up_keeps = product(rows, (in_vmem(target_up),), narrow, after, (own,))
    target_own = exchange(own, 0, narrow)
    sent, target_g = finish(sends, keeps, (target_own, 0), narrow, (up_keeps[0], source_pieces[-1]))
    rows, gate_sends, own, gate_keeps = product(
        source_pieces, (in_vmem(source_gate),), narrow, (sent,), spots=source_spots
    )
    after = (gate_keeps[0],)
    sent, target_u = finish(up_sends, up_keeps, (target_own, -width), narrow, after)
    _, sends, own, keeps = product(rows, (in_vmem(source_up),), narrow, (sent,), (own,))
    sends = resent(sends, (target_g[0][-1],))
    own = exchange(own, 0, narrow)
    sent, source_g = finish(gate_sends, gate_keeps, (own, 0), narrow, (keeps[0], target_own))
    sent, source_u = finish(sends, keeps, (own, -width), narrow, (sent, target_u[0][-1]))
    live, weight = look_up(token_ids, lengths, ratio_weight, (sent,))
    act, target_out = target_end(live, target_g, target_u)
    gated = source_middle(live, weight, source_g)
    ratio_out = ratio_end(act, gated, source_u)
    return (target_out, ratio_out)


def solution(mesh):
    placed = (
        P(("groups", "wide"), "narrow"),
        P(("groups", "wide"), "narrow"),
        P("narrow", "wide"),
        P("narrow", "wide"),
        P("narrow", "wide"),
        P("narrow", "wide"),
        P(("groups", "narrow")),
        P(("groups", "narrow")),
        P(),
    )
    mesh_shape = dict(mesh.shape)

    def body(*args):
        return local(mesh_shape, *args)

    return jax.shard_map(
        body,
        mesh=mesh,
        in_specs=placed,
        out_specs=(P(("groups", "narrow"), "wide"), P(("groups", "narrow"), "wide")),
        check_vma=False,
    )
```

```python
import functools
import math

import jax
import jax.numpy as jnp
from jax import lax
from jax.experimental import pallas as pl
from jax.experimental.pallas import tpu as pltpu
from jax.sharding import PartitionSpec as P

IN_VMEM = pl.BlockSpec(memory_space=pltpu.VMEM)
IN_SMEM = pl.BlockSpec(memory_space=pltpu.SMEM)
ANYWHERE = pl.BlockSpec(memory_space=pl.ANY)
LANES = 128


def in_hbm(array):
    return pltpu.with_memory_space_constraint(array, pltpu.HBM)


def in_vmem(array):
    return pltpu.with_memory_space_constraint(array, pltpu.VMEM)


def pass_kernel(count, *refs):
    for source, dest in zip(refs[:count], refs[-count:]):
        dest[...] = source[...]


def passed(arrays, after):
    return pl.pallas_call(
        functools.partial(pass_kernel, len(arrays)),
        out_shape=[jax.ShapeDtypeStruct(a.shape, a.dtype) for a in arrays],
        in_specs=[IN_VMEM] * len(arrays) + [ANYWHERE] * len(after),
        out_specs=[IN_VMEM] * len(arrays),
        compiler_params=pltpu.CompilerParams(vmem_limit_bytes=2 << 20),
    )(*arrays, *after)


def stack_kernel(*refs):
    row = 0
    for source in refs[:-1]:
        refs[-1][row : row + source.shape[0], :] = source[...]
        row += source.shape[0]


def stacked(arrays):
    rows = sum(a.shape[0] for a in arrays)
    return pl.pallas_call(
        stack_kernel,
        out_shape=jax.ShapeDtypeStruct((rows, arrays[0].shape[1]), arrays[0].dtype),
        in_specs=[IN_VMEM] * len(arrays),
        out_specs=IN_VMEM,
        compiler_params=pltpu.CompilerParams(vmem_limit_bytes=2 << 20),
    )(*arrays)


def gather_pieces(piece, axis, size, relays_after):
    pieces = [piece]
    for offset in range(1, size):
        low = offset & -offset
        source = pieces[offset ^ low]
        if offset != low:
            (source,) = passed([source], (relays_after,))
        pieces.append(lax.ppermute(source, axis, [(i, i ^ low) for i in range(size)]))
    return pieces, [(i, 0) for i in range(size)]


def gather_doubling(piece, axis, size):
    arrays, order, spots, low = [piece], [0], {0: (0, 0)}, size // 2
    while low:
        send = stacked(arrays) if len(arrays) > 1 else piece
        arrays.append(lax.ppermute(send, axis, [(i, i ^ low) for i in range(size)]))
        for place, offset in enumerate(order):
            spots[offset ^ low] = (len(arrays) - 1, place * piece.shape[0])
        order += [offset ^ low for offset in order]
        low //= 2
    return arrays, [spots[offset] for offset in range(size)]


def halving_order(size):
    bits = size.bit_length() - 1
    reverse = [sum(((p >> b) & 1) << (bits - 1 - b) for b in range(bits)) for p in range(size)]
    return reverse[::-1]


def place_rows(arrays, spots, rows, narrow):
    me_wide, me_narrow = lax.axis_index("wide"), lax.axis_index("narrow")
    piece_rows = rows.shape[0] // len(spots)
    block_rows = rows.shape[0] // narrow
    size = math.gcd(piece_rows, block_rows)
    for offset, (index, first) in enumerate(spots):
        for start in range(0, piece_rows, size):
            row = (me_wide ^ offset) * piece_rows + start
            block = (row // block_rows) ^ me_narrow
            place = sum(
                jnp.where(block == known, position, 0)
                for position, known in enumerate(halving_order(narrow))
            )
            spot = pl.multiple_of(place * block_rows + row % block_rows, size)
            rows[pl.ds(spot, size), :] = arrays[index][first + start : first + start + size, :]


def look_up_kernel(slots, ids, lengths, table, *refs):
    live, weight, entries, picked, sem = refs[-5:]
    lookup = pltpu.make_async_copy(table, entries, sem)
    lookup.start()
    for i in range(lengths.shape[0]):
        slot = lax.broadcasted_iota(jnp.int32, (slots, LANES), 0)
        live[i * slots : (i + 1) * slots, :] = (slot < lengths[i]).astype(jnp.float32)
    lookup.wait()

    def pick(i, carry):
        entry = ids[i]
        lane = lax.broadcasted_iota(jnp.int32, (1, LANES), 1)
        row = entries[pl.ds(entry // LANES, 1), :]
        picked[pl.ds(i, 1), :] = jnp.where(lane == entry % LANES, row, 0.0)
        return carry

    lax.fori_loop(0, ids.shape[0], pick, 0)
    weight[...] = jnp.broadcast_to(jnp.sum(picked[...], axis=1, keepdims=True), weight.shape)


def look_up(ids, lengths, table, after):
    table = table.reshape(-1, LANES)
    flag = jax.ShapeDtypeStruct((ids.shape[0], LANES), jnp.float32)
    return pl.pallas_call(
        functools.partial(look_up_kernel, ids.shape[0] // lengths.shape[0]),
        out_shape=[flag, flag],
        in_specs=[IN_SMEM, IN_SMEM] + [ANYWHERE] * (1 + len(after)),
        out_specs=[IN_VMEM, IN_VMEM],
        scratch_shapes=[
            pltpu.VMEM(table.shape, table.dtype),
            pltpu.VMEM(flag.shape, flag.dtype),
            pltpu.SemaphoreType.DMA,
        ],
        compiler_params=pltpu.CompilerParams(vmem_limit_bytes=3 << 20),
    )(*map(in_hbm, (ids, lengths, table)), *after)


def load_kernel(first, matrix, *refs):
    dest, sem = refs[-2:]
    copy = pltpu.make_async_copy(matrix.at[pl.ds(first, dest.shape[0]), :], dest, sem)
    copy.start()
    copy.wait()


def load(matrix, first, rows, after=()):
    return in_vmem(
        pl.pallas_call(
            functools.partial(load_kernel, first),
            out_shape=pltpu.VMEM((rows, matrix.shape[1]), matrix.dtype),
            in_specs=[ANYWHERE] * (1 + len(after)),
            out_specs=IN_VMEM,
            scratch_shapes=[pltpu.SemaphoreType.DMA],
            compiler_params=pltpu.CompilerParams(vmem_limit_bytes=1 << 20),
        )(in_hbm(matrix), *after)
    )


def tile_of(cols):
    for tile in (512, 256, 128):
        if cols % tile == 0:
            return tile
    return cols


def column_tiles(width):
    tile = tile_of(width)
    return [slice(start, start + tile) for start in range(0, width, tile)]


def column_chunks(width):
    tile = tile_of(width)
    first = width // tile // 2 * tile
    return [(0, first), (first, width - first)] if first else [(0, width)]


def product_kernel(pieces, parts, spots, after, narrow, blocks, *refs):
    tokens, matrices = refs[:pieces], refs[pieces : pieces + parts]
    beside, outs = refs[pieces + parts : len(refs) - len(blocks) - (pieces > 1) - after], refs[-len(blocks) :]
    if pieces > 1:
        rows = refs[-len(blocks) - 1]
        place_rows(tokens, spots, rows, narrow)
        tokens = [rows]
    for earlier in beside:
        outs[-1][:, : earlier.shape[1]] = earlier[...]
    for cols in column_tiles(matrices[0].shape[1]):
        total, depth = None, 0
        for matrix in matrices:
            part = tokens[0][:, depth : depth + matrix.shape[0]]
            term = jnp.dot(part, matrix[:, cols], preferred_element_type=jnp.float32)
            total = term if total is None else total + term
            depth += matrix.shape[0]
        for out, (row, col) in zip(outs, blocks):
            if col <= cols.start and cols.stop <= col + out.shape[1]:
                value = total[row : row + out.shape[0]].astype(out.dtype)
                out[:, cols.start - col : cols.stop - col] = value


def part_sizes(total, narrow):
    sizes, left = [], total // 2
    while left > total // narrow:
        left //= 2
        sizes.append(left)
    return sizes + [left]


def product(tokens, matrices, narrow, after, beside=(), spots=(), split=True):
    placing = len(tokens) > 1
    total = sum(t.shape[0] for t in tokens)
    depth, width = tokens[0].shape[1], matrices[0].shape[1]
    sizes = part_sizes(total, narrow)
    sent = [(k, *cols) for k in range(len(sizes) - 1) for cols in (column_chunks(width) if split else [(0, width)])]
    ahead = sum(b.shape[1] for b in beside)
    blocks = [(sum(sizes[:k]), first) for k, first, _ in sent]
    blocks += [(total // 2 + sum(sizes[:k]), 0) for k in range(len(sizes))]
    blocks += [(sum(sizes[:-1]), -ahead)]
    shapes = [(sizes[k], count) for k, _, count in sent] + [(size, width) for size in sizes]
    shapes += [(sizes[-1], ahead + width)]
    found = pl.pallas_call(
        functools.partial(product_kernel, len(tokens), len(matrices), spots, len(after), narrow, blocks),
        out_shape=[jax.ShapeDtypeStruct((total, depth), tokens[0].dtype)] * placing
        + [jax.ShapeDtypeStruct(shape, jnp.bfloat16) for shape in shapes],
        in_specs=[IN_VMEM] * (len(tokens) + len(matrices) + len(beside)) + [ANYWHERE] * len(after),
        out_specs=[IN_VMEM] * (placing + len(shapes)),
        compiler_params=pltpu.CompilerParams(vmem_limit_bytes=4 << 20),
    )(*tokens, *matrices, *beside, *after)
    rows, found = (found[:1], found[1:]) if placing else (tokens, found)
    sends = [(array, k, first) for array, (k, first, _) in zip(found, sent)]
    return rows, sends, found[-1], found[len(sent) : -1]


def resent(sends, after):
    if not sends:
        return sends
    arrays = passed([array for array, _, _ in sends], after)
    return [(array, k, col) for array, (_, k, col) in zip(arrays, sends)]


def exchange(array, step, size):
    return lax.ppermute(array, "narrow", [(i, i ^ (1 << step)) for i in range(size)])


def addends(parts, came, k):
    found = [(parts[k], (0, 0))]
    for array, first, behind, col in came:
        if first <= k < behind:
            found.append((array, (sum(part.shape[0] for part in parts[first:k]), col)))
    return [array for array, _ in found], tuple(place for _, place in found)


def added(refs, places, count, cols):
    total = None
    for ref, (row, col) in zip(refs, places):
        if col <= cols.start and cols.stop <= col + ref.shape[1]:
            term = ref[row : row + count, cols.start - col : cols.stop - col].astype(jnp.float32)
            total = term if total is None else total + term
    return total


def next_kernel(places, *refs):
    out = refs[-1]
    for cols in column_tiles(out.shape[1]):
        out[:, cols] = added(refs, places, out.shape[0], cols).astype(out.dtype)


def finish(sends, keeps, own, narrow, after):
    last = len(keeps) - 1
    came = [(exchange(array, 0, narrow), k, k + 1, col) for array, k, col in sends]
    came.append((own[0], last, last + 1, own[1]))
    sent = keeps[-1]
    for k in range(last):
        arrays, places = addends(keeps, came, k)
        sent = pl.pallas_call(
            functools.partial(next_kernel, places),
            out_shape=jax.ShapeDtypeStruct(keeps[k].shape, jnp.bfloat16),
            in_specs=[IN_VMEM] * len(arrays) + [ANYWHERE] * len(after),
            out_specs=IN_VMEM,
            compiler_params=pltpu.CompilerParams(vmem_limit_bytes=2 << 20),
        )(*arrays, *after)
        came.append((exchange(sent, k + 1, narrow), k + 1, len(keeps), 0))
    return sent, addends(keeps, came, len(keeps) - 1)


def target_kernel(places, live, *refs):
    act, out = refs[-2:]
    count = len(places[0])
    for cols in column_tiles(out.shape[1]):
        gate = added(refs[:count], places[0], out.shape[0], cols)
        upper = added(refs[count:], places[1], out.shape[0], cols)
        value = live[:, :1] * (jax.nn.silu(gate) * upper)
        act[:, cols] = value
        out[:, cols] = value.astype(out.dtype)


def target_end(live, gate, upper):
    arrays = gate[0] + upper[0]
    shape = gate[0][0].shape
    return pl.pallas_call(
        functools.partial(target_kernel, (gate[1], upper[1])),
        out_shape=[jax.ShapeDtypeStruct(shape, jnp.float32), jax.ShapeDtypeStruct(shape, jnp.bfloat16)],
        in_specs=[IN_VMEM] * (1 + len(arrays)),
        out_specs=[IN_VMEM] * 2,
        compiler_params=pltpu.CompilerParams(vmem_limit_bytes=4 << 20),
    )(live, *arrays)


def source_kernel(starts, live, weight, *refs):
    terms, out = refs[:-1], refs[-1]
    for cols in column_tiles(out.shape[1]):
        gate = added(terms, starts, out.shape[0], cols)
        out[:, cols] = (live[:, :1] * weight[:, :1]) * jax.nn.silu(gate)


def source_middle(live, weight, own):
    arrays, starts = own
    return pl.pallas_call(
        functools.partial(source_kernel, starts),
        out_shape=jax.ShapeDtypeStruct((live.shape[0], arrays[0].shape[1]), jnp.float32),
        in_specs=[IN_VMEM] * (2 + len(arrays)),
        out_specs=IN_VMEM,
        compiler_params=pltpu.CompilerParams(vmem_limit_bytes=4 << 20),
    )(live, weight, *arrays)


def ratio_kernel(starts, act, gated, *refs):
    terms, out = refs[:-1], refs[-1]
    for cols in column_tiles(out.shape[1]):
        upper = added(terms, starts, out.shape[0], cols)
        out[:, cols] = (act[:, cols] - gated[:, cols] * upper).astype(out.dtype)


def ratio_end(act, gated, own):
    arrays, starts = own
    return pl.pallas_call(
        functools.partial(ratio_kernel, starts),
        out_shape=jax.ShapeDtypeStruct(act.shape, jnp.bfloat16),
        in_specs=[IN_VMEM] * (2 + len(arrays)),
        out_specs=IN_VMEM,
        compiler_params=pltpu.CompilerParams(vmem_limit_bytes=4 << 20),
    )(act, gated, *arrays)


def local(mesh_shape, target_states, source_states, target_gate, target_up, source_gate, source_up, token_ids, lengths, ratio_weight):
    wide, narrow = mesh_shape["wide"], mesh_shape["narrow"]
    depth, width = target_gate.shape
    half = depth // 2
    gate_top = load(target_gate, 0, half)
    gate_bottom = load(target_gate, half, depth - half, (gate_top,))
    target_pieces, target_spots = gather_pieces(target_states, "wide", wide, gate_bottom)
    (source_states,) = passed([source_states], (gate_top,))
    source_pieces, source_spots = gather_doubling(source_states, "wide", wide)

    gate = (gate_top, gate_bottom)
    rows, sends, own, keeps = product(target_pieces, gate, narrow, (), spots=target_spots)
    after = (keeps[0],)
    _, up_sends, own, up_keeps = product(rows, (in_vmem(target_up),), narrow, after, (own,))
    target_own = exchange(own, 0, narrow)
    sent, target_g = finish(sends, keeps, (target_own, 0), narrow, (up_keeps[0], source_pieces[-1]))
    rows, gate_sends, own, gate_keeps = product(
        source_pieces, (in_vmem(source_gate),), narrow, (sent,), spots=source_spots, split=False
    )
    gate_own = exchange(own, 0, narrow)
    after = (gate_keeps[0],)
    sent, target_u = finish(up_sends, up_keeps, (target_own, -width), narrow, after)
    _, sends, own, keeps = product(rows, (in_vmem(source_up),), narrow, (sent,))
    sends = resent(sends, (target_g[0][-1],))
    own = exchange(own, 0, narrow)
    sent, source_g = finish(gate_sends, gate_keeps, (gate_own, 0), narrow, (keeps[0], target_own))
    sent, source_u = finish(sends, keeps, (own, 0), narrow, (sent, target_u[0][-1]))
    live, weight = look_up(token_ids, lengths, ratio_weight, (sent,))
    act, target_out = target_end(live, target_g, target_u)
    gated = source_middle(live, weight, source_g)
    ratio_out = ratio_end(act, gated, source_u)
    return (target_out, ratio_out)


def solution(mesh):
    placed = (
        P(("groups", "wide"), "narrow"),
        P(("groups", "wide"), "narrow"),
        P("narrow", "wide"),
        P("narrow", "wide"),
        P("narrow", "wide"),
        P("narrow", "wide"),
        P(("groups", "narrow")),
        P(("groups", "narrow")),
        P(),
    )
    mesh_shape = dict(mesh.shape)

    def body(*args):
        return local(mesh_shape, *args)

    return jax.shard_map(
        body,
        mesh=mesh,
        in_specs=placed,
        out_specs=(P(("groups", "narrow"), "wide"), P(("groups", "narrow"), "wide")),
        check_vma=False,
    )
```

```python
import functools
import math

import jax
import jax.numpy as jnp
from jax import lax
from jax.experimental import pallas as pl
from jax.experimental.pallas import tpu as pltpu
from jax.sharding import PartitionSpec as P

IN_VMEM = pl.BlockSpec(memory_space=pltpu.VMEM)
IN_SMEM = pl.BlockSpec(memory_space=pltpu.SMEM)
ANYWHERE = pl.BlockSpec(memory_space=pl.ANY)
LANES = 128


def in_hbm(array):
    return pltpu.with_memory_space_constraint(array, pltpu.HBM)


def in_vmem(array):
    return pltpu.with_memory_space_constraint(array, pltpu.VMEM)


def pass_kernel(count, *refs):
    for source, dest in zip(refs[:count], refs[-count:]):
        dest[...] = source[...]


def passed(arrays, after):
    return pl.pallas_call(
        functools.partial(pass_kernel, len(arrays)),
        out_shape=[jax.ShapeDtypeStruct(a.shape, a.dtype) for a in arrays],
        in_specs=[IN_VMEM] * len(arrays) + [ANYWHERE] * len(after),
        out_specs=[IN_VMEM] * len(arrays),
        compiler_params=pltpu.CompilerParams(vmem_limit_bytes=2 << 20),
    )(*arrays, *after)


def gather_pieces(piece, axis, size, relays_after):
    pieces = [piece]
    for offset in range(1, size):
        low = offset & -offset
        source = pieces[offset ^ low]
        if offset != low:
            (source,) = passed([source], (relays_after,))
        pieces.append(lax.ppermute(source, axis, [(i, i ^ low) for i in range(size)]))
    return pieces, [(i, 0) for i in range(size)]


def gather_chained(piece, axis, size):
    pieces, after = [piece] + [None] * (size - 1), None
    near = [1 << b for b in range(size.bit_length() - 1)]
    for offset in near[::-1] + [o for o in range(size) if o & (o - 1)]:
        low = offset & -offset
        source = pieces[offset ^ low]
        if after is not None and offset == low:
            (source,) = passed([piece], (after,))
        pieces[offset] = lax.ppermute(source, axis, [(i, i ^ low) for i in range(size)])
        after = pieces[offset]
    return pieces, [(i, 0) for i in range(size)]


def halving_order(size):
    bits = size.bit_length() - 1
    reverse = [sum(((p >> b) & 1) << (bits - 1 - b) for b in range(bits)) for p in range(size)]
    return reverse[::-1]


def place_rows(arrays, spots, rows, narrow):
    me_wide, me_narrow = lax.axis_index("wide"), lax.axis_index("narrow")
    piece_rows = rows.shape[0] // len(spots)
    block_rows = rows.shape[0] // narrow
    size = math.gcd(piece_rows, block_rows)
    for offset, (index, first) in enumerate(spots):
        for start in range(0, piece_rows, size):
            row = (me_wide ^ offset) * piece_rows + start
            block = (row // block_rows) ^ me_narrow
            place = sum(
                jnp.where(block == known, position, 0)
                for position, known in enumerate(halving_order(narrow))
            )
            spot = pl.multiple_of(place * block_rows + row % block_rows, size)
            rows[pl.ds(spot, size), :] = arrays[index][first + start : first + start + size, :]


def look_up_kernel(slots, ids, lengths, table, *refs):
    live, weight, entries, picked, sem = refs[-5:]
    lookup = pltpu.make_async_copy(table, entries, sem)
    lookup.start()
    for i in range(lengths.shape[0]):
        slot = lax.broadcasted_iota(jnp.int32, (slots, LANES), 0)
        live[i * slots : (i + 1) * slots, :] = (slot < lengths[i]).astype(jnp.float32)
    lookup.wait()

    def pick(i, carry):
        entry = ids[i]
        lane = lax.broadcasted_iota(jnp.int32, (1, LANES), 1)
        row = entries[pl.ds(entry // LANES, 1), :]
        picked[pl.ds(i, 1), :] = jnp.where(lane == entry % LANES, row, 0.0)
        return carry

    lax.fori_loop(0, ids.shape[0], pick, 0)
    weight[...] = jnp.broadcast_to(jnp.sum(picked[...], axis=1, keepdims=True), weight.shape)


def look_up(ids, lengths, table, after):
    table = table.reshape(-1, LANES)
    flag = jax.ShapeDtypeStruct((ids.shape[0], LANES), jnp.float32)
    return pl.pallas_call(
        functools.partial(look_up_kernel, ids.shape[0] // lengths.shape[0]),
        out_shape=[flag, flag],
        in_specs=[IN_SMEM, IN_SMEM] + [ANYWHERE] * (1 + len(after)),
        out_specs=[IN_VMEM, IN_VMEM],
        scratch_shapes=[
            pltpu.VMEM(table.shape, table.dtype),
            pltpu.VMEM(flag.shape, flag.dtype),
            pltpu.SemaphoreType.DMA,
        ],
        compiler_params=pltpu.CompilerParams(vmem_limit_bytes=3 << 20),
    )(*map(in_hbm, (ids, lengths, table)), *after)


def load_kernel(first, matrix, *refs):
    dest, sem = refs[-2:]
    copy = pltpu.make_async_copy(matrix.at[pl.ds(first, dest.shape[0]), :], dest, sem)
    copy.start()
    copy.wait()


def load(matrix, first, rows, after=()):
    return in_vmem(
        pl.pallas_call(
            functools.partial(load_kernel, first),
            out_shape=pltpu.VMEM((rows, matrix.shape[1]), matrix.dtype),
            in_specs=[ANYWHERE] * (1 + len(after)),
            out_specs=IN_VMEM,
            scratch_shapes=[pltpu.SemaphoreType.DMA],
            compiler_params=pltpu.CompilerParams(vmem_limit_bytes=1 << 20),
        )(in_hbm(matrix), *after)
    )


def tile_of(cols):
    for tile in (512, 256, 128):
        if cols % tile == 0:
            return tile
    return cols


def column_tiles(width):
    tile = tile_of(width)
    return [slice(start, start + tile) for start in range(0, width, tile)]


def column_chunks(width):
    tile = tile_of(width)
    first = width // tile // 2 * tile
    return [(0, first), (first, width - first)] if first else [(0, width)]


def product_kernel(pieces, parts, spots, after, narrow, blocks, *refs):
    tokens, matrices = refs[:pieces], refs[pieces : pieces + parts]
    beside, outs = refs[pieces + parts : len(refs) - len(blocks) - (pieces > 1) - after], refs[-len(blocks) :]
    if pieces > 1:
        rows = refs[-len(blocks) - 1]
        place_rows(tokens, spots, rows, narrow)
        tokens = [rows]
    for earlier in beside:
        outs[-1][:, : earlier.shape[1]] = earlier[...]
    for cols in column_tiles(matrices[0].shape[1]):
        total, depth = None, 0
        for matrix in matrices:
            part = tokens[0][:, depth : depth + matrix.shape[0]]
            term = jnp.dot(part, matrix[:, cols], preferred_element_type=jnp.float32)
            total = term if total is None else total + term
            depth += matrix.shape[0]
        for out, (row, col) in zip(outs, blocks):
            if col <= cols.start and cols.stop <= col + out.shape[1]:
                value = total[row : row + out.shape[0]].astype(out.dtype)
                out[:, cols.start - col : cols.stop - col] = value


def part_sizes(total, narrow):
    sizes, left = [], total // 2
    while left > total // narrow:
        left //= 2
        sizes.append(left)
    return sizes + [left]


def product(tokens, matrices, narrow, after, beside=(), spots=(), split=True):
    placing = len(tokens) > 1
    total = sum(t.shape[0] for t in tokens)
    depth, width = tokens[0].shape[1], matrices[0].shape[1]
    sizes = part_sizes(total, narrow)
    sent = [(k, *cols) for k in range(len(sizes) - 1) for cols in (column_chunks(width) if split else [(0, width)])]
    ahead = sum(b.shape[1] for b in beside)
    blocks = [(sum(sizes[:k]), first) for k, first, _ in sent]
    blocks += [(total // 2 + sum(sizes[:k]), 0) for k in range(len(sizes))]
    blocks += [(sum(sizes[:-1]), -ahead)]
    shapes = [(sizes[k], count) for k, _, count in sent] + [(size, width) for size in sizes]
    shapes += [(sizes[-1], ahead + width)]
    found = pl.pallas_call(
        functools.partial(product_kernel, len(tokens), len(matrices), spots, len(after), narrow, blocks),
        out_shape=[jax.ShapeDtypeStruct((total, depth), tokens[0].dtype)] * placing
        + [jax.ShapeDtypeStruct(shape, jnp.bfloat16) for shape in shapes],
        in_specs=[IN_VMEM] * (len(tokens) + len(matrices) + len(beside)) + [ANYWHERE] * len(after),
        out_specs=[IN_VMEM] * (placing + len(shapes)),
        compiler_params=pltpu.CompilerParams(vmem_limit_bytes=4 << 20),
    )(*tokens, *matrices, *beside, *after)
    rows, found = (found[:1], found[1:]) if placing else (tokens, found)
    sends = [(array, k, first) for array, (k, first, _) in zip(found, sent)]
    return rows, sends, found[-1], found[len(sent) : -1]


def resent(sends, after):
    if not sends:
        return sends
    arrays = passed([array for array, _, _ in sends], after)
    return [(array, k, col) for array, (_, k, col) in zip(arrays, sends)]


def exchange(array, step, size):
    return lax.ppermute(array, "narrow", [(i, i ^ (1 << step)) for i in range(size)])


def addends(parts, came, k):
    found = [(parts[k], (0, 0))]
    for array, first, behind, col in came:
        if first <= k < behind:
            found.append((array, (sum(part.shape[0] for part in parts[first:k]), col)))
    return [array for array, _ in found], tuple(place for _, place in found)


def added(refs, places, count, cols):
    total = None
    for ref, (row, col) in zip(refs, places):
        if col <= cols.start and cols.stop <= col + ref.shape[1]:
            term = ref[row : row + count, cols.start - col : cols.stop - col].astype(jnp.float32)
            total = term if total is None else total + term
    return total


def next_kernel(places, *refs):
    out = refs[-1]
    for cols in column_tiles(out.shape[1]):
        out[:, cols] = added(refs, places, out.shape[0], cols).astype(out.dtype)


def finish(sends, keeps, own, narrow, after):
    last = len(keeps) - 1
    came = [(exchange(array, 0, narrow), k, k + 1, col) for array, k, col in sends]
    came.append((own[0], last, last + 1, own[1]))
    sent = keeps[-1]
    for k in range(last):
        arrays, places = addends(keeps, came, k)
        sent = pl.pallas_call(
            functools.partial(next_kernel, places),
            out_shape=jax.ShapeDtypeStruct(keeps[k].shape, jnp.bfloat16),
            in_specs=[IN_VMEM] * len(arrays) + [ANYWHERE] * len(after),
            out_specs=IN_VMEM,
            compiler_params=pltpu.CompilerParams(vmem_limit_bytes=2 << 20),
        )(*arrays, *after)
        came.append((exchange(sent, k + 1, narrow), k + 1, len(keeps), 0))
    return sent, addends(keeps, came, len(keeps) - 1)


def target_kernel(places, live, *refs):
    act, out = refs[-2:]
    count = len(places[0])
    for cols in column_tiles(out.shape[1]):
        gate = added(refs[:count], places[0], out.shape[0], cols)
        upper = added(refs[count:], places[1], out.shape[0], cols)
        value = live[:, :1] * (jax.nn.silu(gate) * upper)
        act[:, cols] = value
        out[:, cols] = value.astype(out.dtype)


def target_end(live, gate, upper):
    arrays = gate[0] + upper[0]
    shape = gate[0][0].shape
    return pl.pallas_call(
        functools.partial(target_kernel, (gate[1], upper[1])),
        out_shape=[jax.ShapeDtypeStruct(shape, jnp.float32), jax.ShapeDtypeStruct(shape, jnp.bfloat16)],
        in_specs=[IN_VMEM] * (1 + len(arrays)),
        out_specs=[IN_VMEM] * 2,
        compiler_params=pltpu.CompilerParams(vmem_limit_bytes=4 << 20),
    )(live, *arrays)


def source_kernel(starts, live, weight, *refs):
    terms, out = refs[:-1], refs[-1]
    for cols in column_tiles(out.shape[1]):
        gate = added(terms, starts, out.shape[0], cols)
        out[:, cols] = (live[:, :1] * weight[:, :1]) * jax.nn.silu(gate)


def source_middle(live, weight, own):
    arrays, starts = own
    return pl.pallas_call(
        functools.partial(source_kernel, starts),
        out_shape=jax.ShapeDtypeStruct((live.shape[0], arrays[0].shape[1]), jnp.float32),
        in_specs=[IN_VMEM] * (2 + len(arrays)),
        out_specs=IN_VMEM,
        compiler_params=pltpu.CompilerParams(vmem_limit_bytes=4 << 20),
    )(live, weight, *arrays)


def ratio_kernel(starts, act, gated, *refs):
    terms, out = refs[:-1], refs[-1]
    for cols in column_tiles(out.shape[1]):
        upper = added(terms, starts, out.shape[0], cols)
        out[:, cols] = (act[:, cols] - gated[:, cols] * upper).astype(out.dtype)


def ratio_end(act, gated, own):
    arrays, starts = own
    return pl.pallas_call(
        functools.partial(ratio_kernel, starts),
        out_shape=jax.ShapeDtypeStruct(act.shape, jnp.bfloat16),
        in_specs=[IN_VMEM] * (2 + len(arrays)),
        out_specs=IN_VMEM,
        compiler_params=pltpu.CompilerParams(vmem_limit_bytes=4 << 20),
    )(act, gated, *arrays)


def local(mesh_shape, target_states, source_states, target_gate, target_up, source_gate, source_up, token_ids, lengths, ratio_weight):
    wide, narrow = mesh_shape["wide"], mesh_shape["narrow"]
    depth, width = target_gate.shape
    gate = load(target_gate, 0, depth)
    target_pieces, target_spots = gather_pieces(target_states, "wide", wide, gate)
    source_pieces, source_spots = gather_chained(source_states, "wide", wide)

    rows, sends, own, keeps = product(target_pieces, (gate,), narrow, (), spots=target_spots)
    after = (keeps[0],)
    _, up_sends, own, up_keeps = product(rows, (in_vmem(target_up),), narrow, after, (own,))
    target_own = exchange(own, 0, narrow)
    sent, target_g = finish(sends, keeps, (target_own, 0), narrow, (up_keeps[0], *source_pieces[1:]))
    rows, gate_sends, own, gate_keeps = product(
        source_pieces, (in_vmem(source_gate),), narrow, (sent,), spots=source_spots, split=False
    )
    gate_own = exchange(own, 0, narrow)
    after = (gate_keeps[0],)
    sent, target_u = finish(up_sends, up_keeps, (target_own, -width), narrow, after)
    _, sends, own, keeps = product(rows, (in_vmem(source_up),), narrow, (sent,))
    sends = resent(sends, (target_g[0][-1],))
    own = exchange(own, 0, narrow)
    sent, source_g = finish(gate_sends, gate_keeps, (gate_own, 0), narrow, (keeps[0], target_own))
    sent, source_u = finish(sends, keeps, (own, 0), narrow, (sent, target_u[0][-1]))
    live, weight = look_up(token_ids, lengths, ratio_weight, (sent,))
    act, target_out = target_end(live, target_g, target_u)
    gated = source_middle(live, weight, source_g)
    ratio_out = ratio_end(act, gated, source_u)
    return (target_out, ratio_out)


def solution(mesh):
    placed = (
        P(("groups", "wide"), "narrow"),
        P(("groups", "wide"), "narrow"),
        P("narrow", "wide"),
        P("narrow", "wide"),
        P("narrow", "wide"),
        P("narrow", "wide"),
        P(("groups", "narrow")),
        P(("groups", "narrow")),
        P(),
    )
    mesh_shape = dict(mesh.shape)

    def body(*args):
        return local(mesh_shape, *args)

    return jax.shard_map(
        body,
        mesh=mesh,
        in_specs=placed,
        out_specs=(P(("groups", "narrow"), "wide"), P(("groups", "narrow"), "wide")),
        check_vma=False,
    )
```

```python
import functools
import math

import jax
import jax.numpy as jnp
from jax import lax
from jax.experimental import pallas as pl
from jax.experimental.pallas import tpu as pltpu
from jax.sharding import PartitionSpec as P

IN_VMEM = pl.BlockSpec(memory_space=pltpu.VMEM)
IN_SMEM = pl.BlockSpec(memory_space=pltpu.SMEM)
ANYWHERE = pl.BlockSpec(memory_space=pl.ANY)
LANES = 128


def in_hbm(array):
    return pltpu.with_memory_space_constraint(array, pltpu.HBM)


def in_vmem(array):
    return pltpu.with_memory_space_constraint(array, pltpu.VMEM)


def pass_kernel(count, *refs):
    for source, dest in zip(refs[:count], refs[-count:]):
        dest[...] = source[...]


def passed(arrays, after):
    return pl.pallas_call(
        functools.partial(pass_kernel, len(arrays)),
        out_shape=[jax.ShapeDtypeStruct(a.shape, a.dtype) for a in arrays],
        in_specs=[IN_VMEM] * len(arrays) + [ANYWHERE] * len(after),
        out_specs=[IN_VMEM] * len(arrays),
        compiler_params=pltpu.CompilerParams(vmem_limit_bytes=2 << 20),
    )(*arrays, *after)


def stack_kernel(*refs):
    row = 0
    for source in refs[:-1]:
        refs[-1][row : row + source.shape[0], :] = source[...]
        row += source.shape[0]


def stacked(arrays):
    rows = sum(a.shape[0] for a in arrays)
    return pl.pallas_call(
        stack_kernel,
        out_shape=jax.ShapeDtypeStruct((rows, arrays[0].shape[1]), arrays[0].dtype),
        in_specs=[IN_VMEM] * len(arrays),
        out_specs=IN_VMEM,
        compiler_params=pltpu.CompilerParams(vmem_limit_bytes=2 << 20),
    )(*arrays)


def gather_pieces(piece, axis, size, relays_after):
    pieces = [piece] + [None] * (size - 1)
    near = [1 << b for b in range(size.bit_length() - 1)]
    for offset in near[::-1] + [o for o in range(size) if o & (o - 1)]:
        low = offset & -offset
        source = pieces[offset ^ low]
        if offset != low:
            (source,) = passed([source], (relays_after, pieces[low]))
        pieces[offset] = lax.ppermute(source, axis, [(i, i ^ low) for i in range(size)])
    return pieces, [(i, 0) for i in range(size)]


def gather_doubling(piece, axis, size):
    arrays, order, spots, low = [piece], [0], {0: (0, 0)}, size // 2
    while low:
        send = stacked(arrays) if len(arrays) > 1 else piece
        arrays.append(lax.ppermute(send, axis, [(i, i ^ low) for i in range(size)]))
        for place, offset in enumerate(order):
            spots[offset ^ low] = (len(arrays) - 1, place * piece.shape[0])
        order += [offset ^ low for offset in order]
        low //= 2
    return arrays, [spots[offset] for offset in range(size)]


def halving_order(size):
    bits = size.bit_length() - 1
    reverse = [sum(((p >> b) & 1) << (bits - 1 - b) for b in range(bits)) for p in range(size)]
    return reverse[::-1]


def place_rows(arrays, spots, rows, narrow):
    me_wide, me_narrow = lax.axis_index("wide"), lax.axis_index("narrow")
    piece_rows = rows.shape[0] // len(spots)
    block_rows = rows.shape[0] // narrow
    size = math.gcd(piece_rows, block_rows)
    for offset, (index, first) in enumerate(spots):
        for start in range(0, piece_rows, size):
            row = (me_wide ^ offset) * piece_rows + start
            block = (row // block_rows) ^ me_narrow
            place = sum(
                jnp.where(block == known, position, 0)
                for position, known in enumerate(halving_order(narrow))
            )
            spot = pl.multiple_of(place * block_rows + row % block_rows, size)
            rows[pl.ds(spot, size), :] = arrays[index][first + start : first + start + size, :]


def look_up_kernel(slots, ids, lengths, table, *refs):
    live, weight, entries, picked, sem = refs[-5:]
    lookup = pltpu.make_async_copy(table, entries, sem)
    lookup.start()
    for i in range(lengths.shape[0]):
        slot = lax.broadcasted_iota(jnp.int32, (slots, LANES), 0)
        live[i * slots : (i + 1) * slots, :] = (slot < lengths[i]).astype(jnp.float32)
    lookup.wait()

    def pick(i, carry):
        entry = ids[i]
        lane = lax.broadcasted_iota(jnp.int32, (1, LANES), 1)
        row = entries[pl.ds(entry // LANES, 1), :]
        picked[pl.ds(i, 1), :] = jnp.where(lane == entry % LANES, row, 0.0)
        return carry

    lax.fori_loop(0, ids.shape[0], pick, 0)
    weight[...] = jnp.broadcast_to(jnp.sum(picked[...], axis=1, keepdims=True), weight.shape)


def look_up(ids, lengths, table, after):
    table = table.reshape(-1, LANES)
    flag = jax.ShapeDtypeStruct((ids.shape[0], LANES), jnp.float32)
    return pl.pallas_call(
        functools.partial(look_up_kernel, ids.shape[0] // lengths.shape[0]),
        out_shape=[flag, flag],
        in_specs=[IN_SMEM, IN_SMEM] + [ANYWHERE] * (1 + len(after)),
        out_specs=[IN_VMEM, IN_VMEM],
        scratch_shapes=[
            pltpu.VMEM(table.shape, table.dtype),
            pltpu.VMEM(flag.shape, flag.dtype),
            pltpu.SemaphoreType.DMA,
        ],
        compiler_params=pltpu.CompilerParams(vmem_limit_bytes=3 << 20),
    )(*map(in_hbm, (ids, lengths, table)), *after)


def load_kernel(first, matrix, *refs):
    dest, sem = refs[-2:]
    copy = pltpu.make_async_copy(matrix.at[pl.ds(first, dest.shape[0]), :], dest, sem)
    copy.start()
    copy.wait()


def load(matrix, first, rows, after=()):
    return in_vmem(
        pl.pallas_call(
            functools.partial(load_kernel, first),
            out_shape=pltpu.VMEM((rows, matrix.shape[1]), matrix.dtype),
            in_specs=[ANYWHERE] * (1 + len(after)),
            out_specs=IN_VMEM,
            scratch_shapes=[pltpu.SemaphoreType.DMA],
            compiler_params=pltpu.CompilerParams(vmem_limit_bytes=1 << 20),
        )(in_hbm(matrix), *after)
    )


def tile_of(cols):
    for tile in (512, 256, 128):
        if cols % tile == 0:
            return tile
    return cols


def column_tiles(width):
    tile = tile_of(width)
    return [slice(start, start + tile) for start in range(0, width, tile)]


def column_chunks(width):
    tile = tile_of(width)
    first = width // tile // 2 * tile
    return [(0, first), (first, width - first)] if first else [(0, width)]


def product_kernel(pieces, parts, spots, after, narrow, blocks, *refs):
    tokens, matrices = refs[:pieces], refs[pieces : pieces + parts]
    beside, outs = refs[pieces + parts : len(refs) - len(blocks) - (pieces > 1) - after], refs[-len(blocks) :]
    if pieces > 1:
        rows = refs[-len(blocks) - 1]
        place_rows(tokens, spots, rows, narrow)
        tokens = [rows]
    for earlier in beside:
        outs[-1][:, : earlier.shape[1]] = earlier[...]
    for cols in column_tiles(matrices[0].shape[1]):
        total, depth = None, 0
        for matrix in matrices:
            part = tokens[0][:, depth : depth + matrix.shape[0]]
            term = jnp.dot(part, matrix[:, cols], preferred_element_type=jnp.float32)
            total = term if total is None else total + term
            depth += matrix.shape[0]
        for out, (row, col) in zip(outs, blocks):
            if col <= cols.start and cols.stop <= col + out.shape[1]:
                value = total[row : row + out.shape[0]].astype(out.dtype)
                out[:, cols.start - col : cols.stop - col] = value


def part_sizes(total, narrow):
    sizes, left = [], total // 2
    while left > total // narrow:
        left //= 2
        sizes.append(left)
    return sizes + [left]


def product(tokens, matrices, narrow, after, beside=(), spots=(), split=True):
    placing = len(tokens) > 1
    total = sum(t.shape[0] for t in tokens)
    depth, width = tokens[0].shape[1], matrices[0].shape[1]
    sizes = part_sizes(total, narrow)
    sent = [(k, *cols) for k in range(len(sizes) - 1) for cols in (column_chunks(width) if split else [(0, width)])]
    ahead = sum(b.shape[1] for b in beside)
    blocks = [(sum(sizes[:k]), first) for k, first, _ in sent]
    blocks += [(total // 2 + sum(sizes[:k]), 0) for k in range(len(sizes))]
    blocks += [(sum(sizes[:-1]), -ahead)]
    shapes = [(sizes[k], count) for k, _, count in sent] + [(size, width) for size in sizes]
    shapes += [(sizes[-1], ahead + width)]
    found = pl.pallas_call(
        functools.partial(product_kernel, len(tokens), len(matrices), spots, len(after), narrow, blocks),
        out_shape=[jax.ShapeDtypeStruct((total, depth), tokens[0].dtype)] * placing
        + [jax.ShapeDtypeStruct(shape, jnp.bfloat16) for shape in shapes],
        in_specs=[IN_VMEM] * (len(tokens) + len(matrices) + len(beside)) + [ANYWHERE] * len(after),
        out_specs=[IN_VMEM] * (placing + len(shapes)),
        compiler_params=pltpu.CompilerParams(vmem_limit_bytes=4 << 20),
    )(*tokens, *matrices, *beside, *after)
    rows, found = (found[:1], found[1:]) if placing else (tokens, found)
    sends = [(array, k, first) for array, (k, first, _) in zip(found, sent)]
    return rows, sends, found[-1], found[len(sent) : -1]


def resent(sends, after):
    if not sends:
        return sends
    arrays = passed([array for array, _, _ in sends], after)
    return [(array, k, col) for array, (_, k, col) in zip(arrays, sends)]


def exchange(array, step, size):
    return lax.ppermute(array, "narrow", [(i, i ^ (1 << step)) for i in range(size)])


def addends(parts, came, k):
    found = [(parts[k], (0, 0))]
    for array, first, behind, col in came:
        if first <= k < behind:
            found.append((array, (sum(part.shape[0] for part in parts[first:k]), col)))
    return [array for array, _ in found], tuple(place for _, place in found)


def added(refs, places, count, cols):
    total = None
    for ref, (row, col) in zip(refs, places):
        if col <= cols.start and cols.stop <= col + ref.shape[1]:
            term = ref[row : row + count, cols.start - col : cols.stop - col].astype(jnp.float32)
            total = term if total is None else total + term
    return total


def next_kernel(places, *refs):
    out = refs[-1]
    for cols in column_tiles(out.shape[1]):
        out[:, cols] = added(refs, places, out.shape[0], cols).astype(out.dtype)


def finish(sends, keeps, own, narrow, after):
    last = len(keeps) - 1
    came = [(exchange(array, 0, narrow), k, k + 1, col) for array, k, col in sends]
    came.append((own[0], last, last + 1, own[1]))
    sent = keeps[-1]
    for k in range(last):
        arrays, places = addends(keeps, came, k)
        sent = pl.pallas_call(
            functools.partial(next_kernel, places),
            out_shape=jax.ShapeDtypeStruct(keeps[k].shape, jnp.bfloat16),
            in_specs=[IN_VMEM] * len(arrays) + [ANYWHERE] * len(after),
            out_specs=IN_VMEM,
            compiler_params=pltpu.CompilerParams(vmem_limit_bytes=2 << 20),
        )(*arrays, *after)
        came.append((exchange(sent, k + 1, narrow), k + 1, len(keeps), 0))
    return sent, addends(keeps, came, len(keeps) - 1)


def target_kernel(places, live, *refs):
    act, out = refs[-2:]
    count = len(places[0])
    for cols in column_tiles(out.shape[1]):
        gate = added(refs[:count], places[0], out.shape[0], cols)
        upper = added(refs[count:], places[1], out.shape[0], cols)
        value = live[:, :1] * (jax.nn.silu(gate) * upper)
        act[:, cols] = value
        out[:, cols] = value.astype(out.dtype)


def target_end(live, gate, upper):
    arrays = gate[0] + upper[0]
    shape = gate[0][0].shape
    return pl.pallas_call(
        functools.partial(target_kernel, (gate[1], upper[1])),
        out_shape=[jax.ShapeDtypeStruct(shape, jnp.float32), jax.ShapeDtypeStruct(shape, jnp.bfloat16)],
        in_specs=[IN_VMEM] * (1 + len(arrays)),
        out_specs=[IN_VMEM] * 2,
        compiler_params=pltpu.CompilerParams(vmem_limit_bytes=4 << 20),
    )(live, *arrays)


def source_kernel(starts, live, weight, *refs):
    terms, out = refs[:-1], refs[-1]
    for cols in column_tiles(out.shape[1]):
        gate = added(terms, starts, out.shape[0], cols)
        out[:, cols] = (live[:, :1] * weight[:, :1]) * jax.nn.silu(gate)


def source_middle(live, weight, own):
    arrays, starts = own
    return pl.pallas_call(
        functools.partial(source_kernel, starts),
        out_shape=jax.ShapeDtypeStruct((live.shape[0], arrays[0].shape[1]), jnp.float32),
        in_specs=[IN_VMEM] * (2 + len(arrays)),
        out_specs=IN_VMEM,
        compiler_params=pltpu.CompilerParams(vmem_limit_bytes=4 << 20),
    )(live, weight, *arrays)


def ratio_kernel(starts, act, gated, *refs):
    terms, out = refs[:-1], refs[-1]
    for cols in column_tiles(out.shape[1]):
        upper = added(terms, starts, out.shape[0], cols)
        out[:, cols] = (act[:, cols] - gated[:, cols] * upper).astype(out.dtype)


def ratio_end(act, gated, own):
    arrays, starts = own
    return pl.pallas_call(
        functools.partial(ratio_kernel, starts),
        out_shape=jax.ShapeDtypeStruct(act.shape, jnp.bfloat16),
        in_specs=[IN_VMEM] * (2 + len(arrays)),
        out_specs=IN_VMEM,
        compiler_params=pltpu.CompilerParams(vmem_limit_bytes=4 << 20),
    )(act, gated, *arrays)


def local(mesh_shape, target_states, source_states, target_gate, target_up, source_gate, source_up, token_ids, lengths, ratio_weight):
    wide, narrow = mesh_shape["wide"], mesh_shape["narrow"]
    depth, width = target_gate.shape
    gate = load(target_gate, 0, depth)
    target_pieces, target_spots = gather_pieces(target_states, "wide", wide, gate)
    source_pieces, source_spots = gather_doubling(source_states, "wide", wide)

    rows, sends, own, keeps = product(target_pieces, (gate,), narrow, (), spots=target_spots)
    after = (keeps[0],)
    _, up_sends, own, up_keeps = product(rows, (in_vmem(target_up),), narrow, after, (own,))
    target_own = exchange(own, 0, narrow)
    sent, target_g = finish(sends, keeps, (target_own, 0), narrow, (up_keeps[0], source_pieces[-1]))
    rows, gate_sends, own, gate_keeps = product(
        source_pieces, (in_vmem(source_gate),), narrow, (sent,), spots=source_spots, split=False
    )
    gate_own = exchange(own, 0, narrow)
    after = (gate_keeps[0],)
    sent, target_u = finish(up_sends, up_keeps, (target_own, -width), narrow, after)
    _, sends, own, keeps = product(rows, (in_vmem(source_up),), narrow, (sent,))
    sends = resent(sends, (target_g[0][-1],))
    own = exchange(own, 0, narrow)
    sent, source_g = finish(gate_sends, gate_keeps, (gate_own, 0), narrow, (keeps[0], target_own))
    sent, source_u = finish(sends, keeps, (own, 0), narrow, (sent, target_u[0][-1]))
    live, weight = look_up(token_ids, lengths, ratio_weight, (sent,))
    act, target_out = target_end(live, target_g, target_u)
    gated = source_middle(live, weight, source_g)
    ratio_out = ratio_end(act, gated, source_u)
    return (target_out, ratio_out)


def solution(mesh):
    placed = (
        P(("groups", "wide"), "narrow"),
        P(("groups", "wide"), "narrow"),
        P("narrow", "wide"),
        P("narrow", "wide"),
        P("narrow", "wide"),
        P("narrow", "wide"),
        P(("groups", "narrow")),
        P(("groups", "narrow")),
        P(),
    )
    mesh_shape = dict(mesh.shape)

    def body(*args):
        return local(mesh_shape, *args)

    return jax.shard_map(
        body,
        mesh=mesh,
        in_specs=placed,
        out_specs=(P(("groups", "narrow"), "wide"), P(("groups", "narrow"), "wide")),
        check_vma=False,
    )
```

```python
import functools
import math

import jax
import jax.numpy as jnp
from jax import lax
from jax.experimental import pallas as pl
from jax.experimental.pallas import tpu as pltpu
from jax.sharding import PartitionSpec as P

IN_VMEM = pl.BlockSpec(memory_space=pltpu.VMEM)
IN_SMEM = pl.BlockSpec(memory_space=pltpu.SMEM)
ANYWHERE = pl.BlockSpec(memory_space=pl.ANY)
LANES = 128


def in_hbm(array):
    return pltpu.with_memory_space_constraint(array, pltpu.HBM)


def in_vmem(array):
    return pltpu.with_memory_space_constraint(array, pltpu.VMEM)


def pass_kernel(count, *refs):
    for source, dest in zip(refs[:count], refs[-count:]):
        dest[...] = source[...]


def passed(arrays, after):
    return pl.pallas_call(
        functools.partial(pass_kernel, len(arrays)),
        out_shape=[jax.ShapeDtypeStruct(a.shape, a.dtype) for a in arrays],
        in_specs=[IN_VMEM] * len(arrays) + [ANYWHERE] * len(after),
        out_specs=[IN_VMEM] * len(arrays),
        compiler_params=pltpu.CompilerParams(vmem_limit_bytes=2 << 20),
    )(*arrays, *after)


def gather_pieces(piece, axis, size, relays_after):
    pieces = [piece]
    for offset in range(1, size):
        low = offset & -offset
        source = pieces[offset ^ low]
        if offset != low:
            (source,) = passed([source], (relays_after,))
        pieces.append(lax.ppermute(source, axis, [(i, i ^ low) for i in range(size)]))
    return pieces, [(i, 0) for i in range(size)]


def gather_chained(piece, axis, size):
    pieces, after = [piece] + [None] * (size - 1), None
    near = [1 << b for b in range(size.bit_length() - 1)]
    for offset in near[::-1] + [o for o in range(size) if o & (o - 1)]:
        low = offset & -offset
        source = pieces[offset ^ low]
        if after is not None and offset == low:
            (source,) = passed([piece], (after,))
        pieces[offset] = lax.ppermute(source, axis, [(i, i ^ low) for i in range(size)])
        after = pieces[offset]
    return pieces, [(i, 0) for i in range(size)]


def halving_order(size):
    bits = size.bit_length() - 1
    reverse = [sum(((p >> b) & 1) << (bits - 1 - b) for b in range(bits)) for p in range(size)]
    return reverse[::-1]


def place_rows(arrays, spots, rows, narrow):
    me_wide, me_narrow = lax.axis_index("wide"), lax.axis_index("narrow")
    piece_rows = rows.shape[0] // len(spots)
    block_rows = rows.shape[0] // narrow
    size = math.gcd(piece_rows, block_rows)
    for offset, (index, first) in enumerate(spots):
        for start in range(0, piece_rows, size):
            row = (me_wide ^ offset) * piece_rows + start
            block = (row // block_rows) ^ me_narrow
            place = sum(
                jnp.where(block == known, position, 0)
                for position, known in enumerate(halving_order(narrow))
            )
            spot = pl.multiple_of(place * block_rows + row % block_rows, size)
            rows[pl.ds(spot, size), :] = arrays[index][first + start : first + start + size, :]


def look_up_kernel(slots, ids, lengths, table, *refs):
    live, weight, entries, picked, sem = refs[-5:]
    lookup = pltpu.make_async_copy(table, entries, sem)
    lookup.start()
    for i in range(lengths.shape[0]):
        slot = lax.broadcasted_iota(jnp.int32, (slots, LANES), 0)
        live[i * slots : (i + 1) * slots, :] = (slot < lengths[i]).astype(jnp.float32)
    lookup.wait()

    def pick(i, carry):
        entry = ids[i]
        lane = lax.broadcasted_iota(jnp.int32, (1, LANES), 1)
        row = entries[pl.ds(entry // LANES, 1), :]
        picked[pl.ds(i, 1), :] = jnp.where(lane == entry % LANES, row, 0.0)
        return carry

    lax.fori_loop(0, ids.shape[0], pick, 0)
    weight[...] = jnp.broadcast_to(jnp.sum(picked[...], axis=1, keepdims=True), weight.shape)


def look_up(ids, lengths, table, after):
    table = table.reshape(-1, LANES)
    flag = jax.ShapeDtypeStruct((ids.shape[0], LANES), jnp.float32)
    return pl.pallas_call(
        functools.partial(look_up_kernel, ids.shape[0] // lengths.shape[0]),
        out_shape=[flag, flag],
        in_specs=[IN_SMEM, IN_SMEM] + [ANYWHERE] * (1 + len(after)),
        out_specs=[IN_VMEM, IN_VMEM],
        scratch_shapes=[
            pltpu.VMEM(table.shape, table.dtype),
            pltpu.VMEM(flag.shape, flag.dtype),
            pltpu.SemaphoreType.DMA,
        ],
        compiler_params=pltpu.CompilerParams(vmem_limit_bytes=3 << 20),
    )(*map(in_hbm, (ids, lengths, table)), *after)


def load_kernel(first, matrix, *refs):
    dest, sem = refs[-2:]
    copy = pltpu.make_async_copy(matrix.at[pl.ds(first, dest.shape[0]), :], dest, sem)
    copy.start()
    copy.wait()


def load(matrix, first, rows, after=()):
    return in_vmem(
        pl.pallas_call(
            functools.partial(load_kernel, first),
            out_shape=pltpu.VMEM((rows, matrix.shape[1]), matrix.dtype),
            in_specs=[ANYWHERE] * (1 + len(after)),
            out_specs=IN_VMEM,
            scratch_shapes=[pltpu.SemaphoreType.DMA],
            compiler_params=pltpu.CompilerParams(vmem_limit_bytes=1 << 20),
        )(in_hbm(matrix), *after)
    )


def tile_of(cols):
    for tile in (512, 256, 128):
        if cols % tile == 0:
            return tile
    return cols


def column_tiles(width):
    tile = tile_of(width)
    return [slice(start, start + tile) for start in range(0, width, tile)]


def column_chunks(width):
    tile = tile_of(width)
    first = width // tile // 2 * tile
    return [(0, first), (first, width - first)] if first else [(0, width)]


def product_kernel(pieces, parts, spots, after, narrow, blocks, *refs):
    tokens, matrices = refs[:pieces], refs[pieces : pieces + parts]
    beside, outs = refs[pieces + parts : len(refs) - len(blocks) - (pieces > 1) - after], refs[-len(blocks) :]
    if pieces > 1:
        rows = refs[-len(blocks) - 1]
        place_rows(tokens, spots, rows, narrow)
        tokens = [rows]
    for earlier in beside:
        outs[-1][:, : earlier.shape[1]] = earlier[...]
    for cols in column_tiles(matrices[0].shape[1]):
        total, depth = None, 0
        for matrix in matrices:
            part = tokens[0][:, depth : depth + matrix.shape[0]]
            term = jnp.dot(part, matrix[:, cols], preferred_element_type=jnp.float32)
            total = term if total is None else total + term
            depth += matrix.shape[0]
        for out, (row, col) in zip(outs, blocks):
            if col <= cols.start and cols.stop <= col + out.shape[1]:
                value = total[row : row + out.shape[0]].astype(out.dtype)
                out[:, cols.start - col : cols.stop - col] = value


def part_sizes(total, narrow):
    sizes, left = [], total // 2
    while left > total // narrow:
        left //= 2
        sizes.append(left)
    return sizes + [left]


def product(tokens, matrices, narrow, after, beside=(), spots=(), split=True):
    placing = len(tokens) > 1
    total = sum(t.shape[0] for t in tokens)
    depth, width = tokens[0].shape[1], matrices[0].shape[1]
    sizes = part_sizes(total, narrow)
    sent = [(k, *cols) for k in range(len(sizes) - 1) for cols in (column_chunks(width) if split else [(0, width)])]
    ahead = sum(b.shape[1] for b in beside)
    blocks = [(sum(sizes[:k]), first) for k, first, _ in sent]
    blocks += [(total // 2 + sum(sizes[:k]), 0) for k in range(len(sizes))]
    blocks += [(sum(sizes[:-1]), -ahead)]
    shapes = [(sizes[k], count) for k, _, count in sent] + [(size, width) for size in sizes]
    shapes += [(sizes[-1], ahead + width)]
    found = pl.pallas_call(
        functools.partial(product_kernel, len(tokens), len(matrices), spots, len(after), narrow, blocks),
        out_shape=[jax.ShapeDtypeStruct((total, depth), tokens[0].dtype)] * placing
        + [jax.ShapeDtypeStruct(shape, jnp.bfloat16) for shape in shapes],
        in_specs=[IN_VMEM] * (len(tokens) + len(matrices) + len(beside)) + [ANYWHERE] * len(after),
        out_specs=[IN_VMEM] * (placing + len(shapes)),
        compiler_params=pltpu.CompilerParams(vmem_limit_bytes=4 << 20),
    )(*tokens, *matrices, *beside, *after)
    rows, found = (found[:1], found[1:]) if placing else (tokens, found)
    sends = [(array, k, first) for array, (k, first, _) in zip(found, sent)]
    return rows, sends, found[-1], found[len(sent) : -1]


def resent(sends, after):
    if not sends:
        return sends
    arrays = passed([array for array, _, _ in sends], after)
    return [(array, k, col) for array, (_, k, col) in zip(arrays, sends)]


def exchange(array, step, size):
    return lax.ppermute(array, "narrow", [(i, i ^ (1 << step)) for i in range(size)])


def addends(parts, came, k):
    found = [(parts[k], (0, 0))]
    for array, first, behind, col in came:
        if first <= k < behind:
            found.append((array, (sum(part.shape[0] for part in parts[first:k]), col)))
    return [array for array, _ in found], tuple(place for _, place in found)


def added(refs, places, count, cols):
    total = None
    for ref, (row, col) in zip(refs, places):
        if col <= cols.start and cols.stop <= col + ref.shape[1]:
            term = ref[row : row + count, cols.start - col : cols.stop - col].astype(jnp.float32)
            total = term if total is None else total + term
    return total


def next_kernel(places, *refs):
    out = refs[-1]
    for cols in column_tiles(out.shape[1]):
        out[:, cols] = added(refs, places, out.shape[0], cols).astype(out.dtype)


def finish(sends, keeps, own, narrow, after):
    last = len(keeps) - 1
    came = [(exchange(array, 0, narrow), k, k + 1, col) for array, k, col in sends]
    came.append((own[0], last, last + 1, own[1]))
    sent = keeps[-1]
    for k in range(last):
        arrays, places = addends(keeps, came, k)
        sent = pl.pallas_call(
            functools.partial(next_kernel, places),
            out_shape=jax.ShapeDtypeStruct(keeps[k].shape, jnp.bfloat16),
            in_specs=[IN_VMEM] * len(arrays) + [ANYWHERE] * len(after),
            out_specs=IN_VMEM,
            compiler_params=pltpu.CompilerParams(vmem_limit_bytes=2 << 20),
        )(*arrays, *after)
        came.append((exchange(sent, k + 1, narrow), k + 1, len(keeps), 0))
    return sent, addends(keeps, came, len(keeps) - 1)


def target_kernel(places, live, *refs):
    act, out = refs[-2:]
    count = len(places[0])
    for cols in column_tiles(out.shape[1]):
        gate = added(refs[:count], places[0], out.shape[0], cols)
        upper = added(refs[count:], places[1], out.shape[0], cols)
        value = live[:, :1] * (jax.nn.silu(gate) * upper)
        act[:, cols] = value
        out[:, cols] = value.astype(out.dtype)


def target_end(live, gate, upper):
    arrays = gate[0] + upper[0]
    shape = gate[0][0].shape
    return pl.pallas_call(
        functools.partial(target_kernel, (gate[1], upper[1])),
        out_shape=[jax.ShapeDtypeStruct(shape, jnp.float32), jax.ShapeDtypeStruct(shape, jnp.bfloat16)],
        in_specs=[IN_VMEM] * (1 + len(arrays)),
        out_specs=[IN_VMEM] * 2,
        compiler_params=pltpu.CompilerParams(vmem_limit_bytes=4 << 20),
    )(live, *arrays)


def source_kernel(starts, live, weight, *refs):
    terms, out = refs[:-1], refs[-1]
    for cols in column_tiles(out.shape[1]):
        gate = added(terms, starts, out.shape[0], cols)
        out[:, cols] = (live[:, :1] * weight[:, :1]) * jax.nn.silu(gate)


def source_middle(live, weight, own):
    arrays, starts = own
    return pl.pallas_call(
        functools.partial(source_kernel, starts),
        out_shape=jax.ShapeDtypeStruct((live.shape[0], arrays[0].shape[1]), jnp.float32),
        in_specs=[IN_VMEM] * (2 + len(arrays)),
        out_specs=IN_VMEM,
        compiler_params=pltpu.CompilerParams(vmem_limit_bytes=4 << 20),
    )(live, weight, *arrays)


def ratio_kernel(starts, act, gated, *refs):
    terms, out = refs[:-1], refs[-1]
    for cols in column_tiles(out.shape[1]):
        upper = added(terms, starts, out.shape[0], cols)
        out[:, cols] = (act[:, cols] - gated[:, cols] * upper).astype(out.dtype)


def ratio_end(act, gated, own):
    arrays, starts = own
    return pl.pallas_call(
        functools.partial(ratio_kernel, starts),
        out_shape=jax.ShapeDtypeStruct(act.shape, jnp.bfloat16),
        in_specs=[IN_VMEM] * (2 + len(arrays)),
        out_specs=IN_VMEM,
        compiler_params=pltpu.CompilerParams(vmem_limit_bytes=4 << 20),
    )(act, gated, *arrays)


def local(mesh_shape, target_states, source_states, target_gate, target_up, source_gate, source_up, token_ids, lengths, ratio_weight):
    wide, narrow = mesh_shape["wide"], mesh_shape["narrow"]
    depth, width = target_gate.shape
    gate = load(target_gate, 0, depth)
    target_pieces, target_spots = gather_pieces(target_states, "wide", wide, gate)
    source_pieces, source_spots = gather_chained(source_states, "wide", wide)

    rows, sends, own, keeps = product(target_pieces, (gate,), narrow, (), spots=target_spots)
    after = (keeps[0],)
    target_own = exchange(own, 0, narrow)
    _, up_sends, own, up_keeps = product(rows, (in_vmem(target_up),), narrow, after)
    up_own = exchange(own, 0, narrow)
    sent, target_g = finish(sends, keeps, (target_own, 0), narrow, (up_keeps[0], *source_pieces[1:]))
    rows, gate_sends, own, gate_keeps = product(
        source_pieces, (in_vmem(source_gate),), narrow, (sent,), spots=source_spots, split=False
    )
    gate_own = exchange(own, 0, narrow)
    after = (gate_keeps[0],)
    sent, target_u = finish(up_sends, up_keeps, (up_own, 0), narrow, after)
    _, sends, own, keeps = product(rows, (in_vmem(source_up),), narrow, (sent,))
    sends = resent(sends, (target_g[0][-1],))
    own = exchange(own, 0, narrow)
    sent, source_g = finish(gate_sends, gate_keeps, (gate_own, 0), narrow, (keeps[0], target_own, up_own))
    sent, source_u = finish(sends, keeps, (own, 0), narrow, (sent, target_u[0][-1]))
    live, weight = look_up(token_ids, lengths, ratio_weight, (sent,))
    act, target_out = target_end(live, target_g, target_u)
    gated = source_middle(live, weight, source_g)
    ratio_out = ratio_end(act, gated, source_u)
    return (target_out, ratio_out)


def solution(mesh):
    placed = (
        P(("groups", "wide"), "narrow"),
        P(("groups", "wide"), "narrow"),
        P("narrow", "wide"),
        P("narrow", "wide"),
        P("narrow", "wide"),
        P("narrow", "wide"),
        P(("groups", "narrow")),
        P(("groups", "narrow")),
        P(),
    )
    mesh_shape = dict(mesh.shape)

    def body(*args):
        return local(mesh_shape, *args)

    return jax.shard_map(
        body,
        mesh=mesh,
        in_specs=placed,
        out_specs=(P(("groups", "narrow"), "wide"), P(("groups", "narrow"), "wide")),
        check_vma=False,
    )
```
